512 devices in a mesh: sample: 8 (over z), space: 64 (over x, y, core).
Axes of the slice: x: 4, y: 8, z: 8, core: 2. Of those that a mesh axis runs over, the one named last changes fastest.
Arguments:
- inflow_seeds: int32 [8, 2], P('sample'), may hold values from 0 to 47
- rotor_cells: int32 [64, 3], replicated, may hold values from 0 to 191, as said below
- fluctuation: float32 [3, 192, 48, 128], P(None, 'space'), may hold values from -6 to 6
- profile: float32 [48], replicated, may hold values from 0.5 to 1.5
- correction: float32 [192, 48, 128], P('space'), may hold values from -0.7 to 0.7
- observed: float32 [192, 48, 128], P('space'), may hold values from -6 to 6
Outputs:
- velocity: float32 [8, 3, 192, 48, 128], P('sample', None, 'space')
- gradient: float32 [192, 48, 128], P('space')
The draws below stay inside these ranges and needn't reach their ends.
Inputs may be any that keep to these rules, and one draw needn't show every extreme that they name: `inflow_seeds`: column 0 is the spanwise offset and column 1 the vertical offset of a sample's inflow. `rotor_cells`: column 0 is a turbine's streamwise cell, column 1 the first of its 8 spanwise cells (at most 120), column 2 the lowest of its 8 vertical cells (1 to 23). Discs may intersect.
All inputs are finite; a program needn't handle non-finite values.
Results may differ from the reference program's by a relative error of at most 0.0001.
Values sent between devices are 32-bit elements; how exact they have to be, the bound alone decides.
No kernel may reach another device: no remote copies, remote signals or barrier semaphores. Data moves between devices by JAX's collectives and lax.ppermute only.
A program may use at most 64 MiB of HBM per device.

```python
import math
import jax
import jax.numpy as jnp
from jax import lax

NX = 192
NY = 128
NZ = 48
SAMPLES = 8
TURB = 64
ROTOR = 8


def draw_rotor_cells(key, part):
    key = jax.random.fold_in(key, 7)
    key_stream, key_span, key_height = jax.random.split(key, 3)
    stream_cells = jax.random.randint(key_stream, (TURB,), 0, NX)
    stream_cells = stream_cells.at[0].set(NX - 1).at[1].set(0)
    span_cells = jax.random.randint(key_span, (TURB,), 0, NY - ROTOR + 1)
    height_cells = jax.random.randint(key_height, (TURB,), 1, NZ // 2)
    return jnp.stack([stream_cells, span_cells, height_cells], axis=1).astype(jnp.int32)


def set_ends(entries, own_key, smallest, top_value):
    place = [jax.random.randint(jax.random.fold_in(own_key, axis), (), 0, length) for axis, length in enumerate(entries.shape)]
    longest = entries.shape.index(max(entries.shape))
    next_to = place[:longest] + [(place[longest] + 1) % entries.shape[longest]] + place[longest + 1:]
    return entries.at[tuple(place)].set(smallest).at[tuple(next_to)].set(top_value)


def level_of(stream_key, extent, shards, low, top_value):
    loudness = 1.0
    for position, shards_of in shards:
        steps = jax.random.uniform(jax.random.fold_in(jax.random.fold_in(stream_key, 6), position), (shards_of,), jnp.float32, low / len(shards), top_value / len(shards))
        loudness = loudness * jnp.repeat(jnp.exp(steps), extent[position] // shards_of).reshape((-1,) + (1,) * (len(extent) - 1 - position))
    return loudness


def noise(rng, extent, deviation, reach, pieces=(), kind=jnp.bfloat16):
    level = level_of(rng, extent, pieces, -0.22, 0.18) if pieces else 1.0
    array = jax.random.normal(rng, extent, jnp.float32) * deviation * level
    return jnp.minimum(jnp.maximum(array, -reach), reach).astype(kind)


def setup_inputs(seed: int = 0) -> dict:
    keys = jax.random.split(jax.random.key(seed), 7)
    return {
        "inflow_seeds": set_ends(jax.random.randint(keys[0], (SAMPLES, 2), 0, NZ), jax.random.fold_in(keys[0], 1), 0, NZ - 1).astype(jnp.int32),
        "rotor_cells": draw_rotor_cells(jax.random.fold_in(keys[6], 71), 0),
        "fluctuation": noise(keys[2], (3, NX, NZ, NY), 1.0, 6.0, ((1, 64),), jnp.float32),
        "profile": jnp.clip(jax.random.uniform(keys[3], (NZ,), jnp.float32, 0.5, 1.5), 0.5, 1.5),
        "correction": jnp.clip(jax.random.uniform(keys[4], (NX, NZ, NY), jnp.float32, -0.7, 0.7) * level_of(keys[4], (NX, NZ, NY), ((0, 64),), -0.4, 0.0), -0.7, 0.7),
        "observed": noise(keys[5], (NX, NZ, NY), 1.0, 6.0, ((0, 64),), jnp.float32),
    }


TIME_STEP = 0.2
BASE_VISCOSITY = 0.15
THRUST = 1.0
PRECISE = lax.Precision.HIGHEST


def along_stream(field):
    return 0.5 * (jnp.roll(field, -1, axis=-3) - jnp.roll(field, 1, axis=-3))


def along_height(field):
    return 0.5 * (jnp.roll(field, -1, axis=-2) - jnp.roll(field, 1, axis=-2))


def along_span(field):
    return 0.5 * (jnp.roll(field, -1, axis=-1) - jnp.roll(field, 1, axis=-1))


def laplace(field):
    summed = jnp.roll(field, -1, axis=-3) + jnp.roll(field, 1, axis=-3)
    summed = summed + jnp.roll(field, -1, axis=-2) + jnp.roll(field, 1, axis=-2)
    summed = summed + jnp.roll(field, -1, axis=-1) + jnp.roll(field, 1, axis=-1)
    return summed - 6.0 * field


def symbol(wave_x, wave_z, wave_y):
    sine_x = jnp.sin((2.0 * math.pi / NX) * wave_x.astype(jnp.float32))
    sine_z = jnp.sin((2.0 * math.pi / NZ) * wave_z.astype(jnp.float32))
    sine_y = jnp.sin((2.0 * math.pi / NY) * wave_y.astype(jnp.float32))
    summed = sine_x * sine_x + sine_z * sine_z + sine_y * sine_y
    null_mode = (wave_x % (NX // 2) == 0) & (wave_z % (NZ // 2) == 0) & (wave_y % (NY // 2) == 0)
    return jnp.where(null_mode, 0.0, -1.0 / jnp.where(null_mode, 1.0, summed))


def rotor_field(rotor_cells, stream_cells):
    rotor_stream = rotor_cells[:, 0:1]
    rotor_span = rotor_cells[:, 1:2]
    rotor_base = rotor_cells[:, 2:3]
    heights = jnp.arange(NZ, dtype=jnp.int32)[None, :]
    spans = jnp.arange(NY, dtype=jnp.int32)[None, :]
    in_stream = (stream_cells[None, :] == rotor_stream).astype(jnp.float32)
    in_height = ((heights >= rotor_base) & (heights < rotor_base + ROTOR)).astype(jnp.float32)
    in_span = ((spans >= rotor_span) & (spans < rotor_span + ROTOR)).astype(jnp.float32)
    sheet = (in_stream[:, :, None] * in_height[:, None, :]).reshape(in_stream.shape[0], -1)
    counted = jnp.dot(sheet.T, in_span, precision=PRECISE)
    return counted.reshape(stream_cells.shape[0], NZ, NY)


def project(trial, symbol_table):
    source = along_stream(trial[0]) + along_span(trial[1]) + along_height(trial[2])
    spectrum = jnp.fft.rfftn(source, axes=(0, 2, 1))
    pressure = jnp.fft.irfftn(spectrum * symbol_table, s=(NX, NY, NZ), axes=(0, 2, 1))
    push = jnp.stack([along_stream(pressure), along_span(pressure), along_height(pressure)])
    return trial - push


def reference(inflow_seeds, rotor_cells, fluctuation, profile, correction, observed):
    viscosity = BASE_VISCOSITY * jnp.exp(correction)
    rotor_count = rotor_field(rotor_cells, jnp.arange(NX, dtype=jnp.int32))
    column = profile[:, None]
    wave_x = jnp.arange(NX, dtype=jnp.int32)[:, None, None]
    wave_z = jnp.arange(NZ // 2 + 1, dtype=jnp.int32)[None, :, None]
    wave_y = jnp.arange(NY, dtype=jnp.int32)[None, None, :]
    symbol_table = symbol(wave_x, wave_z, wave_y)
    gradient = jnp.zeros((NX, NZ, NY), jnp.float32)
    results = []
    for sample in range(SAMPLES):
        shifted = jnp.roll(fluctuation, inflow_seeds[sample, 0], axis=3)
        shifted = jnp.roll(shifted, inflow_seeds[sample, 1], axis=2)
        initial = jnp.concatenate([shifted[:1] + column, shifted[1:]], axis=0)
        laplace_start = laplace(initial)
        forcing = -column * along_stream(initial) + viscosity * laplace_start - THRUST * rotor_count * initial
        middle = project(initial + TIME_STEP * forcing, symbol_table)
        laplace_mid = laplace(middle)
        forcing = -column * along_stream(middle) + viscosity * laplace_mid - THRUST * rotor_count * middle
        velocity = project(0.5 * initial + 0.5 * (middle + TIME_STEP * forcing), symbol_table)
        misfit = velocity[0] - observed
        blank = jnp.zeros_like(misfit)
        adjoint_two = project(jnp.stack([misfit, blank, blank]), symbol_table)
        pulled = column * along_stream(adjoint_two) + laplace(viscosity * adjoint_two) - THRUST * rotor_count * adjoint_two
        adjoint_one = project(0.5 * adjoint_two + 0.5 * TIME_STEP * pulled, symbol_table)
        section_terms = 0.5 * jnp.sum(adjoint_two * laplace_mid, axis=0) + jnp.sum(adjoint_one * laplace_start, axis=0)
        gradient = gradient + TIME_STEP * viscosity * section_terms
        results.append(velocity)
    return jnp.stack(results), gradient
```

```python
import functools
import math

import jax
import jax.numpy as jnp
import ml_dtypes
import numpy as np
from jax import lax
from jax.experimental import pallas as pl
from jax.experimental.pallas import tpu as pltpu
from jax.sharding import PartitionSpec as P

NX = 192
NY = 128
NZ = 48
ROTOR = 8
SPACE = 64
SLAB = NX // SPACE

TIME_STEP = 0.2
BASE_VISCOSITY = 0.15
THRUST = 1.0
F32 = jnp.float32
BF16 = jnp.bfloat16


def real_basis(length):
    half = length // 2
    cells = np.arange(length)[:, None]
    waves = np.arange(half)[None, :]
    phase = 2.0 * np.pi / length * ((cells * waves) % length)
    even = np.cos(phase) * math.sqrt(2.0 / length)
    even[:, 0] = math.sqrt(1.0 / length)
    odd = np.sin(phase) * math.sqrt(2.0 / length)
    odd[:, 0] = (1.0 - 2.0 * (np.arange(length) % 2)) * math.sqrt(1.0 / length)
    return np.concatenate([even, odd], axis=1)


def sine_of(length):
    half = length // 2
    waves = np.arange(length) % half
    return np.sin(2.0 * np.pi / length * waves)


def two_part(matrix):
    matrix = np.asarray(matrix, np.float32)
    high = matrix.astype(ml_dtypes.bfloat16)
    low = (matrix - high.astype(np.float32)).astype(ml_dtypes.bfloat16)
    return np.stack([high, low])


BASIS_X = real_basis(NX)
BASIS_Y = real_basis(NY)
BASIS_Z = real_basis(NZ)


def stream_rows(first, count):
    device = np.arange(SPACE)[None, :]
    slot = np.arange(first, first + count)[:, None]
    return ((SLAB * device + slot) % NX).reshape(-1)


TO_Y = two_part(BASIS_Y)
FROM_Y = two_part(BASIS_Y.T)
TO_Z = two_part(BASIS_Z.T)
FROM_Z = two_part(BASIS_Z)
TO_X3 = two_part(BASIS_X[stream_rows(0, 3)].T)
TO_X5 = two_part(BASIS_X[stream_rows(-1, 5)].T)
FROM_X7 = two_part(BASIS_X[stream_rows(-2, 7)])
FROM_X5 = two_part(BASIS_X[stream_rows(-1, 5)])
SINE_X = np.broadcast_to(sine_of(NX)[:, None], (NX, NY)).astype(np.float32)


def split(value):
    high = value.astype(BF16)
    return high, (value - high.astype(F32)).astype(BF16)


def dot(a, b):
    return jnp.dot(a, b, preferred_element_type=F32)


def left_product(matrix, value):
    high, low = split(value)
    return dot(matrix[0], high) + dot(matrix[0], low) + dot(matrix[1], high)


def right_product(value, matrix):
    high, low = split(value)
    return dot(high, matrix[0]) + dot(low, matrix[0]) + dot(high, matrix[1])


def up_z(f):
    return pltpu.roll(f, NZ - 1, 0)


def down_z(f):
    return pltpu.roll(f, 1, 0)


def up_y(f):
    return pltpu.roll(f, NY - 1, 1)


def down_y(f):
    return pltpu.roll(f, 1, 1)


def along_height(f):
    return 0.5 * (up_z(f) - down_z(f))


def along_span(f):
    return 0.5 * (up_y(f) - down_y(f))


def along_stream(planes, j):
    return 0.5 * (planes[j + 1] - planes[j - 1])


def laplace(planes, j):
    f = planes[j]
    summed = planes[j + 1] + planes[j - 1] + up_z(f) + down_z(f) + up_y(f) + down_y(f)
    return summed - 6.0 * f


def to_modes(planes, to_z, to_y, out_ref):
    count = len(planes)
    side = left_product(to_z, jnp.concatenate(planes, axis=1))
    rows = jnp.concatenate([side[:, NY * i : NY * (i + 1)] for i in range(count)], axis=0)
    rows = right_product(rows, to_y)
    for i in range(count):
        out_ref[pl.ds(i, NZ, stride=count), :] = rows[NZ * i : NZ * (i + 1)]
    out_ref[NZ * count :, :] = jnp.zeros(((SPACE - NZ) * count, NY), F32)


def from_modes(in_ref, count, from_z, from_y):
    rows = jnp.concatenate([in_ref[pl.ds(i, NZ, stride=count), :] for i in range(count)], axis=0)
    rows = right_product(rows, from_y)
    side = jnp.concatenate([rows[NZ * i : NZ * (i + 1)] for i in range(count)], axis=1)
    side = left_product(from_z, side)
    return [side[:, NY * i : NY * (i + 1)] for i in range(count)]


def gather_slots(in_ref, first, count, total):
    parts = [in_ref[pl.ds(i, SPACE, stride=total), :] for i in range(first, first + count)]
    return jnp.concatenate(parts, axis=0)


def scatter_slots(out_ref, rows, first, count, total):
    for i in range(count):
        out_ref[pl.ds(first + i, SPACE, stride=total), :] = rows[SPACE * i : SPACE * (i + 1)]


def swap_waves(modes, sine):
    half = NX // 2
    return jnp.concatenate([sine[:half] * modes[half:], -sine[half:] * modes[:half]], axis=0)


def start_kernel(
    seeds, own, low, high, correction, rotor, column, to_z, to_y,
    buffer, first_trial, initial_out, laplace_out, viscosity_out,
):
    span_shift = seeds[0, 0]
    height_shift = seeds[0, 1]
    profile = column[...]
    outer = {-1: low[6], 3: high[6]}
    viscosity = {}
    for j in range(-1, 4):
        raw = correction[j] if 0 <= j < 3 else outer[j]
        viscosity[j] = BASE_VISCOSITY * jnp.exp(raw)
        viscosity_out[j + 1] = viscosity[j]
    trial = []
    for c in range(3):
        state = {}
        for j in range(-2, 5):
            if j < 0:
                raw = low[2 * c + j + 2]
            elif j < 3:
                raw = own[c, j]
            else:
                raw = high[2 * c + j - 3]
            raw = pltpu.roll(pltpu.roll(raw, span_shift, 1), height_shift, 0)
            state[j] = raw + profile if c == 0 else raw
        moved = {}
        for j in range(-1, 4):
            curvature = laplace(state, j)
            forcing = (
                viscosity[j] * curvature
                - profile * along_stream(state, j)
                - THRUST * rotor[j + 1] * state[j]
            )
            moved[j] = state[j] + TIME_STEP * forcing
            first_trial[5 * c + j + 1] = moved[j]
            if 0 <= j < 3:
                initial_out[3 * c + j] = state[j]
                laplace_out[3 * c + j] = curvature
        trial.append(moved)
    sources = [
        along_stream(trial[0], j) + along_span(trial[1][j]) + along_height(trial[2][j])
        for j in range(3)
    ]
    to_modes(sources, to_z, to_y, buffer)


def solve_one_kernel(modes_in, green, to_x, from_x, out):
    spectrum = left_product(to_x, gather_slots(modes_in, 0, 3, 3)) * green[...]
    scatter_slots(out, left_product(from_x, spectrum), 0, 7, 7)


def middle_kernel(
    modes_in, first_trial, initial, viscosity, rotor, observed, low, high, column,
    from_z, from_y, to_z, to_y,
    buffer, second_trial, laplace_out,
):
    profile = column[...]
    found = from_modes(modes_in, 7, from_z, from_y)
    pressure = {j - 2: found[j] for j in range(7)}
    seen = {j: observed[j] for j in range(3)}
    seen[-1] = low[7]
    seen[3] = high[7]
    trial = []
    for c in range(3):
        middle = {}
        for j in range(-1, 4):
            if c == 0:
                push = along_stream(pressure, j)
            elif c == 1:
                push = along_span(pressure[j])
            else:
                push = along_height(pressure[j])
            middle[j] = first_trial[5 * c + j + 1] - push
        moved = []
        for j in range(3):
            curvature = laplace(middle, j)
            laplace_out[3 * c + j] = curvature
            forcing = (
                viscosity[j + 1] * curvature
                - profile * along_stream(middle, j)
                - THRUST * rotor[j + 1] * middle[j]
            )
            moved.append(0.5 * initial[3 * c + j] + 0.5 * (middle[j] + TIME_STEP * forcing))
            if c > 0:
                second_trial[3 * (c - 1) + j] = moved[j]
        trial.append(moved)
    sheets = [trial[0][j] - seen[j] for j in range(3)]
    for j in range(3):
        sheets.append(
            along_span(trial[1][j]) + along_height(trial[2][j]) + along_stream(seen, j)
        )
    to_modes(sheets, to_z, to_y, buffer)


def solve_two_kernel(modes_in, green, sine_in, to_x, from_x, out):
    sine = sine_in[...]
    inverse = green[...]
    both = jnp.concatenate(
        [gather_slots(modes_in, 0, 3, 6), gather_slots(modes_in, 3, 3, 6)], axis=1
    )
    both = left_product(to_x, both)
    lead = both[:, :NY]
    second = inverse * (swap_waves(lead, sine) + both[:, NY:])
    misfit = lead - swap_waves(second, sine)
    third = inverse * swap_waves(misfit, sine)
    stream = misfit - swap_waves(third, sine)
    wide = left_product(from_x, jnp.concatenate([stream, third], axis=1))
    scatter_slots(out, wide[:, :NY], 0, 5, 13)
    scatter_slots(out, wide[:, NY:], 5, 5, 13)
    scatter_slots(out, left_product(from_x[:, SPACE : 4 * SPACE, :], second), 10, 3, 13)


def adjoint_kernel(
    modes_in, second_trial, laplace_mid, viscosity, rotor, observed, column,
    from_z, from_y, to_z, to_y,
    buffer, fourth_trial, velocity, share_out,
):
    profile = column[...]
    found = from_modes(modes_in, 13, from_z, from_y)
    stream = {j - 1: found[j] for j in range(5)}
    third = {j - 1: found[5 + j] for j in range(5)}
    second = found[10:]
    for j in range(3):
        velocity[0, 0, j] = stream[j] + observed[j] + along_stream(third, j)
        velocity[0, 1, j] = second_trial[j] - along_span(second[j])
        velocity[0, 2, j] = second_trial[3 + j] - along_height(second[j])
    share = [None] * 3
    trial = []
    for c in range(3):
        if c == 0:
            adjoint = stream
        elif c == 1:
            adjoint = {j: -along_span(third[j]) for j in range(-1, 4)}
        else:
            adjoint = {j: -along_height(third[j]) for j in range(-1, 4)}
        spread = {j: viscosity[j + 1] * adjoint[j] for j in range(-1, 4)}
        moved = []
        for j in range(3):
            pulled = (
                profile * along_stream(adjoint, j)
                + laplace(spread, j)
                - THRUST * rotor[j + 1] * adjoint[j]
            )
            moved.append(0.5 * adjoint[j] + 0.5 * TIME_STEP * pulled)
            fourth_trial[3 * c + j] = moved[j]
            term = adjoint[j] * laplace_mid[3 * c + j]
            share[j] = term if c == 0 else share[j] + term
        trial.append(moved)
    for j in range(3):
        share_out[j] = 0.5 * share[j]
    cross = [along_span(trial[1][j]) + along_height(trial[2][j]) for j in range(3)]
    lead = [0.5 * trial[0][j] for j in range(3)]
    sheets = [
        lead[0],
        cross[0] + lead[1],
        cross[1] + lead[2] - lead[0],
        cross[2] - lead[1],
        -lead[2],
    ]
    to_modes(sheets, to_z, to_y, buffer)


def solve_four_kernel(modes_in, green, to_x, from_x, out):
    spectrum = left_product(to_x, gather_slots(modes_in, 0, 5, 5)) * green[...]
    scatter_slots(out, left_product(from_x, spectrum), 0, 5, 5)


def gradient_kernel(
    modes_in, fourth_trial, laplace_start, viscosity, share, from_z, from_y, out
):
    found = from_modes(modes_in, 5, from_z, from_y)
    pressure = {j - 1: found[j] for j in range(5)}
    for j in range(3):
        push = [along_stream(pressure, j), along_span(pressure[j]), along_height(pressure[j])]
        total = share[j]
        for c in range(3):
            total = total + (fourth_trial[3 * c + j] - push[c]) * laplace_start[3 * c + j]
        total = TIME_STEP * viscosity[j + 1] * total
        for copy in range(out.shape[0]):
            out[copy, NZ * j : NZ * (j + 1), :] = total


def local_call(kernel, name, outs, *args):
    specs = [pl.BlockSpec(memory_space=pltpu.VMEM) for _ in args]
    if args[0].dtype == jnp.int32:
        specs[0] = pl.BlockSpec(memory_space=pltpu.SMEM)
    shapes = [jax.ShapeDtypeStruct(shape, F32) for shape in outs]
    spaces = [pl.BlockSpec(memory_space=pltpu.VMEM) for _ in outs]
    single = len(outs) == 1
    return pl.pallas_call(
        kernel,
        out_shape=shapes[0] if single else shapes,
        in_specs=specs,
        out_specs=spaces[0] if single else spaces,
        name=name,
        compiler_params=pltpu.CompilerParams(vmem_limit_bytes=24 * 1024 * 1024),
    )(*args)


def exchange(rows, axis="space"):
    count = lax.axis_size(axis)
    wide = rows.reshape(count, 1, rows.size // count)
    return lax.all_to_all(wide, axis, 0, 0, tiled=True).reshape(rows.shape)


def rotor_field(rotor_cells, stream_cells):
    rotor_stream = rotor_cells[:, 0:1]
    rotor_span = rotor_cells[:, 1:2]
    rotor_base = rotor_cells[:, 2:3]
    heights = jnp.arange(NZ, dtype=jnp.int32)[None, :]
    spans = jnp.arange(NY, dtype=jnp.int32)[None, :]
    in_stream = (stream_cells[None, :] == rotor_stream).astype(F32)
    in_height = ((heights >= rotor_base) & (heights < rotor_base + ROTOR)).astype(F32)
    in_span = ((spans >= rotor_span) & (spans < rotor_span + ROTOR)).astype(F32)
    sheet = (in_stream[:, :, None] * in_height[:, None, :]).reshape(in_stream.shape[0], -1)
    counted = jnp.dot(sheet.T, in_span, preferred_element_type=F32)
    return counted.reshape(stream_cells.shape[0], NZ, NY)


def green_table(position):
    square_x = jnp.asarray((sine_of(NX) ** 2).astype(np.float32))[:, None]
    square_y = jnp.asarray((sine_of(NY) ** 2).astype(np.float32))[None, :]
    square_z = jnp.asarray((sine_of(NZ) ** 2).astype(np.float32))
    height = jnp.minimum(position, NZ - 1)
    summed = square_x + lax.dynamic_index_in_dim(square_z, height, keepdims=False) + square_y
    null_x = jnp.asarray(np.arange(NX) % (NX // 2) == 0)[:, None]
    null_y = jnp.asarray(np.arange(NY) % (NY // 2) == 0)[None, :]
    null_mode = null_x & null_y & (height % (NZ // 2) == 0)
    table = jnp.where(null_mode, 0.0, -1.0 / jnp.where(null_mode, 1.0, summed))
    return jnp.where(position < NZ, table, 0.0)


def shards(inflow_seeds, rotor_cells, fluctuation, profile, correction, observed):
    position = lax.axis_index("space")
    samples = lax.axis_size("sample")
    forward = [(i, (i + 1) % SPACE) for i in range(SPACE)]
    backward = [(target, source) for source, target in forward]
    plane = (NZ, NY)
    last = jnp.concatenate(
        [fluctuation[:, 1:].reshape(6, NZ, NY), correction[2:], observed[2:]], axis=0
    )
    first = jnp.concatenate(
        [fluctuation[:, :2].reshape(6, NZ, NY), correction[:1], observed[:1]], axis=0
    )
    low = lax.ppermute(last, "space", forward)
    high = lax.ppermute(first, "space", backward)
    cells = (position * SLAB + jnp.arange(-1, SLAB + 1, dtype=jnp.int32)) % NX
    rotor = rotor_field(rotor_cells, cells)
    column = jnp.broadcast_to(profile[:, None], plane)
    green = green_table(position)
    to_y, from_y = jnp.asarray(TO_Y), jnp.asarray(FROM_Y)
    to_z, from_z = jnp.asarray(TO_Z), jnp.asarray(FROM_Z)

    buffer, first_trial, initial, laplace_start, viscosity = local_call(
        start_kernel, "start",
        [(SPACE * 3, NY), (15, *plane), (9, *plane), (9, *plane), (5, *plane)],
        inflow_seeds, fluctuation, low, high, correction, rotor, column, to_z, to_y,
    )
    buffer = exchange(buffer)
    buffer = local_call(
        solve_one_kernel, "solve_one", [(SPACE * 7, NY)],
        buffer, green, jnp.asarray(TO_X3), jnp.asarray(FROM_X7),
    )
    buffer = exchange(buffer)
    buffer, second_trial, laplace_mid = local_call(
        middle_kernel, "middle",
        [(SPACE * 6, NY), (6, *plane), (9, *plane)],
        buffer, first_trial, initial, viscosity, rotor, observed, low, high, column,
        from_z, from_y, to_z, to_y,
    )
    buffer = exchange(buffer)
    buffer = local_call(
        solve_two_kernel, "solve_two", [(SPACE * 13, NY)],
        buffer, green, jnp.asarray(SINE_X), jnp.asarray(TO_X3), jnp.asarray(FROM_X5),
    )
    buffer = exchange(buffer)
    buffer, fourth_trial, velocity, share = local_call(
        adjoint_kernel, "adjoint",
        [(SPACE * 5, NY), (9, *plane), (1, 3, 3, *plane), (3, *plane)],
        buffer, second_trial, laplace_mid, viscosity, rotor, observed, column,
        from_z, from_y, to_z, to_y,
    )
    buffer = exchange(buffer)
    buffer = local_call(
        solve_four_kernel, "solve_four", [(SPACE * 5, NY)],
        buffer, green, jnp.asarray(TO_X5), jnp.asarray(FROM_X5),
    )
    buffer = exchange(buffer)
    terms = local_call(
        gradient_kernel, "gradient", [(samples, SLAB * NZ, NY)],
        buffer, fourth_trial, laplace_start, viscosity, share, from_z, from_y,
    )
    terms = lax.all_to_all(terms, "sample", 0, 0, tiled=True)
    gradient = jnp.sum(terms, axis=0).reshape(SLAB, *plane)
    return (velocity, gradient)


def solution(mesh):
    return jax.shard_map(
        shards,
        mesh=mesh,
        in_specs=(
            P("sample", None),
            P(),
            P(None, "space", None, None),
            P(),
            P("space", None, None),
            P("space", None, None),
        ),
        out_specs=(P("sample", None, "space", None, None), P("space", None, None)),
        check_vma=False,
    )
```

```python
import functools
import math

import jax
import jax.numpy as jnp
import ml_dtypes
import numpy as np
from jax import lax
from jax.experimental import pallas as pl
from jax.experimental.pallas import tpu as pltpu
from jax.sharding import PartitionSpec as P

NX = 192
NY = 128
NZ = 48
ROTOR = 8
SPACE = 64
SLAB = NX // SPACE

TIME_STEP = 0.2
BASE_VISCOSITY = 0.15
THRUST = 1.0
F32 = jnp.float32
BF16 = jnp.bfloat16


def real_basis(length):
    half = length // 2
    cells = np.arange(length)[:, None]
    waves = np.arange(half)[None, :]
    phase = 2.0 * np.pi / length * ((cells * waves) % length)
    even = np.cos(phase) * math.sqrt(2.0 / length)
    even[:, 0] = math.sqrt(1.0 / length)
    odd = np.sin(phase) * math.sqrt(2.0 / length)
    odd[:, 0] = (1.0 - 2.0 * (np.arange(length) % 2)) * math.sqrt(1.0 / length)
    return np.concatenate([even, odd], axis=1)


def sine_of(length):
    half = length // 2
    waves = np.arange(length) % half
    return np.sin(2.0 * np.pi / length * waves)


def in_parts(matrix, count):
    parts = []
    rest = np.asarray(matrix, np.float64)
    for _ in range(count):
        parts.append(rest.astype(ml_dtypes.bfloat16))
        rest = rest - parts[-1].astype(np.float64)
    return np.stack(parts)


BASIS_X = real_basis(NX)
BASIS_Y = real_basis(NY)
BASIS_Z = real_basis(NZ)


def stream_rows(first, count):
    device = np.arange(SPACE)[None, :]
    slot = np.arange(first, first + count)[:, None]
    return ((SLAB * device + slot) % NX).reshape(-1)


TO_Y = in_parts(BASIS_Y, 2)
TO_Z = in_parts(BASIS_Z.T, 2)
TO_X = in_parts(BASIS_X[stream_rows(0, 3)].T, 2)
FROM_Y = in_parts(BASIS_Y.T, 3)
FROM_Z = in_parts(BASIS_Z, 3)
FROM_X = in_parts(BASIS_X[stream_rows(0, 4)], 3)
SINE_X = np.broadcast_to(sine_of(NX)[:, None], (NX, NY)).astype(np.float32)


def split(value, count):
    parts = []
    for _ in range(count - 1):
        parts.append(value.astype(BF16))
        value = value - parts[-1].astype(F32)
    return parts + [value.astype(BF16)]


def dot(a, b):
    return jnp.dot(a, b, preferred_element_type=F32)


def left_product(matrix, value):
    count = matrix.shape[0]
    parts = split(value, count)
    pairs = [(i, order - i) for order in reversed(range(count)) for i in range(order + 1)]
    return sum(dot(matrix[i], parts[k]) for i, k in pairs)


def right_product(value, matrix):
    count = matrix.shape[0]
    parts = split(value, count)
    pairs = [(i, order - i) for order in reversed(range(count)) for i in range(order + 1)]
    return sum(dot(parts[k], matrix[i]) for i, k in pairs)


def up_z(f):
    return pltpu.roll(f, NZ - 1, 0)


def down_z(f):
    return pltpu.roll(f, 1, 0)


def up_y(f):
    return pltpu.roll(f, NY - 1, 1)


def down_y(f):
    return pltpu.roll(f, 1, 1)


def along_height(f):
    return 0.5 * (up_z(f) - down_z(f))


def along_span(f):
    return 0.5 * (up_y(f) - down_y(f))


def along_stream(planes, j):
    return 0.5 * (planes[j + 1] - planes[j - 1])


def laplace(planes, j):
    f = planes[j]
    summed = planes[j + 1] + planes[j - 1] + up_z(f) + down_z(f) + up_y(f) + down_y(f)
    return summed - 6.0 * f


def cross_laplace(f):
    return along_span(along_span(f)) + along_height(along_height(f))


def with_plane_below(planes, source):
    below = 2.0 * planes[1] - planes[3] + 4.0 * (source - cross_laplace(planes[1]))
    return {-1: below, 0: planes[0], 1: planes[1], 2: planes[2], 3: planes[3]}


def to_modes(planes, to_z, to_y, out_ref):
    count = len(planes)
    side = left_product(to_z, jnp.concatenate(planes, axis=1))
    rows = jnp.concatenate([side[:, NY * i : NY * (i + 1)] for i in range(count)], axis=0)
    rows = right_product(rows, to_y)
    for i in range(count):
        out_ref[pl.ds(i, NZ, stride=count), :] = rows[NZ * i : NZ * (i + 1)]
    out_ref[NZ * count :, :] = jnp.zeros(((SPACE - NZ) * count, NY), F32)


def from_modes(in_ref, count, from_z, from_y):
    rows = jnp.concatenate([in_ref[pl.ds(i, NZ, stride=count), :] for i in range(count)], axis=0)
    rows = right_product(rows, from_y)
    side = jnp.concatenate([rows[NZ * i : NZ * (i + 1)] for i in range(count)], axis=1)
    side = left_product(from_z, side)
    return [side[:, NY * i : NY * (i + 1)] for i in range(count)]


def gather_slots(in_ref, first, count, total):
    parts = [in_ref[pl.ds(i, SPACE, stride=total), :] for i in range(first, first + count)]
    return jnp.concatenate(parts, axis=0)


def scatter_slots(out_ref, rows, first, count, total):
    for i in range(count):
        out_ref[pl.ds(first + i, SPACE, stride=total), :] = rows[SPACE * i : SPACE * (i + 1)]


def swap_waves(modes, sine):
    half = NX // 2
    return jnp.concatenate([sine[:half] * modes[half:], -sine[half:] * modes[:half]], axis=0)


def start_kernel(
    seeds, own, low, high, correction, rotor, column, green, to_z, to_y,
    buffer, first_trial, source_out, initial_out, laplace_out, viscosity_out,
):
    span_shift = seeds[0, 0]
    height_shift = seeds[0, 1]
    profile = column[...]
    viscosity = {}
    for j in range(-2, 5):
        if j < 0:
            raw = low[8 + j]
        elif j < 3:
            raw = correction[j]
        else:
            raw = high[3 + j]
        viscosity[j] = BASE_VISCOSITY * jnp.exp(raw)
        viscosity_out[j + 2] = viscosity[j]
    trial = []
    for c in range(3):
        state = {}
        for j in range(-2, 5):
            if j < 0:
                raw = low[2 * c + j + 2]
            elif j < 3:
                raw = own[c, j]
            else:
                raw = high[2 * c + j - 3]
            raw = pltpu.roll(pltpu.roll(raw, span_shift, 1), height_shift, 0)
            state[j] = raw + profile if c == 0 else raw
        moved = {}
        for j in range(-1, 4):
            curvature = laplace(state, j)
            forcing = (
                viscosity[j] * curvature
                - profile * along_stream(state, j)
                - THRUST * rotor[j + 1] * state[j]
            )
            moved[j] = state[j] + TIME_STEP * forcing
            first_trial[5 * c + j + 1] = moved[j]
            if 0 <= j < 3:
                initial_out[3 * c + j] = state[j]
                laplace_out[3 * c + j] = curvature
        trial.append(moved)
    sources = [
        along_stream(trial[0], j) + along_span(trial[1][j]) + along_height(trial[2][j])
        for j in range(3)
    ]
    source_out[...] = sources[1]
    to_modes(sources, to_z, to_y, buffer)


def solve_kernel(modes_in, green, to_x, from_x, out):
    spectrum = left_product(to_x, gather_slots(modes_in, 0, 3, 3)) * green[...]
    scatter_slots(out, left_product(from_x, spectrum), 0, 4, 4)


def middle_kernel(
    modes_in, first_trial, source, initial, viscosity, rotor, observed, low, high, column,
    from_z, from_y, to_z, to_y,
    buffer, second_trial, source_out, laplace_out,
):
    profile = column[...]
    pressure = with_plane_below(from_modes(modes_in, 4, from_z, from_y), source[...])
    seen = {j: observed[j] for j in range(3)}
    seen[-1] = low[8]
    seen[3] = high[8]
    span = {j: first_trial[6 + j] - along_span(pressure[j]) for j in range(-1, 4)}
    height = {j: first_trial[11 + j] - along_height(pressure[j]) for j in range(-1, 4)}
    stream = {j: first_trial[1 + j] - along_stream(pressure, j) for j in range(3)}
    stream[-1] = stream[1] + 2.0 * (along_span(span[0]) + along_height(height[0]))
    stream[3] = stream[1] - 2.0 * (along_span(span[2]) + along_height(height[2]))
    trial = []
    for c, middle in enumerate((stream, span, height)):
        moved = {}
        for j in range(3):
            curvature = laplace(middle, j)
            laplace_out[3 * c + j] = curvature
            forcing = (
                viscosity[j + 2] * curvature
                - profile * along_stream(middle, j)
                - THRUST * rotor[j + 1] * middle[j]
            )
            moved[j] = 0.5 * initial[3 * c + j] + 0.5 * (middle[j] + TIME_STEP * forcing)
            second_trial[3 * c + j] = moved[j]
        trial.append(moved)
    cross = [along_span(trial[1][j]) + along_height(trial[2][j]) for j in range(3)]
    source_out[...] = along_stream(trial[0], 1) + cross[1]
    sheets = [trial[0][j] - seen[j] for j in range(3)]
    sheets += [cross[j] + along_stream(seen, j) for j in range(3)]
    to_modes(sheets, to_z, to_y, buffer)


def solve_both_kernel(modes_in, green, sine_in, to_x, from_x, out):
    sine = sine_in[...]
    inverse = green[...]
    both = jnp.concatenate(
        [gather_slots(modes_in, 0, 3, 6), gather_slots(modes_in, 3, 3, 6)], axis=1
    )
    both = left_product(to_x, both)
    lead = both[:, :NY]
    second = inverse * (swap_waves(lead, sine) + both[:, NY:])
    third = inverse * swap_waves(lead - swap_waves(second, sine), sine)
    wide = left_product(from_x, jnp.concatenate([second, third], axis=1))
    scatter_slots(out, wide[:, :NY], 0, 4, 8)
    scatter_slots(out, wide[:, NY:], 4, 4, 8)


def adjoint_kernel(
    modes_in, second_trial, source, laplace_mid, viscosity, rotor, observed, column,
    from_z, from_y, to_z, to_y,
    buffer, fourth_trial, source_out, velocity, share_out,
):
    profile = column[...]
    found = from_modes(modes_in, 8, from_z, from_y)
    second = with_plane_below(found[:4], source[...])
    misfit = []
    for j in range(3):
        stream = second_trial[j] - along_stream(second, j)
        velocity[0, 0, j] = stream
        velocity[0, 1, j] = second_trial[3 + j] - along_span(second[j])
        velocity[0, 2, j] = second_trial[6 + j] - along_height(second[j])
        misfit.append(stream - observed[j])
    third = with_plane_below(found[4:], 0.5 * (misfit[2] - misfit[0]))
    span = {j: -along_span(third[j]) for j in range(-1, 4)}
    height = {j: -along_height(third[j]) for j in range(-1, 4)}
    cross = {j: along_span(span[j]) + along_height(height[j]) for j in range(-1, 4)}
    stream = {j: misfit[j] - along_stream(third, j) for j in range(3)}
    stream[-1] = stream[1] + 2.0 * cross[0]
    stream[3] = stream[1] - 2.0 * cross[2]
    stream[-2] = stream[0] + 2.0 * cross[-1]
    stream[4] = stream[2] - 2.0 * cross[3]
    share = [None] * 3
    trial = []
    for c, adjoint in enumerate((stream, span, height)):
        spread = {j: viscosity[j + 2] * adjoint[j] for j in adjoint}
        moved = {}
        for j in range(-1, 4) if c == 0 else range(3):
            pulled = (
                profile * along_stream(adjoint, j)
                + laplace(spread, j)
                - THRUST * rotor[j + 1] * adjoint[j]
            )
            moved[j] = 0.5 * adjoint[j] + 0.5 * TIME_STEP * pulled
        for j in range(3):
            fourth_trial[3 * c + j] = moved[j]
            term = adjoint[j] * laplace_mid[3 * c + j]
            share[j] = term if c == 0 else share[j] + term
        trial.append(moved)
    for j in range(3):
        share_out[j] = 0.5 * share[j]
    sources = [
        along_stream(trial[0], j) + along_span(trial[1][j]) + along_height(trial[2][j])
        for j in range(3)
    ]
    source_out[...] = sources[1]
    to_modes(sources, to_z, to_y, buffer)


def gradient_kernel(
    modes_in, fourth_trial, source, laplace_start, viscosity, share, from_z, from_y, out
):
    pressure = with_plane_below(from_modes(modes_in, 4, from_z, from_y), source[...])
    for j in range(3):
        push = [along_stream(pressure, j), along_span(pressure[j]), along_height(pressure[j])]
        total = share[j]
        for c in range(3):
            total = total + (fourth_trial[3 * c + j] - push[c]) * laplace_start[3 * c + j]
        total = TIME_STEP * viscosity[j + 2] * total
        for copy in range(out.shape[0]):
            out[copy, NZ * j : NZ * (j + 1), :] = total


def local_call(kernel, name, outs, *args):
    specs = [pl.BlockSpec(memory_space=pltpu.VMEM) for _ in args]
    if name == "start":
        specs[0] = pl.BlockSpec(memory_space=pltpu.SMEM)
        specs[7] = pl.BlockSpec(memory_space=pl.ANY)
    shapes = [jax.ShapeDtypeStruct(shape, F32) for shape in outs]
    spaces = [pl.BlockSpec(memory_space=pltpu.VMEM) for _ in outs]
    single = len(outs) == 1
    return pl.pallas_call(
        kernel,
        out_shape=shapes[0] if single else shapes,
        in_specs=specs,
        out_specs=spaces[0] if single else spaces,
        name=name,
        compiler_params=pltpu.CompilerParams(vmem_limit_bytes=24 * 1024 * 1024),
    )(*args)


def exchange(rows, axis="space"):
    count = lax.axis_size(axis)
    wide = rows.reshape(count, 1, rows.size // count)
    return lax.all_to_all(wide, axis, 0, 0, tiled=True).reshape(rows.shape)


def rotor_field(rotor_cells, stream_cells):
    rotor_stream = rotor_cells[:, 0:1]
    rotor_span = rotor_cells[:, 1:2]
    rotor_base = rotor_cells[:, 2:3]
    heights = jnp.arange(NZ, dtype=jnp.int32)[None, :]
    spans = jnp.arange(NY, dtype=jnp.int32)[None, :]
    in_stream = (stream_cells[None, :] == rotor_stream).astype(F32)
    in_height = ((heights >= rotor_base) & (heights < rotor_base + ROTOR)).astype(F32)
    in_span = ((spans >= rotor_span) & (spans < rotor_span + ROTOR)).astype(F32)
    sheet = (in_stream[:, :, None] * in_height[:, None, :]).reshape(in_stream.shape[0], -1)
    counted = jnp.dot(sheet.T, in_span, preferred_element_type=F32)
    return counted.reshape(stream_cells.shape[0], NZ, NY)


def green_table(position):
    square_x = jnp.asarray((sine_of(NX) ** 2).astype(np.float32))[:, None]
    square_y = jnp.asarray((sine_of(NY) ** 2).astype(np.float32))[None, :]
    square_z = jnp.asarray((sine_of(NZ) ** 2).astype(np.float32))
    height = jnp.minimum(position, NZ - 1)
    summed = square_x + lax.dynamic_index_in_dim(square_z, height, keepdims=False) + square_y
    null_x = jnp.asarray(np.arange(NX) % (NX // 2) == 0)[:, None]
    null_y = jnp.asarray(np.arange(NY) % (NY // 2) == 0)[None, :]
    null_mode = null_x & null_y & (height % (NZ // 2) == 0)
    table = jnp.where(null_mode, 0.0, -1.0 / jnp.where(null_mode, 1.0, summed))
    return jnp.where(position < NZ, table, 0.0)


def shards(inflow_seeds, rotor_cells, fluctuation, profile, correction, observed):
    position = lax.axis_index("space")
    samples = lax.axis_size("sample")
    forward = [(i, (i + 1) % SPACE) for i in range(SPACE)]
    backward = [(target, source) for source, target in forward]
    plane = (NZ, NY)
    last = jnp.concatenate(
        [fluctuation[:, 1:].reshape(6, NZ, NY), correction[1:], observed[2:]], axis=0
    )
    first = jnp.concatenate(
        [fluctuation[:, :2].reshape(6, NZ, NY), correction[:2], observed[:1]], axis=0
    )
    low = lax.ppermute(last, "space", forward)
    high = lax.ppermute(first, "space", backward)
    cells = (position * SLAB + jnp.arange(-1, SLAB + 1, dtype=jnp.int32)) % NX
    rotor = rotor_field(rotor_cells, cells)
    column = jnp.broadcast_to(profile[:, None], plane)
    green = green_table(position)
    to_x, from_x = jnp.asarray(TO_X), jnp.asarray(FROM_X)
    to_y, from_y = jnp.asarray(TO_Y), jnp.asarray(FROM_Y)
    to_z, from_z = jnp.asarray(TO_Z), jnp.asarray(FROM_Z)

    buffer, first_trial, source, initial, laplace_start, viscosity = local_call(
        start_kernel, "start",
        [(SPACE * 3, NY), (15, *plane), plane, (9, *plane), (9, *plane), (7, *plane)],
        inflow_seeds, fluctuation, low, high, correction, rotor, column, green, to_z, to_y,
    )
    buffer = exchange(buffer)
    buffer = local_call(
        solve_kernel, "solve_one", [(SPACE * 4, NY)], buffer, green, to_x, from_x
    )
    buffer = exchange(buffer)
    buffer, second_trial, source, laplace_mid = local_call(
        middle_kernel, "middle",
        [(SPACE * 6, NY), (9, *plane), plane, (9, *plane)],
        buffer, first_trial, source, initial, viscosity, rotor, observed, low, high, column,
        from_z, from_y, to_z, to_y,
    )
    buffer = exchange(buffer)
    buffer = local_call(
        solve_both_kernel, "solve_two", [(SPACE * 8, NY)],
        buffer, green, jnp.asarray(SINE_X), to_x, from_x,
    )
    buffer = exchange(buffer)
    buffer, fourth_trial, source, velocity, share = local_call(
        adjoint_kernel, "adjoint",
        [(SPACE * 3, NY), (9, *plane), plane, (1, 3, 3, *plane), (3, *plane)],
        buffer, second_trial, source, laplace_mid, viscosity, rotor, observed, column,
        from_z, from_y, to_z, to_y,
    )
    buffer = exchange(buffer)
    buffer = local_call(
        solve_kernel, "solve_four", [(SPACE * 4, NY)], buffer, green, to_x, from_x
    )
    buffer = exchange(buffer)
    terms = local_call(
        gradient_kernel, "gradient", [(samples, SLAB * NZ, NY)],
        buffer, fourth_trial, source, laplace_start, viscosity, share, from_z, from_y,
    )
    terms = lax.all_to_all(terms, "sample", 0, 0, tiled=True)
    gradient = jnp.sum(terms, axis=0).reshape(SLAB, *plane)
    return (velocity, gradient)


def solution(mesh):
    return jax.shard_map(
        shards,
        mesh=mesh,
        in_specs=(
            P("sample", None),
            P(),
            P(None, "space", None, None),
            P(),
            P("space", None, None),
            P("space", None, None),
        ),
        out_specs=(P("sample", None, "space", None, None), P("space", None, None)),
        check_vma=False,
    )
```

```python
import functools
import math

import jax
import jax.numpy as jnp
import ml_dtypes
import numpy as np
from jax import lax
from jax.experimental import pallas as pl
from jax.experimental.pallas import tpu as pltpu
from jax.sharding import PartitionSpec as P

NX = 192
NY = 128
NZ = 48
ROTOR = 8
SPACE = 64
SLAB = NX // SPACE

TIME_STEP = 0.2
BASE_VISCOSITY = 0.15
THRUST = 1.0
F32 = jnp.float32
BF16 = jnp.bfloat16


def real_basis(length):
    half = length // 2
    cells = np.arange(length)[:, None]
    waves = np.arange(half)[None, :]
    phase = 2.0 * np.pi / length * ((cells * waves) % length)
    even = np.cos(phase) * math.sqrt(2.0 / length)
    even[:, 0] = math.sqrt(1.0 / length)
    odd = np.sin(phase) * math.sqrt(2.0 / length)
    odd[:, 0] = (1.0 - 2.0 * (np.arange(length) % 2)) * math.sqrt(1.0 / length)
    return np.concatenate([even, odd], axis=1)


def sine_of(length):
    half = length // 2
    waves = np.arange(length) % half
    return np.sin(2.0 * np.pi / length * waves)


def in_parts(matrix, count):
    parts = []
    rest = np.asarray(matrix, np.float64)
    for _ in range(count):
        parts.append(rest.astype(ml_dtypes.bfloat16))
        rest = rest - parts[-1].astype(np.float64)
    return np.stack(parts)


BASIS_X = real_basis(NX)
BASIS_Y = real_basis(NY)
BASIS_Z = real_basis(NZ)


def stream_rows(first, count):
    device = np.arange(SPACE)[None, :]
    slot = np.arange(first, first + count)[:, None]
    return ((SLAB * device + slot) % NX).reshape(-1)


TO_Y = in_parts(BASIS_Y, 2)
TO_Z = in_parts(BASIS_Z.T, 2)
TO_X = in_parts(BASIS_X[stream_rows(0, 3)].T, 2)
FROM_Y = in_parts(BASIS_Y.T, 3)
FROM_Z = in_parts(BASIS_Z, 3)
FROM_X = in_parts(BASIS_X[stream_rows(0, 4)], 3)
SINE_X = np.broadcast_to(sine_of(NX)[:, None], (NX, NY)).astype(np.float32)
SQUARES = (sine_of(NX)[:, None] ** 2 + sine_of(NY)[None, :] ** 2).astype(np.float32)
SQUARES_Z = np.zeros((1, SPACE), np.float32)
SQUARES_Z[0, :NZ] = sine_of(NZ) ** 2


def split(value, count):
    parts = []
    for _ in range(count - 1):
        parts.append(value.astype(BF16))
        value = value - parts[-1].astype(F32)
    return parts + [value.astype(BF16)]


def dot(a, b):
    return jnp.dot(a, b, preferred_element_type=F32)


def left_product(matrix, value):
    count = matrix.shape[0]
    parts = split(value, count)
    pairs = [(i, order - i) for order in reversed(range(count)) for i in range(order + 1)]
    return sum(dot(matrix[i], parts[k]) for i, k in pairs)


def right_product(value, matrix):
    count = matrix.shape[0]
    parts = split(value, count)
    pairs = [(i, order - i) for order in reversed(range(count)) for i in range(order + 1)]
    return sum(dot(parts[k], matrix[i]) for i, k in pairs)


def up_z(f):
    return pltpu.roll(f, NZ - 1, 0)


def down_z(f):
    return pltpu.roll(f, 1, 0)


def up_y(f):
    return pltpu.roll(f, NY - 1, 1)


def down_y(f):
    return pltpu.roll(f, 1, 1)


def along_height(f):
    return 0.5 * (up_z(f) - down_z(f))


def along_span(f):
    return 0.5 * (up_y(f) - down_y(f))


def along_stream(planes, j):
    return 0.5 * (planes[j + 1] - planes[j - 1])


def laplace(planes, j):
    f = planes[j]
    summed = planes[j + 1] + planes[j - 1] + up_z(f) + down_z(f) + up_y(f) + down_y(f)
    return summed - 6.0 * f


def cross_laplace(f):
    return along_span(along_span(f)) + along_height(along_height(f))


def with_plane_below(planes, source):
    below = 2.0 * planes[1] - planes[3] + 4.0 * (source - cross_laplace(planes[1]))
    return {-1: below, 0: planes[0], 1: planes[1], 2: planes[2], 3: planes[3]}


def to_modes(planes, to_z, to_y, out_ref):
    count = len(planes)
    side = left_product(to_z, jnp.concatenate(planes, axis=1))
    rows = jnp.concatenate([side[:, NY * i : NY * (i + 1)] for i in range(count)], axis=0)
    rows = right_product(rows, to_y)
    for i in range(count):
        out_ref[pl.ds(i, NZ, stride=count), :] = rows[NZ * i : NZ * (i + 1)]
    out_ref[NZ * count :, :] = jnp.zeros(((SPACE - NZ) * count, NY), F32)


def from_modes(in_ref, count, from_z, from_y):
    rows = jnp.concatenate([in_ref[pl.ds(i, NZ, stride=count), :] for i in range(count)], axis=0)
    rows = right_product(rows, from_y)
    side = jnp.concatenate([rows[NZ * i : NZ * (i + 1)] for i in range(count)], axis=1)
    side = left_product(from_z, side)
    return [side[:, NY * i : NY * (i + 1)] for i in range(count)]


def gather_slots(in_ref, first, count, total):
    parts = [in_ref[pl.ds(i, SPACE, stride=total), :] for i in range(first, first + count)]
    return jnp.concatenate(parts, axis=0)


def scatter_slots(out_ref, rows, first, count, total):
    for i in range(count):
        out_ref[pl.ds(first + i, SPACE, stride=total), :] = rows[SPACE * i : SPACE * (i + 1)]


def swap_waves(modes, sine):
    half = NX // 2
    return jnp.concatenate([sine[:half] * modes[half:], -sine[half:] * modes[:half]], axis=0)


def count_rotors(cells):
    stream = cells[0:1, :]
    span = cells[1:2, :]
    base = cells[2:3, :]
    turbines = cells.shape[1]
    spans = lax.broadcasted_iota(jnp.int32, (NY, turbines), 0)
    in_span = ((spans >= span) & (spans < span + ROTOR)).astype(F32).astype(BF16)
    heights = lax.broadcasted_iota(jnp.int32, (NZ, turbines), 0)
    in_height = (heights >= base) & (heights < base + ROTOR)
    first = lax.axis_index("space") * SLAB
    sheets = []
    for j in range(-1, 4):
        here = stream == lax.rem(first + (j + NX), NX)
        sheets.append((in_height & here).astype(F32).astype(BF16))
    counted = lax.dot_general(
        jnp.concatenate(sheets, axis=0), in_span, (((1,), (1,)), ((), ())),
        preferred_element_type=F32,
    )
    return [counted[NZ * i : NZ * (i + 1)] for i in range(5)]


def spread_profile(row):
    cells = lax.broadcasted_iota(jnp.int32, (NZ, NZ), 0)
    others = lax.broadcasted_iota(jnp.int32, (NZ, NZ), 1)
    column = jnp.sum(jnp.where(cells == others, row, 0.0), axis=1, keepdims=True)
    return jnp.broadcast_to(column, (NZ, NY))


def start_kernel(
    seeds, own, low, high, correction, cells, heights, to_z, to_y,
    buffer, first_trial, source_out, initial_out, laplace_out, viscosity_out, rotor_out,
    column_out,
):
    span_shift = seeds[0, 0]
    height_shift = seeds[0, 1]
    profile = spread_profile(heights[...])
    column_out[...] = profile
    rotor = count_rotors(cells)
    for j in range(5):
        rotor_out[j] = rotor[j]
    viscosity = {}
    for j in range(-2, 5):
        if j < 0:
            raw = low[8 + j]
        elif j < 3:
            raw = correction[j]
        else:
            raw = high[3 + j]
        viscosity[j] = BASE_VISCOSITY * jnp.exp(raw)
        viscosity_out[j + 2] = viscosity[j]
    trial = []
    for c in range(3):
        state = {}
        for j in range(-2, 5):
            if j < 0:
                raw = low[2 * c + j + 2]
            elif j < 3:
                raw = own[c, j]
            else:
                raw = high[2 * c + j - 3]
            raw = pltpu.roll(pltpu.roll(raw, span_shift, 1), height_shift, 0)
            state[j] = raw + profile if c == 0 else raw
        moved = {}
        for j in range(-1, 4):
            curvature = laplace(state, j)
            forcing = (
                viscosity[j] * curvature
                - profile * along_stream(state, j)
                - THRUST * rotor[j + 1] * state[j]
            )
            moved[j] = state[j] + TIME_STEP * forcing
            first_trial[5 * c + j + 1] = moved[j]
            if c == 0:
                initial_out[j + 1] = state[j]
            elif 0 <= j < 3:
                initial_out[3 * c + 2 + j] = state[j]
            if 0 <= j < 3:
                laplace_out[3 * c + j] = curvature
        trial.append(moved)
    sources = [
        along_stream(trial[0], j) + along_span(trial[1][j]) + along_height(trial[2][j])
        for j in range(3)
    ]
    source_out[...] = sources[1]
    to_modes(sources, to_z, to_y, buffer)


def green_table(squares, squares_z):
    place = lax.broadcasted_iota(jnp.int32, (1, SPACE), 1)
    mine = jnp.where(place == lax.axis_index("space"), squares_z[...], 0.0)
    summed = squares[...] + jnp.sum(mine, axis=1, keepdims=True)
    null_mode = summed == 0.0
    return jnp.where(null_mode, 0.0, -1.0 / jnp.where(null_mode, 1.0, summed))


def solve_rows(modes_in, green, to_x, from_x, out):
    spectrum = left_product(to_x, gather_slots(modes_in, 0, 3, 3)) * green
    scatter_slots(out, left_product(from_x, spectrum), 0, 4, 4)


def solve_first_kernel(modes_in, squares, squares_z, to_x, from_x, out, green_out):
    green = green_table(squares, squares_z)
    green_out[...] = green
    solve_rows(modes_in, green, to_x, from_x, out)


def solve_kernel(modes_in, green, to_x, from_x, out):
    solve_rows(modes_in, green[...], to_x, from_x, out)


def middle_kernel(
    modes_in, first_trial, source, initial, viscosity, rotor, observed, column,
    from_z, from_y, to_z, to_y,
    buffer, second_trial, source_out, laplace_out,
):
    profile = column[...]
    pressure = with_plane_below(from_modes(modes_in, 4, from_z, from_y), source[...])
    span = {j: first_trial[6 + j] - along_span(pressure[j]) for j in range(-1, 4)}
    height = {j: first_trial[11 + j] - along_height(pressure[j]) for j in range(-1, 4)}
    stream = {j: first_trial[1 + j] - along_stream(pressure, j) for j in range(3)}
    cross = {j: along_span(span[j]) + along_height(height[j]) for j in range(-1, 4)}
    stream[-1] = stream[1] + 2.0 * cross[0]
    stream[3] = stream[1] - 2.0 * cross[2]
    stream[-2] = stream[0] + 2.0 * cross[-1]
    stream[4] = stream[2] - 2.0 * cross[3]
    trial = []
    for c, middle in enumerate((stream, span, height)):
        moved = {}
        for j in range(-1, 4) if c == 0 else range(3):
            start = initial[j + 1] if c == 0 else initial[3 * c + 2 + j]
            curvature = laplace(middle, j)
            forcing = (
                viscosity[j + 2] * curvature
                - profile * along_stream(middle, j)
                - THRUST * rotor[j + 1] * middle[j]
            )
            moved[j] = 0.5 * start + 0.5 * (middle[j] + TIME_STEP * forcing)
            if 0 <= j < 3:
                laplace_out[3 * c + j] = curvature
                second_trial[3 * c + j] = moved[j]
        trial.append(moved)
    sources = [
        along_stream(trial[0], j) + along_span(trial[1][j]) + along_height(trial[2][j])
        for j in range(3)
    ]
    source_out[...] = sources[1]
    sheets = [trial[0][j] - observed[j] for j in range(3)] + sources
    to_modes(sheets, to_z, to_y, buffer)


def solve_both_kernel(modes_in, green, sine_in, to_x, from_x, out):
    sine = sine_in[...]
    inverse = green[...]
    both = jnp.concatenate(
        [gather_slots(modes_in, 0, 3, 6), gather_slots(modes_in, 3, 3, 6)], axis=1
    )
    both = left_product(to_x, both)
    lead = both[:, :NY]
    second = inverse * both[:, NY:]
    third = inverse * swap_waves(lead - swap_waves(second, sine), sine)
    wide = left_product(from_x, jnp.concatenate([second, third], axis=1))
    scatter_slots(out, wide[:, :NY], 0, 4, 8)
    scatter_slots(out, wide[:, NY:], 4, 4, 8)


def adjoint_kernel(
    modes_in, second_trial, source, laplace_mid, viscosity, rotor, observed, column,
    from_z, from_y, to_z, to_y,
    buffer, fourth_trial, source_out, velocity, share_out,
):
    profile = column[...]
    found = from_modes(modes_in, 8, from_z, from_y)
    second = with_plane_below(found[:4], source[...])
    misfit = []
    for j in range(3):
        stream = second_trial[j] - along_stream(second, j)
        velocity[0, 0, j] = stream
        velocity[0, 1, j] = second_trial[3 + j] - along_span(second[j])
        velocity[0, 2, j] = second_trial[6 + j] - along_height(second[j])
        misfit.append(stream - observed[j])
    third = with_plane_below(found[4:], 0.5 * (misfit[2] - misfit[0]))
    span = {j: -along_span(third[j]) for j in range(-1, 4)}
    height = {j: -along_height(third[j]) for j in range(-1, 4)}
    cross = {j: along_span(span[j]) + along_height(height[j]) for j in range(-1, 4)}
    stream = {j: misfit[j] - along_stream(third, j) for j in range(3)}
    stream[-1] = stream[1] + 2.0 * cross[0]
    stream[3] = stream[1] - 2.0 * cross[2]
    stream[-2] = stream[0] + 2.0 * cross[-1]
    stream[4] = stream[2] - 2.0 * cross[3]
    share = [None] * 3
    trial = []
    for c, adjoint in enumerate((stream, span, height)):
        spread = {j: viscosity[j + 2] * adjoint[j] for j in adjoint}
        moved = {}
        for j in range(-1, 4) if c == 0 else range(3):
            pulled = (
                profile * along_stream(adjoint, j)
                + laplace(spread, j)
                - THRUST * rotor[j + 1] * adjoint[j]
            )
            moved[j] = 0.5 * adjoint[j] + 0.5 * TIME_STEP * pulled
        for j in range(3):
            fourth_trial[3 * c + j] = moved[j]
            term = adjoint[j] * laplace_mid[3 * c + j]
            share[j] = term if c == 0 else share[j] + term
        trial.append(moved)
    for j in range(3):
        share_out[j] = 0.5 * share[j]
    sources = [
        along_stream(trial[0], j) + along_span(trial[1][j]) + along_height(trial[2][j])
        for j in range(3)
    ]
    source_out[...] = sources[1]
    to_modes(sources, to_z, to_y, buffer)


def gradient_kernel(
    modes_in, fourth_trial, source, laplace_start, viscosity, share, from_z, from_y, out
):
    pressure = with_plane_below(from_modes(modes_in, 4, from_z, from_y), source[...])
    for j in range(3):
        push = [along_stream(pressure, j), along_span(pressure[j]), along_height(pressure[j])]
        total = share[j]
        for c in range(3):
            total = total + (fourth_trial[3 * c + j] - push[c]) * laplace_start[3 * c + j]
        total = TIME_STEP * viscosity[j + 2] * total
        for copy in range(out.shape[0]):
            out[copy, NZ * j : NZ * (j + 1), :] = total


def local_call(kernel, name, outs, *args):
    specs = [pl.BlockSpec(memory_space=pltpu.VMEM) for _ in args]
    if name == "start":
        specs[0] = pl.BlockSpec(memory_space=pltpu.SMEM)
    shapes = [jax.ShapeDtypeStruct(shape, F32) for shape in outs]
    spaces = [pl.BlockSpec(memory_space=pltpu.VMEM) for _ in outs]
    single = len(outs) == 1
    return pl.pallas_call(
        kernel,
        out_shape=shapes[0] if single else shapes,
        in_specs=specs,
        out_specs=spaces[0] if single else spaces,
        name=name,
        compiler_params=pltpu.CompilerParams(vmem_limit_bytes=24 * 1024 * 1024),
    )(*args)


def exchange(rows, axis="space"):
    count = lax.axis_size(axis)
    wide = rows.reshape(count, 1, rows.size // count)
    return lax.all_to_all(wide, axis, 0, 0, tiled=True).reshape(rows.shape)


def shards(inflow_seeds, rotor_cells, fluctuation, profile, correction, observed):
    samples = lax.axis_size("sample")
    forward = [(i, (i + 1) % SPACE) for i in range(SPACE)]
    backward = [(target, source) for source, target in forward]
    plane = (NZ, NY)
    last = jnp.concatenate([fluctuation[:, 1:].reshape(6, NZ, NY), correction[1:]], axis=0)
    first = jnp.concatenate([fluctuation[:, :2].reshape(6, NZ, NY), correction[:2]], axis=0)
    low = lax.ppermute(last, "space", forward)
    high = lax.ppermute(first, "space", backward)
    to_x, from_x = jnp.asarray(TO_X), jnp.asarray(FROM_X)
    to_y, from_y = jnp.asarray(TO_Y), jnp.asarray(FROM_Y)
    to_z, from_z = jnp.asarray(TO_Z), jnp.asarray(FROM_Z)

    buffer, first_trial, source, initial, laplace_start, viscosity, rotor, column = local_call(
        start_kernel, "start",
        [
            (SPACE * 3, NY), (15, *plane), plane, (11, *plane), (9, *plane), (7, *plane),
            (5, *plane), plane,
        ],
        inflow_seeds, fluctuation, low, high, correction, rotor_cells.T, profile[None, :],
        to_z, to_y,
    )
    buffer = exchange(buffer)
    buffer, green = local_call(
        solve_first_kernel, "solve_one", [(SPACE * 4, NY), (NX, NY)],
        buffer, jnp.asarray(SQUARES), jnp.asarray(SQUARES_Z), to_x, from_x,
    )
    buffer = exchange(buffer)
    buffer, second_trial, source, laplace_mid = local_call(
        middle_kernel, "middle",
        [(SPACE * 6, NY), (9, *plane), plane, (9, *plane)],
        buffer, first_trial, source, initial, viscosity, rotor, observed, column,
        from_z, from_y, to_z, to_y,
    )
    buffer = exchange(buffer)
    buffer = local_call(
        solve_both_kernel, "solve_two", [(SPACE * 8, NY)],
        buffer, green, jnp.asarray(SINE_X), to_x, from_x,
    )
    buffer = exchange(buffer)
    buffer, fourth_trial, source, velocity, share = local_call(
        adjoint_kernel, "adjoint",
        [(SPACE * 3, NY), (9, *plane), plane, (1, 3, 3, *plane), (3, *plane)],
        buffer, second_trial, source, laplace_mid, viscosity, rotor, observed, column,
        from_z, from_y, to_z, to_y,
    )
    buffer = exchange(buffer)
    buffer = local_call(
        solve_kernel, "solve_four", [(SPACE * 4, NY)], buffer, green, to_x, from_x
    )
    buffer = exchange(buffer)
    terms = local_call(
        gradient_kernel, "gradient", [(samples, SLAB * NZ, NY)],
        buffer, fourth_trial, source, laplace_start, viscosity, share, from_z, from_y,
    )
    terms = lax.all_to_all(terms, "sample", 0, 0, tiled=True)
    gradient = jnp.sum(terms, axis=0).reshape(SLAB, *plane)
    return (velocity, gradient)


def solution(mesh):
    return jax.shard_map(
        shards,
        mesh=mesh,
        in_specs=(
            P("sample", None),
            P(),
            P(None, "space", None, None),
            P(),
            P("space", None, None),
            P("space", None, None),
        ),
        out_specs=(P("sample", None, "space", None, None), P("space", None, None)),
        check_vma=False,
    )
```

```python
import functools
import math

import jax
import jax.numpy as jnp
import ml_dtypes
import numpy as np
from jax import lax
from jax.experimental import pallas as pl
from jax.experimental.pallas import tpu as pltpu
from jax.sharding import PartitionSpec as P

NX = 192
NY = 128
NZ = 48
ROTOR = 8
SPACE = 64
SLAB = NX // SPACE

TIME_STEP = 0.2
BASE_VISCOSITY = 0.15
THRUST = 1.0
F32 = jnp.float32
BF16 = jnp.bfloat16


def real_basis(length):
    half = length // 2
    cells = np.arange(length)[:, None]
    waves = np.arange(half)[None, :]
    phase = 2.0 * np.pi / length * ((cells * waves) % length)
    even = np.cos(phase) * math.sqrt(2.0 / length)
    even[:, 0] = math.sqrt(1.0 / length)
    odd = np.sin(phase) * math.sqrt(2.0 / length)
    odd[:, 0] = (1.0 - 2.0 * (np.arange(length) % 2)) * math.sqrt(1.0 / length)
    return np.concatenate([even, odd], axis=1)


def sine_of(length):
    half = length // 2
    waves = np.arange(length) % half
    return np.sin(2.0 * np.pi / length * waves)


def in_parts(matrix, count):
    parts = []
    rest = np.asarray(matrix, np.float64)
    for _ in range(count):
        parts.append(rest.astype(ml_dtypes.bfloat16))
        rest = rest - parts[-1].astype(np.float64)
    return np.stack(parts)


BASIS_X = real_basis(NX)
BASIS_Y = real_basis(NY)
BASIS_Z = real_basis(NZ)


def stream_rows(first, count):
    device = np.arange(SPACE)[None, :]
    slot = np.arange(first, first + count)[:, None]
    return ((SLAB * device + slot) % NX).reshape(-1)


TO_Y = in_parts(BASIS_Y, 2)
TO_Z = in_parts(BASIS_Z.T, 2)
TO_X = in_parts(BASIS_X[stream_rows(0, 3)].T, 2)
FROM_Y = in_parts(BASIS_Y.T, 3)
FROM_Z = in_parts(BASIS_Z, 3)
FROM_X = in_parts(BASIS_X[stream_rows(0, 4)], 3)
SINE_X = np.broadcast_to(sine_of(NX)[:, None], (NX, NY)).astype(np.float32)
SQUARES = np.zeros((NX + 8, NY), np.float32)
SQUARES[:NX] = sine_of(NX)[:, None] ** 2 + sine_of(NY)[None, :] ** 2
SQUARES[NX, :NZ] = sine_of(NZ) ** 2


def split(value, count):
    parts = []
    for _ in range(count - 1):
        parts.append(value.astype(BF16))
        value = value - parts[-1].astype(F32)
    return parts + [value.astype(BF16)]


def dot(a, b):
    return jnp.dot(a, b, preferred_element_type=F32)


def left_product(matrix, value):
    count = matrix.shape[0]
    parts = split(value, count)
    pairs = [(i, order - i) for order in reversed(range(count)) for i in range(order + 1)]
    return sum(dot(matrix[i], parts[k]) for i, k in pairs)


def right_product(value, matrix):
    count = matrix.shape[0]
    parts = split(value, count)
    pairs = [(i, order - i) for order in reversed(range(count)) for i in range(order + 1)]
    return sum(dot(parts[k], matrix[i]) for i, k in pairs)


def up_z(f):
    return pltpu.roll(f, NZ - 1, 0)


def down_z(f):
    return pltpu.roll(f, 1, 0)


def up_y(f):
    return pltpu.roll(f, NY - 1, 1)


def down_y(f):
    return pltpu.roll(f, 1, 1)


def along_height(f):
    return 0.5 * (up_z(f) - down_z(f))


def along_span(f):
    return 0.5 * (up_y(f) - down_y(f))


def along_stream(planes, j):
    return 0.5 * (planes[j + 1] - planes[j - 1])


def laplace(planes, j):
    f = planes[j]
    summed = planes[j + 1] + planes[j - 1] + up_z(f) + down_z(f) + up_y(f) + down_y(f)
    return summed - 6.0 * f


def cross_laplace(f):
    return along_span(along_span(f)) + along_height(along_height(f))


def with_plane_below(planes, source):
    below = 2.0 * planes[1] - planes[3] + 4.0 * (source - cross_laplace(planes[1]))
    return {-1: below, 0: planes[0], 1: planes[1], 2: planes[2], 3: planes[3]}


def to_modes(planes, to_z, to_y, out_ref):
    count = len(planes)
    side = left_product(to_z, jnp.concatenate(planes, axis=1))
    rows = jnp.concatenate([side[:, NY * i : NY * (i + 1)] for i in range(count)], axis=0)
    rows = right_product(rows, to_y)
    for i in range(count):
        out_ref[pl.ds(i, NZ, stride=count), :] = rows[NZ * i : NZ * (i + 1)]
    out_ref[NZ * count :, :] = jnp.zeros(((SPACE - NZ) * count, NY), F32)


def from_modes(in_ref, count, from_z, from_y):
    rows = jnp.concatenate([in_ref[pl.ds(i, NZ, stride=count), :] for i in range(count)], axis=0)
    rows = right_product(rows, from_y)
    side = jnp.concatenate([rows[NZ * i : NZ * (i + 1)] for i in range(count)], axis=1)
    side = left_product(from_z, side)
    return [side[:, NY * i : NY * (i + 1)] for i in range(count)]


def gather_slots(in_ref, first, count, total):
    parts = [in_ref[pl.ds(i, SPACE, stride=total), :] for i in range(first, first + count)]
    return jnp.concatenate(parts, axis=0)


def scatter_slots(out_ref, rows, first, count, total):
    for i in range(count):
        out_ref[pl.ds(first + i, SPACE, stride=total), :] = rows[SPACE * i : SPACE * (i + 1)]


def swap_waves(modes, sine):
    half = NX // 2
    return jnp.concatenate([sine[:half] * modes[half:], -sine[half:] * modes[:half]], axis=0)


def count_rotors(cells):
    stream = cells[0:1, :]
    span = cells[1:2, :]
    base = cells[2:3, :]
    turbines = cells.shape[1]
    spans = lax.broadcasted_iota(jnp.int32, (NY, turbines), 0)
    in_span = ((spans >= span) & (spans < span + ROTOR)).astype(F32).astype(BF16)
    heights = lax.broadcasted_iota(jnp.int32, (NZ, turbines), 0)
    in_height = (heights >= base) & (heights < base + ROTOR)
    first = lax.axis_index("space") * SLAB
    sheets = []
    for j in range(-1, 4):
        here = stream == lax.rem(first + (j + NX), NX)
        sheets.append((in_height & here).astype(F32).astype(BF16))
    counted = lax.dot_general(
        jnp.concatenate(sheets, axis=0), in_span, (((1,), (1,)), ((), ())),
        preferred_element_type=F32,
    )
    return [counted[NZ * i : NZ * (i + 1)] for i in range(5)]


def spread_profile(row):
    cells = lax.broadcasted_iota(jnp.int32, (NZ, NZ), 0)
    others = lax.broadcasted_iota(jnp.int32, (NZ, NZ), 1)
    column = jnp.sum(jnp.where(cells == others, row, 0.0), axis=1, keepdims=True)
    return jnp.broadcast_to(column, (NZ, NY))


def pack_kernel(own, correction, inner, outer, arrived):
    even = lax.rem(lax.axis_index("space"), 2) == 0

    def fill(first, last):
        copies = []
        for i, (target, start) in enumerate(((last, 1), (first, 0))):
            planes = pl.ds(start, 2)
            copies.append(
                pltpu.make_async_copy(own.at[:, planes], target.at[0:3], arrived.at[2 * i])
            )
            copies.append(
                pltpu.make_async_copy(
                    correction.at[planes], target.at[3], arrived.at[2 * i + 1]
                )
            )
        for copy in copies:
            copy.start()
        for copy in copies:
            copy.wait()

    @pl.when(even)
    def _():
        fill(outer, inner)

    @pl.when(jnp.logical_not(even))
    def _():
        fill(inner, outer)


def rolled(plane, seeds):
    return pltpu.roll(pltpu.roll(plane, seeds[0, 0], 1), seeds[0, 1], 0)


def prepare_kernel(
    seeds, own, correction, cells, heights, state_out, viscosity_out, rotor_out, column_out
):
    profile = spread_profile(heights[...])
    column_out[...] = profile
    rotor = count_rotors(cells)
    for j in range(5):
        rotor_out[j] = rotor[j]
    for j in range(3):
        viscosity_out[j] = BASE_VISCOSITY * jnp.exp(correction[j])
        for c in range(3):
            plane = rolled(own[c, j], seeds)
            state_out[3 * c + j] = plane + profile if c == 0 else plane


def start_kernel(
    seeds, inner, outer, own_state, own_viscosity, rotor, column, to_z, to_y,
    buffer, first_trial, source_out, beside_out, laplace_out, viscosity_out,
):
    even = lax.rem(lax.axis_index("space"), 2) == 0
    profile = column[...]

    def halo(j, c):
        i = j + 2 if j < 0 else j - 3
        low = outer if j < 0 else inner
        high = inner if j < 0 else outer
        return jnp.where(even, low[c, i], high[c, i])

    viscosity = {}
    for j in range(-2, 5):
        if 0 <= j < 3:
            viscosity[j] = own_viscosity[j]
        else:
            viscosity[j] = BASE_VISCOSITY * jnp.exp(halo(j, 3))
        viscosity_out[j + 2] = viscosity[j]
    trial = []
    for c in range(3):
        state = {}
        for j in range(-2, 5):
            if 0 <= j < 3:
                state[j] = own_state[3 * c + j]
            else:
                state[j] = rolled(halo(j, c), seeds)
                if c == 0:
                    state[j] = state[j] + profile
        moved = {}
        for j in range(-1, 4):
            curvature = laplace(state, j)
            forcing = (
                viscosity[j] * curvature
                - profile * along_stream(state, j)
                - THRUST * rotor[j + 1] * state[j]
            )
            moved[j] = state[j] + TIME_STEP * forcing
            first_trial[5 * c + j + 1] = moved[j]
            if 0 <= j < 3:
                laplace_out[3 * c + j] = curvature
        trial.append(moved)
        if c == 0:
            beside_out[0] = state[-1]
            beside_out[1] = state[3]
    sources = [
        along_stream(trial[0], j) + along_span(trial[1][j]) + along_height(trial[2][j])
        for j in range(3)
    ]
    source_out[...] = sources[1]
    to_modes(sources, to_z, to_y, buffer)


def green_table(squares):
    place = lax.broadcasted_iota(jnp.int32, (1, NY), 1)
    mine = jnp.where(place == lax.axis_index("space"), squares[NX : NX + 1, :], 0.0)
    summed = squares[:NX, :] + jnp.sum(mine, axis=1, keepdims=True)
    null_mode = summed == 0.0
    return jnp.where(null_mode, 0.0, -1.0 / jnp.where(null_mode, 1.0, summed))


def solve_rows(modes_in, green, to_x, from_x, out):
    spectrum = left_product(to_x, gather_slots(modes_in, 0, 3, 3)) * green
    scatter_slots(out, left_product(from_x, spectrum), 0, 4, 4)


def solve_first_kernel(modes_in, squares, to_x, from_x, out, green_out):
    green = green_table(squares)
    green_out[...] = green
    solve_rows(modes_in, green, to_x, from_x, out)


def solve_kernel(modes_in, green, to_x, from_x, out):
    solve_rows(modes_in, green[...], to_x, from_x, out)


def middle_kernel(
    modes_in, first_trial, source, state, beside, viscosity, rotor, observed, column,
    from_z, from_y, to_z, to_y,
    buffer, second_trial, source_out, laplace_out,
):
    profile = column[...]
    pressure = with_plane_below(from_modes(modes_in, 4, from_z, from_y), source[...])
    span = {j: first_trial[6 + j] - along_span(pressure[j]) for j in range(-1, 4)}
    height = {j: first_trial[11 + j] - along_height(pressure[j]) for j in range(-1, 4)}
    stream = {j: first_trial[1 + j] - along_stream(pressure, j) for j in range(3)}
    cross = {j: along_span(span[j]) + along_height(height[j]) for j in range(-1, 4)}
    stream[-1] = stream[1] + 2.0 * cross[0]
    stream[3] = stream[1] - 2.0 * cross[2]
    stream[-2] = stream[0] + 2.0 * cross[-1]
    stream[4] = stream[2] - 2.0 * cross[3]
    trial = []
    for c, middle in enumerate((stream, span, height)):
        moved = {}
        for j in range(-1, 4) if c == 0 else range(3):
            start = state[3 * c + j] if 0 <= j < 3 else beside[0 if j < 0 else 1]
            curvature = laplace(middle, j)
            forcing = (
                viscosity[j + 2] * curvature
                - profile * along_stream(middle, j)
                - THRUST * rotor[j + 1] * middle[j]
            )
            moved[j] = 0.5 * start + 0.5 * (middle[j] + TIME_STEP * forcing)
            if 0 <= j < 3:
                laplace_out[3 * c + j] = curvature
                second_trial[3 * c + j] = moved[j]
        trial.append(moved)
    sources = [
        along_stream(trial[0], j) + along_span(trial[1][j]) + along_height(trial[2][j])
        for j in range(3)
    ]
    source_out[...] = sources[1]
    sheets = [trial[0][j] - observed[j] for j in range(3)] + sources
    to_modes(sheets, to_z, to_y, buffer)


def solve_both_kernel(modes_in, green, sine_in, to_x, from_x, out):
    sine = sine_in[...]
    inverse = green[...]
    both = jnp.concatenate(
        [gather_slots(modes_in, 0, 3, 6), gather_slots(modes_in, 3, 3, 6)], axis=1
    )
    both = left_product(to_x, both)
    lead = both[:, :NY]
    second = inverse * both[:, NY:]
    third = inverse * swap_waves(lead - swap_waves(second, sine), sine)
    wide = left_product(from_x, jnp.concatenate([second, third], axis=1))
    scatter_slots(out, wide[:, :NY], 0, 4, 8)
    scatter_slots(out, wide[:, NY:], 4, 4, 8)


def adjoint_kernel(
    modes_in, second_trial, source, laplace_mid, viscosity, rotor, observed, column,
    from_z, from_y, to_z, to_y,
    buffer, fourth_trial, source_out, velocity, share_out,
):
    profile = column[...]
    found = from_modes(modes_in, 8, from_z, from_y)
    second = with_plane_below(found[:4], source[...])
    misfit = []
    for j in range(3):
        stream = second_trial[j] - along_stream(second, j)
        velocity[0, 0, j] = stream
        velocity[0, 1, j] = second_trial[3 + j] - along_span(second[j])
        velocity[0, 2, j] = second_trial[6 + j] - along_height(second[j])
        misfit.append(stream - observed[j])
    third = with_plane_below(found[4:], 0.5 * (misfit[2] - misfit[0]))
    span = {j: -along_span(third[j]) for j in range(-1, 4)}
    height = {j: -along_height(third[j]) for j in range(-1, 4)}
    cross = {j: along_span(span[j]) + along_height(height[j]) for j in range(-1, 4)}
    stream = {j: misfit[j] - along_stream(third, j) for j in range(3)}
    stream[-1] = stream[1] + 2.0 * cross[0]
    stream[3] = stream[1] - 2.0 * cross[2]
    stream[-2] = stream[0] + 2.0 * cross[-1]
    stream[4] = stream[2] - 2.0 * cross[3]
    share = [None] * 3
    trial = []
    for c, adjoint in enumerate((stream, span, height)):
        spread = {j: viscosity[j + 2] * adjoint[j] for j in adjoint}
        moved = {}
        for j in range(-1, 4) if c == 0 else range(3):
            pulled = (
                profile * along_stream(adjoint, j)
                + laplace(spread, j)
                - THRUST * rotor[j + 1] * adjoint[j]
            )
            moved[j] = 0.5 * adjoint[j] + 0.5 * TIME_STEP * pulled
        for j in range(3):
            fourth_trial[3 * c + j] = moved[j]
            term = adjoint[j] * laplace_mid[3 * c + j]
            share[j] = term if c == 0 else share[j] + term
        trial.append(moved)
    for j in range(3):
        share_out[j] = 0.5 * share[j]
    sources = [
        along_stream(trial[0], j) + along_span(trial[1][j]) + along_height(trial[2][j])
        for j in range(3)
    ]
    source_out[...] = sources[1]
    to_modes(sources, to_z, to_y, buffer)


def gradient_kernel(
    modes_in, fourth_trial, source, laplace_start, viscosity, share, from_z, from_y, out
):
    pressure = with_plane_below(from_modes(modes_in, 4, from_z, from_y), source[...])
    for j in range(3):
        push = [along_stream(pressure, j), along_span(pressure[j]), along_height(pressure[j])]
        total = share[j]
        for c in range(3):
            total = total + (fourth_trial[3 * c + j] - push[c]) * laplace_start[3 * c + j]
        total = TIME_STEP * viscosity[j + 2] * total
        for copy in range(out.shape[0]):
            out[copy, NZ * j : NZ * (j + 1), :] = total


def local_call(kernel, outs, *args, spaces={}, scratch=()):
    specs = [pl.BlockSpec(memory_space=spaces.get(i, pltpu.VMEM)) for i in range(len(args))]
    shapes = [jax.ShapeDtypeStruct(shape, F32) for shape in outs]
    out_specs = [pl.BlockSpec(memory_space=pltpu.VMEM) for _ in outs]
    single = len(outs) == 1
    return pl.pallas_call(
        kernel,
        out_shape=shapes[0] if single else shapes,
        in_specs=specs,
        out_specs=out_specs[0] if single else out_specs,
        scratch_shapes=scratch,
        name=kernel.__name__,
        compiler_params=pltpu.CompilerParams(vmem_limit_bytes=24 * 1024 * 1024),
    )(*args)


def exchange(rows, axis="space"):
    count = lax.axis_size(axis)
    wide = rows.reshape(count, 1, rows.size // count)
    return lax.all_to_all(wide, axis, 0, 0, tiled=True).reshape(rows.shape)


def shards(inflow_seeds, rotor_cells, fluctuation, profile, correction, observed):
    samples = lax.axis_size("sample")
    within = [(i, i + 1 - 2 * (i % 2)) for i in range(SPACE)]
    between = [(i, (i - 1 + 2 * (i % 2)) % SPACE) for i in range(SPACE)]
    plane = (NZ, NY)
    inner, outer = local_call(
        pack_kernel, [(4, 2, *plane), (4, 2, *plane)],
        pltpu.with_memory_space_constraint(fluctuation, pltpu.HBM),
        pltpu.with_memory_space_constraint(correction, pltpu.HBM),
        spaces={0: pltpu.HBM, 1: pltpu.HBM}, scratch=[pltpu.SemaphoreType.DMA((4,))],
    )
    inner = lax.ppermute(inner, "space", within)
    outer = lax.ppermute(outer, "space", between)
    to_x, from_x = jnp.asarray(TO_X), jnp.asarray(FROM_X)
    to_y, from_y = jnp.asarray(TO_Y), jnp.asarray(FROM_Y)
    to_z, from_z = jnp.asarray(TO_Z), jnp.asarray(FROM_Z)

    state, viscosity, rotor, column = local_call(
        prepare_kernel, [(9, *plane), (3, *plane), (5, *plane), plane],
        inflow_seeds, fluctuation, correction, rotor_cells.T, profile[None, :],
        spaces={0: pltpu.SMEM},
    )
    buffer, first_trial, source, beside, laplace_start, viscosity = local_call(
        start_kernel,
        [(SPACE * 3, NY), (15, *plane), plane, (2, *plane), (9, *plane), (7, *plane)],
        inflow_seeds, inner, outer, state, viscosity, rotor, column, to_z, to_y,
        spaces={0: pltpu.SMEM},
    )
    buffer = exchange(buffer)
    buffer, green = local_call(
        solve_first_kernel, [(SPACE * 4, NY), (NX, NY)],
        buffer, jnp.asarray(SQUARES), to_x, from_x,
    )
    buffer = exchange(buffer)
    buffer, second_trial, source, laplace_mid = local_call(
        middle_kernel,
        [(SPACE * 6, NY), (9, *plane), plane, (9, *plane)],
        buffer, first_trial, source, state, beside, viscosity, rotor, observed, column,
        from_z, from_y, to_z, to_y,
    )
    buffer = exchange(buffer)
    buffer = local_call(
        solve_both_kernel, [(SPACE * 8, NY)],
        buffer, green, jnp.asarray(SINE_X), to_x, from_x,
    )
    buffer = exchange(buffer)
    buffer, fourth_trial, source, velocity, share = local_call(
        adjoint_kernel,
        [(SPACE * 3, NY), (9, *plane), plane, (1, 3, 3, *plane), (3, *plane)],
        buffer, second_trial, source, laplace_mid, viscosity, rotor, observed, column,
        from_z, from_y, to_z, to_y,
    )
    buffer = exchange(buffer)
    buffer = local_call(
        solve_kernel, [(SPACE * 4, NY)], buffer, green, to_x, from_x
    )
    buffer = exchange(buffer)
    terms = local_call(
        gradient_kernel, [(samples, SLAB * NZ, NY)],
        buffer, fourth_trial, source, laplace_start, viscosity, share, from_z, from_y,
    )
    terms = lax.all_to_all(terms, "sample", 0, 0, tiled=True)
    gradient = jnp.sum(terms, axis=0).reshape(SLAB, *plane)
    return (velocity, gradient)


def solution(mesh):
    return jax.shard_map(
        shards,
        mesh=mesh,
        in_specs=(
            P("sample", None),
            P(),
            P(None, "space", None, None),
            P(),
            P("space", None, None),
            P("space", None, None),
        ),
        out_specs=(P("sample", None, "space", None, None), P("space", None, None)),
        check_vma=False,
    )
```

```python
import functools
import math

import jax
import jax.numpy as jnp
import ml_dtypes
import numpy as np
from jax import lax
from jax.experimental import pallas as pl
from jax.experimental.pallas import tpu as pltpu
from jax.sharding import PartitionSpec as P

NX = 192
NY = 128
NZ = 48
ROTOR = 8
SPACE = 64
SLAB = NX // SPACE

TIME_STEP = 0.2
BASE_VISCOSITY = 0.15
THRUST = 1.0
F32 = jnp.float32
BF16 = jnp.bfloat16


def real_basis(length):
    half = length // 2
    cells = np.arange(length)[:, None]
    waves = np.arange(half)[None, :]
    phase = 2.0 * np.pi / length * ((cells * waves) % length)
    even = np.cos(phase) * math.sqrt(2.0 / length)
    even[:, 0] = math.sqrt(1.0 / length)
    odd = np.sin(phase) * math.sqrt(2.0 / length)
    odd[:, 0] = (1.0 - 2.0 * (np.arange(length) % 2)) * math.sqrt(1.0 / length)
    return np.concatenate([even, odd], axis=1)


def sine_of(length):
    half = length // 2
    waves = np.arange(length) % half
    return np.sin(2.0 * np.pi / length * waves)


def in_parts(matrix, count):
    parts = []
    rest = np.asarray(matrix, np.float64)
    for _ in range(count):
        parts.append(rest.astype(ml_dtypes.bfloat16))
        rest = rest - parts[-1].astype(np.float64)
    return np.stack(parts)


BASIS_X = real_basis(NX)
BASIS_Y = real_basis(NY)
BASIS_Z = real_basis(NZ)


def stream_rows(first, count):
    device = np.arange(SPACE)[None, :]
    slot = np.arange(first, first + count)[:, None]
    return ((SLAB * device + slot) % NX).reshape(-1)


def pairs_of(count):
    return [(i, order - i) for order in reversed(range(count)) for i in range(order + 1)]


def left_table(matrix, count):
    parts = in_parts(matrix, count)
    return np.concatenate([parts[i] for i, _ in pairs_of(count)], axis=1)


def left_narrow_table(matrix, count):
    parts = list(in_parts(matrix, count))
    return np.concatenate(parts if count == 2 else parts + parts[:1], axis=1)


def right_table(matrix, count):
    parts = list(in_parts(matrix, count))
    none = np.zeros_like(parts[0])
    if count == 2:
        rows = [(parts[0], parts[1]), (parts[0], none)]
    else:
        rows = [(parts[0], parts[1]), (parts[0], parts[1]), (parts[0], none), (parts[2], none)]
    return np.concatenate([np.concatenate(row, axis=1) for row in rows], axis=0)


TO_Y = right_table(BASIS_Y, 2)
TO_Z = left_table(BASIS_Z.T, 2)
TO_X = left_narrow_table(BASIS_X[stream_rows(0, 3)].T, 2)
TO_X_WIDE = left_table(BASIS_X[stream_rows(0, 3)].T, 2)
FROM_Y = right_table(BASIS_Y.T, 3)
FROM_Z = left_table(BASIS_Z, 3)
FROM_X = left_narrow_table(BASIS_X[stream_rows(0, 4)], 3)
FROM_X_WIDE = left_table(BASIS_X[stream_rows(0, 4)], 3)
SINE_X = np.broadcast_to(sine_of(NX)[:, None], (NX, NY)).astype(np.float32)
SQUARES = np.zeros((NX + 8, NY), np.float32)
SQUARES[:NX] = sine_of(NX)[:, None] ** 2 + sine_of(NY)[None, :] ** 2
SQUARES[NX, :NZ] = sine_of(NZ) ** 2


def split(value, count):
    parts = []
    for _ in range(count - 1):
        parts.append(value.astype(BF16))
        value = value - parts[-1].astype(F32)
    return parts + [value.astype(BF16)]


def dot(a, b):
    return jnp.dot(a, b, preferred_element_type=F32)


def left_product(table, value, count):
    parts = split(value, count)
    return dot(table[...], jnp.concatenate([parts[k] for _, k in pairs_of(count)], axis=0))


def left_narrow_product(table, value, count):
    parts = split(value, count)
    none = jnp.zeros_like(parts[0])
    if count == 2:
        rows = [(parts[0], parts[1]), (parts[0], none)]
    else:
        rows = [(parts[0], parts[1]), (parts[0], parts[1]), (parts[0], none), (none, parts[2])]
    wide = jnp.concatenate([jnp.concatenate(row, axis=1) for row in rows], axis=0)
    found = dot(table[...], wide)
    return found[:, :NY] + found[:, NY:]


def right_product(value, table, count):
    parts = split(value, count)
    wide = jnp.concatenate(parts if count == 2 else parts + parts[:1], axis=1)
    found = dot(wide, table[...])
    return found[:, :NY] + found[:, NY:]


def up_z(f):
    return pltpu.roll(f, NZ - 1, 0)


def down_z(f):
    return pltpu.roll(f, 1, 0)


def up_y(f):
    return pltpu.roll(f, NY - 1, 1)


def down_y(f):
    return pltpu.roll(f, 1, 1)


def along_height(f):
    return 0.5 * (up_z(f) - down_z(f))


def along_span(f):
    return 0.5 * (up_y(f) - down_y(f))


def along_stream(planes, j):
    return 0.5 * (planes[j + 1] - planes[j - 1])


def laplace(planes, j):
    f = planes[j]
    summed = planes[j + 1] + planes[j - 1] + up_z(f) + down_z(f) + up_y(f) + down_y(f)
    return summed - 6.0 * f


def cross_laplace(f):
    return along_span(along_span(f)) + along_height(along_height(f))


def with_plane_below(planes, source):
    below = 2.0 * planes[1] - planes[3] + 4.0 * (source - cross_laplace(planes[1]))
    return {-1: below, 0: planes[0], 1: planes[1], 2: planes[2], 3: planes[3]}


def to_modes(planes, to_z, to_y, out_ref):
    count = len(planes)
    side = left_product(to_z, jnp.concatenate(planes, axis=1), 2)
    rows = jnp.concatenate([side[:, NY * i : NY * (i + 1)] for i in range(count)], axis=0)
    rows = right_product(rows, to_y, 2)
    for i in range(count):
        out_ref[pl.ds(i, NZ, stride=count), :] = rows[NZ * i : NZ * (i + 1)]
    out_ref[NZ * count :, :] = jnp.zeros(((SPACE - NZ) * count, NY), F32)


def from_modes(in_ref, count, from_z, from_y):
    rows = jnp.concatenate([in_ref[pl.ds(i, NZ, stride=count), :] for i in range(count)], axis=0)
    rows = right_product(rows, from_y, 3)
    side = jnp.concatenate([rows[NZ * i : NZ * (i + 1)] for i in range(count)], axis=1)
    side = left_product(from_z, side, 3)
    return [side[:, NY * i : NY * (i + 1)] for i in range(count)]


def gather_slots(in_ref, first, count, total):
    parts = [in_ref[pl.ds(i, SPACE, stride=total), :] for i in range(first, first + count)]
    return jnp.concatenate(parts, axis=0)


def scatter_slots(out_ref, rows, first, count, total):
    for i in range(count):
        out_ref[pl.ds(first + i, SPACE, stride=total), :] = rows[SPACE * i : SPACE * (i + 1)]


def swap_waves(modes, sine):
    half = NX // 2
    return jnp.concatenate([sine[:half] * modes[half:], -sine[half:] * modes[:half]], axis=0)


def count_rotors(cells):
    stream = cells[0:1, :]
    span = cells[1:2, :]
    base = cells[2:3, :]
    turbines = cells.shape[1]
    spans = lax.broadcasted_iota(jnp.int32, (NY, turbines), 0)
    in_span = ((spans >= span) & (spans < span + ROTOR)).astype(F32).astype(BF16)
    heights = lax.broadcasted_iota(jnp.int32, (NZ, turbines), 0)
    in_height = (heights >= base) & (heights < base + ROTOR)
    first = lax.axis_index("space") * SLAB
    sheets = []
    for j in range(-1, 4):
        here = stream == lax.rem(first + (j + NX), NX)
        sheets.append((in_height & here).astype(F32).astype(BF16))
    counted = lax.dot_general(
        jnp.concatenate(sheets, axis=0), in_span, (((1,), (1,)), ((), ())),
        preferred_element_type=F32,
    )
    return [counted[NZ * i : NZ * (i + 1)] for i in range(5)]


def spread_profile(row):
    cells = lax.broadcasted_iota(jnp.int32, (NZ, NZ), 0)
    others = lax.broadcasted_iota(jnp.int32, (NZ, NZ), 1)
    column = jnp.sum(jnp.where(cells == others, row, 0.0), axis=1, keepdims=True)
    return jnp.broadcast_to(column, (NZ, NY))


def pack_kernel(own, correction, inner, outer, arrived):
    even = lax.rem(lax.axis_index("space"), 2) == 0

    def fill(first, last):
        copies = []
        for i, (target, start) in enumerate(((last, 1), (first, 0))):
            planes = pl.ds(start, 2)
            copies.append(
                pltpu.make_async_copy(own.at[:, planes], target.at[0:3], arrived.at[2 * i])
            )
            copies.append(
                pltpu.make_async_copy(
                    correction.at[planes], target.at[3], arrived.at[2 * i + 1]
                )
            )
        for copy in copies:
            copy.start()
        for copy in copies:
            copy.wait()

    @pl.when(even)
    def _():
        fill(outer, inner)

    @pl.when(jnp.logical_not(even))
    def _():
        fill(inner, outer)


def rolled(plane, shifts):
    return pltpu.roll(pltpu.roll(plane, shifts[0], 1), shifts[1], 0)


def shifts_of(seeds):
    row = seeds[...]
    return row[0, 0], row[0, 1]


def prepare_kernel(
    seeds, own, correction, cells, heights, state_out, viscosity_out, rotor_out, column_out
):
    shifts = shifts_of(seeds)
    profile = spread_profile(heights[...])
    column_out[...] = profile
    rotor = count_rotors(cells)
    for j in range(5):
        rotor_out[j] = rotor[j]
    for j in range(3):
        viscosity_out[j] = BASE_VISCOSITY * jnp.exp(correction[j])
        for c in range(3):
            plane = rolled(own[c, j], shifts)
            state_out[3 * c + j] = plane + profile if c == 0 else plane


def start_kernel(
    seeds, inner, outer, own_state, own_viscosity, rotor, column, to_z, to_y,
    buffer, first_trial, source_out, beside_out, laplace_out, viscosity_out,
):
    even = lax.rem(lax.axis_index("space"), 2) == 0
    shifts = shifts_of(seeds)
    profile = column[...]

    def halo(j, c):
        i = j + 2 if j < 0 else j - 3
        low = outer if j < 0 else inner
        high = inner if j < 0 else outer
        return jnp.where(even, low[c, i], high[c, i])

    viscosity = {}
    for j in range(-2, 5):
        if 0 <= j < 3:
            viscosity[j] = own_viscosity[j]
        else:
            viscosity[j] = BASE_VISCOSITY * jnp.exp(halo(j, 3))
        viscosity_out[j + 2] = viscosity[j]
    trial = []
    for c in range(3):
        state = {}
        for j in range(-2, 5):
            if 0 <= j < 3:
                state[j] = own_state[3 * c + j]
            else:
                state[j] = rolled(halo(j, c), shifts)
                if c == 0:
                    state[j] = state[j] + profile
        moved = {}
        for j in range(-1, 4):
            curvature = laplace(state, j)
            forcing = (
                viscosity[j] * curvature
                - profile * along_stream(state, j)
                - THRUST * rotor[j + 1] * state[j]
            )
            moved[j] = state[j] + TIME_STEP * forcing
            first_trial[5 * c + j + 1] = moved[j]
            if 0 <= j < 3:
                laplace_out[3 * c + j] = curvature
        trial.append(moved)
        if c == 0:
            beside_out[0] = state[-1]
            beside_out[1] = state[3]
    sources = [
        along_stream(trial[0], j) + along_span(trial[1][j]) + along_height(trial[2][j])
        for j in range(3)
    ]
    source_out[...] = sources[1]
    to_modes(sources, to_z, to_y, buffer)


def green_table(squares):
    place = lax.broadcasted_iota(jnp.int32, (1, NY), 1)
    mine = jnp.where(place == lax.axis_index("space"), squares[NX : NX + 1, :], 0.0)
    summed = squares[:NX, :] + jnp.sum(mine, axis=1, keepdims=True)
    null_mode = summed == 0.0
    return jnp.where(null_mode, 0.0, -1.0 / jnp.where(null_mode, 1.0, summed))


def solve_rows(modes_in, green, to_x, from_x, out):
    spectrum = left_narrow_product(to_x, gather_slots(modes_in, 0, 3, 3), 2) * green
    scatter_slots(out, left_narrow_product(from_x, spectrum, 3), 0, 4, 4)


def solve_first_kernel(modes_in, squares, to_x, from_x, out, green_out):
    green = green_table(squares)
    green_out[...] = green
    solve_rows(modes_in, green, to_x, from_x, out)


def solve_last_kernel(modes_in, green, to_x, from_x, velocity, out, velocity_out, sent):
    copy = pltpu.make_async_copy(velocity, velocity_out, sent)
    copy.start()
    solve_rows(modes_in, green[...], to_x, from_x, out)
    copy.wait()


def middle_kernel(
    modes_in, first_trial, source, state, beside, viscosity, rotor, observed, column,
    from_z, from_y, to_z, to_y,
    buffer, second_trial, source_out, laplace_out,
):
    profile = column[...]
    pressure = with_plane_below(from_modes(modes_in, 4, from_z, from_y), source[...])
    span = {j: first_trial[6 + j] - along_span(pressure[j]) for j in range(-1, 4)}
    height = {j: first_trial[11 + j] - along_height(pressure[j]) for j in range(-1, 4)}
    stream = {j: first_trial[1 + j] - along_stream(pressure, j) for j in range(3)}
    cross = {j: along_span(span[j]) + along_height(height[j]) for j in range(-1, 4)}
    stream[-1] = stream[1] + 2.0 * cross[0]
    stream[3] = stream[1] - 2.0 * cross[2]
    stream[-2] = stream[0] + 2.0 * cross[-1]
    stream[4] = stream[2] - 2.0 * cross[3]
    trial = []
    for c, middle in enumerate((stream, span, height)):
        moved = {}
        for j in range(-1, 4) if c == 0 else range(3):
            start = state[3 * c + j] if 0 <= j < 3 else beside[0 if j < 0 else 1]
            curvature = laplace(middle, j)
            forcing = (
                viscosity[j + 2] * curvature
                - profile * along_stream(middle, j)
                - THRUST * rotor[j + 1] * middle[j]
            )
            moved[j] = 0.5 * start + 0.5 * (middle[j] + TIME_STEP * forcing)
            if 0 <= j < 3:
                laplace_out[3 * c + j] = curvature
                second_trial[3 * c + j] = moved[j]
        trial.append(moved)
    sources = [
        along_stream(trial[0], j) + along_span(trial[1][j]) + along_height(trial[2][j])
        for j in range(3)
    ]
    source_out[...] = sources[1]
    sheets = [trial[0][j] - observed[j] for j in range(3)] + sources
    to_modes(sheets, to_z, to_y, buffer)


def solve_both_kernel(modes_in, green, sine_in, to_x, from_x, out):
    sine = sine_in[...]
    inverse = green[...]
    both = jnp.concatenate(
        [gather_slots(modes_in, 0, 3, 6), gather_slots(modes_in, 3, 3, 6)], axis=1
    )
    both = left_product(to_x, both, 2)
    lead = both[:, :NY]
    second = inverse * both[:, NY:]
    third = inverse * swap_waves(lead - swap_waves(second, sine), sine)
    wide = left_product(from_x, jnp.concatenate([second, third], axis=1), 3)
    scatter_slots(out, wide[:, :NY], 0, 4, 8)
    scatter_slots(out, wide[:, NY:], 4, 4, 8)


def adjoint_kernel(
    modes_in, second_trial, source, laplace_mid, viscosity, rotor, observed, column,
    from_z, from_y, to_z, to_y,
    buffer, fourth_trial, source_out, velocity, share_out,
):
    profile = column[...]
    found = from_modes(modes_in, 8, from_z, from_y)
    second = with_plane_below(found[:4], source[...])
    misfit = []
    for j in range(3):
        stream = second_trial[j] - along_stream(second, j)
        velocity[0, 0, j] = stream
        velocity[0, 1, j] = second_trial[3 + j] - along_span(second[j])
        velocity[0, 2, j] = second_trial[6 + j] - along_height(second[j])
        misfit.append(stream - observed[j])
    third = with_plane_below(found[4:], 0.5 * (misfit[2] - misfit[0]))
    span = {j: -along_span(third[j]) for j in range(-1, 4)}
    height = {j: -along_height(third[j]) for j in range(-1, 4)}
    cross = {j: along_span(span[j]) + along_height(height[j]) for j in range(-1, 4)}
    stream = {j: misfit[j] - along_stream(third, j) for j in range(3)}
    stream[-1] = stream[1] + 2.0 * cross[0]
    stream[3] = stream[1] - 2.0 * cross[2]
    stream[-2] = stream[0] + 2.0 * cross[-1]
    stream[4] = stream[2] - 2.0 * cross[3]
    share = [None] * 3
    trial = []
    for c, adjoint in enumerate((stream, span, height)):
        spread = {j: viscosity[j + 2] * adjoint[j] for j in adjoint}
        moved = {}
        for j in range(-1, 4) if c == 0 else range(3):
            pulled = (
                profile * along_stream(adjoint, j)
                + laplace(spread, j)
                - THRUST * rotor[j + 1] * adjoint[j]
            )
            moved[j] = 0.5 * adjoint[j] + 0.5 * TIME_STEP * pulled
        for j in range(3):
            fourth_trial[3 * c + j] = moved[j]
            term = adjoint[j] * laplace_mid[3 * c + j]
            share[j] = term if c == 0 else share[j] + term
        trial.append(moved)
    for j in range(3):
        share_out[j] = 0.5 * share[j]
    sources = [
        along_stream(trial[0], j) + along_span(trial[1][j]) + along_height(trial[2][j])
        for j in range(3)
    ]
    source_out[...] = sources[1]
    to_modes(sources, to_z, to_y, buffer)


def gradient_kernel(
    modes_in, fourth_trial, source, laplace_start, viscosity, share, from_z, from_y, out
):
    pressure = with_plane_below(from_modes(modes_in, 4, from_z, from_y), source[...])
    for j in range(3):
        push = [along_stream(pressure, j), along_span(pressure[j]), along_height(pressure[j])]
        total = share[j]
        for c in range(3):
            total = total + (fourth_trial[3 * c + j] - push[c]) * laplace_start[3 * c + j]
        total = TIME_STEP * viscosity[j + 2] * total
        for copy in range(out.shape[0]):
            out[copy, NZ * j : NZ * (j + 1), :] = total


def local_call(kernel, outs, *args, spaces={}, out_spaces={}, scratch=()):
    specs = [pl.BlockSpec(memory_space=spaces.get(i, pltpu.VMEM)) for i in range(len(args))]
    out_spaces = [out_spaces.get(i, pltpu.VMEM) for i in range(len(outs))]
    shapes = [space(shape, F32) for space, shape in zip(out_spaces, outs)]
    out_specs = [pl.BlockSpec(memory_space=space) for space in out_spaces]
    single = len(outs) == 1
    return pl.pallas_call(
        kernel,
        out_shape=shapes[0] if single else shapes,
        in_specs=specs,
        out_specs=out_specs[0] if single else out_specs,
        scratch_shapes=scratch,
        name=kernel.__name__,
        compiler_params=pltpu.CompilerParams(vmem_limit_bytes=24 * 1024 * 1024),
    )(*args)


def exchange(rows, axis="space"):
    count = lax.axis_size(axis)
    wide = rows.reshape(count, 1, rows.size // count)
    return lax.all_to_all(wide, axis, 0, 0, tiled=True).reshape(rows.shape)


def shards(inflow_seeds, rotor_cells, fluctuation, profile, correction, observed):
    samples = lax.axis_size("sample")
    within = [(i, i + 1 - 2 * (i % 2)) for i in range(SPACE)]
    between = [(i, (i - 1 + 2 * (i % 2)) % SPACE) for i in range(SPACE)]
    plane = (NZ, NY)
    inner, outer = local_call(
        pack_kernel, [(4, 2, *plane), (4, 2, *plane)],
        pltpu.with_memory_space_constraint(fluctuation, pltpu.HBM),
        pltpu.with_memory_space_constraint(correction, pltpu.HBM),
        spaces={0: pltpu.HBM, 1: pltpu.HBM}, scratch=[pltpu.SemaphoreType.DMA((4,))],
    )
    inner = lax.ppermute(inner, "space", within)
    outer = lax.ppermute(outer, "space", between)
    to_x, from_x = jnp.asarray(TO_X), jnp.asarray(FROM_X)
    to_y, from_y = jnp.asarray(TO_Y), jnp.asarray(FROM_Y)
    to_z, from_z = jnp.asarray(TO_Z), jnp.asarray(FROM_Z)

    state, viscosity, rotor, column = local_call(
        prepare_kernel, [(9, *plane), (3, *plane), (5, *plane), plane],
        inflow_seeds, fluctuation, correction, rotor_cells.T, profile[None, :],
    )
    buffer, first_trial, source, beside, laplace_start, viscosity = local_call(
        start_kernel,
        [(SPACE * 3, NY), (15, *plane), plane, (2, *plane), (9, *plane), (7, *plane)],
        inflow_seeds, inner, outer, state, viscosity, rotor, column, to_z, to_y,
    )
    buffer = exchange(buffer)
    buffer, green = local_call(
        solve_first_kernel, [(SPACE * 4, NY), (NX, NY)],
        buffer, jnp.asarray(SQUARES), to_x, from_x,
    )
    buffer = exchange(buffer)
    buffer, second_trial, source, laplace_mid = local_call(
        middle_kernel,
        [(SPACE * 6, NY), (9, *plane), plane, (9, *plane)],
        buffer, first_trial, source, state, beside, viscosity, rotor, observed, column,
        from_z, from_y, to_z, to_y,
    )
    buffer = exchange(buffer)
    buffer = local_call(
        solve_both_kernel, [(SPACE * 8, NY)],
        buffer, green, jnp.asarray(SINE_X), jnp.asarray(TO_X_WIDE), jnp.asarray(FROM_X_WIDE),
    )
    buffer = exchange(buffer)
    buffer, fourth_trial, source, velocity, share = local_call(
        adjoint_kernel,
        [(SPACE * 3, NY), (9, *plane), plane, (1, 3, 3, *plane), (3, *plane)],
        buffer, second_trial, source, laplace_mid, viscosity, rotor, observed, column,
        from_z, from_y, to_z, to_y,
    )
    buffer = exchange(buffer)
    buffer, velocity = local_call(
        solve_last_kernel, [(SPACE * 4, NY), velocity.shape],
        buffer, green, to_x, from_x, velocity,
        out_spaces={1: pltpu.HBM}, scratch=[pltpu.SemaphoreType.DMA],
    )
    buffer = exchange(buffer)
    terms = local_call(
        gradient_kernel, [(samples, SLAB * NZ, NY)],
        buffer, fourth_trial, source, laplace_start, viscosity, share, from_z, from_y,
    )
    terms = lax.all_to_all(terms, "sample", 0, 0, tiled=True)
    gradient = jnp.sum(terms, axis=0).reshape(SLAB, *plane)
    return (velocity, gradient)


def solution(mesh):
    return jax.shard_map(
        shards,
        mesh=mesh,
        in_specs=(
            P("sample", None),
            P(),
            P(None, "space", None, None),
            P(),
            P("space", None, None),
            P("space", None, None),
        ),
        out_specs=(P("sample", None, "space", None, None), P("space", None, None)),
        check_vma=False,
    )
```

```python
import functools
import math

import jax
import jax.numpy as jnp
import ml_dtypes
import numpy as np
from jax import lax
from jax.experimental import pallas as pl
from jax.experimental.pallas import tpu as pltpu
from jax.sharding import PartitionSpec as P

NX = 192
NY = 128
NZ = 48
ROTOR = 8
SPACE = 64
SLAB = NX // SPACE

TIME_STEP = 0.2
BASE_VISCOSITY = 0.15
THRUST = 1.0
F32 = jnp.float32
BF16 = jnp.bfloat16


def real_basis(length):
    half = length // 2
    cells = np.arange(length)[:, None]
    waves = np.arange(half)[None, :]
    phase = 2.0 * np.pi / length * ((cells * waves) % length)
    even = np.cos(phase) * math.sqrt(2.0 / length)
    even[:, 0] = math.sqrt(1.0 / length)
    odd = np.sin(phase) * math.sqrt(2.0 / length)
    odd[:, 0] = (1.0 - 2.0 * (np.arange(length) % 2)) * math.sqrt(1.0 / length)
    return np.concatenate([even, odd], axis=1)


def sine_of(length):
    half = length // 2
    waves = np.arange(length) % half
    return np.sin(2.0 * np.pi / length * waves)


def in_parts(matrix, count):
    parts = []
    rest = np.asarray(matrix, np.float64)
    for _ in range(count):
        parts.append(rest.astype(ml_dtypes.bfloat16))
        rest = rest - parts[-1].astype(np.float64)
    return np.stack(parts)


BASIS_X = real_basis(NX)
BASIS_Y = real_basis(NY)
BASIS_Z = real_basis(NZ)


def stream_rows(first, count):
    device = np.arange(SPACE)[None, :]
    slot = np.arange(first, first + count)[:, None]
    return ((SLAB * device + slot) % NX).reshape(-1)


def pairs_of(count):
    return [(i, order - i) for order in reversed(range(count)) for i in range(order + 1)]


def left_table(matrix, count):
    parts = in_parts(matrix, count)
    return np.concatenate([parts[i] for i, _ in pairs_of(count)], axis=1)


def left_narrow_table(matrix, count):
    parts = list(in_parts(matrix, count))
    return np.concatenate(parts if count == 2 else parts + parts[:1], axis=1)


def right_table(matrix, count):
    parts = list(in_parts(matrix, count))
    none = np.zeros_like(parts[0])
    if count == 2:
        rows = [(parts[0], parts[1]), (parts[0], none)]
    else:
        rows = [(parts[0], parts[1]), (parts[0], parts[1]), (parts[0], none), (parts[2], none)]
    return np.concatenate([np.concatenate(row, axis=1) for row in rows], axis=0)


TO_Y = right_table(BASIS_Y, 2)
TO_Z = left_table(BASIS_Z.T, 2)
TO_X = left_narrow_table(BASIS_X[stream_rows(0, 3)].T, 2)
TO_X_WIDE = left_table(BASIS_X[stream_rows(0, 3)].T, 2)
FROM_Y = right_table(BASIS_Y.T, 3)
FROM_Z = left_table(BASIS_Z, 3)
FROM_X = left_narrow_table(BASIS_X[stream_rows(0, 4)], 3)
FROM_X_WIDE = left_table(BASIS_X[stream_rows(0, 4)], 3)
BLOCK = 32
BLOCKS = NY // BLOCK
UNITS = NZ * BLOCKS // SPACE


def symbol_table():
    table = np.ones((NX + SPACE, NY))
    table[:NX] = sine_of(NX)[:, None]
    squares = (sine_of(NZ) ** 2)[:, None] + (sine_of(NY) ** 2)[None, :]
    table[NX:, : UNITS * BLOCK] = squares.reshape(SPACE, UNITS * BLOCK)
    return table.astype(np.float32)


SYMBOLS = symbol_table()


def split(value, count):
    parts = []
    for _ in range(count - 1):
        parts.append(value.astype(BF16))
        value = value - parts[-1].astype(F32)
    return parts + [value.astype(BF16)]


def dot(a, b):
    return jnp.dot(a, b, preferred_element_type=F32)


def left_product(table, value, count):
    parts = split(value, count)
    return dot(table[...], jnp.concatenate([parts[k] for _, k in pairs_of(count)], axis=0))


def left_narrow_product(table, value, count):
    parts = split(value, count)
    none = jnp.zeros_like(parts[0])
    if count == 2:
        rows = [(parts[0], parts[1]), (parts[0], none)]
    else:
        rows = [(parts[0], parts[1]), (parts[0], parts[1]), (parts[0], none), (none, parts[2])]
    wide = jnp.concatenate([jnp.concatenate(row, axis=1) for row in rows], axis=0)
    found = dot(table[...], wide)
    return found[:, :NY] + found[:, NY:]


def right_product(value, table, count):
    parts = split(value, count)
    wide = jnp.concatenate(parts if count == 2 else parts + parts[:1], axis=1)
    found = dot(wide, table[...])
    return found[:, :NY] + found[:, NY:]


def up_z(f):
    return pltpu.roll(f, NZ - 1, 0)


def down_z(f):
    return pltpu.roll(f, 1, 0)


def up_y(f):
    return pltpu.roll(f, NY - 1, 1)


def down_y(f):
    return pltpu.roll(f, 1, 1)


def along_height(f):
    return 0.5 * (up_z(f) - down_z(f))


def along_span(f):
    return 0.5 * (up_y(f) - down_y(f))


def along_stream(planes, j):
    return 0.5 * (planes[j + 1] - planes[j - 1])


def laplace(planes, j):
    f = planes[j]
    summed = planes[j + 1] + planes[j - 1] + up_z(f) + down_z(f) + up_y(f) + down_y(f)
    return summed - 6.0 * f


def cross_laplace(f):
    return along_span(along_span(f)) + along_height(along_height(f))


def with_plane_below(planes, source):
    below = 2.0 * planes[1] - planes[3] + 4.0 * (source - cross_laplace(planes[1]))
    return {-1: below, 0: planes[0], 1: planes[1], 2: planes[2], 3: planes[3]}


def block_of(array):
    return lax.broadcasted_iota(jnp.int32, array.shape, 1) // BLOCK


def move(array, blocks):
    return pltpu.roll(array, BLOCK * blocks, 1)


THIRD = NZ // UNITS


def by_device(sheet_ref, first):
    a, b, c = [sheet_ref[pl.ds(first + i, THIRD, stride=UNITS), :] for i in range(UNITS)]
    block = block_of(a)
    return [a, move(jnp.where(block == 3, a, b), 1), move(jnp.where(block >= 2, b, c), 2), move(c, 3)]


def by_height(parts):
    block = block_of(parts[0])
    b, c, d = move(parts[1], 3), move(parts[2], 2), move(parts[3], 1)
    return [
        jnp.where(block == 3, b, parts[0]),
        jnp.where(block < 2, b, c),
        jnp.where(block == 0, c, d),
    ]


def to_modes(planes, to_z, to_y, out_ref, sheet_ref):
    count = len(planes)
    side = left_product(to_z, jnp.concatenate(planes, axis=1), 2)
    rows = jnp.concatenate([side[:, NY * i : NY * (i + 1)] for i in range(count)], axis=0)
    sheet_ref[: NZ * count, :] = right_product(rows, to_y, 2)
    sheets = [by_device(sheet_ref, NZ * i) for i in range(count)]
    fourth = sheets.pop(3) if count > 3 else None
    width = len(sheets)
    for row, parts in enumerate(sheets):
        for i in range(BLOCKS):
            part = parts[i]
            if row < UNITS and fourth is not None:
                part = jnp.where(block_of(part) == 3, move(fourth[i], 3 - row), part)
            out_ref[pl.ds(i * width + row, THIRD, stride=BLOCKS * width), :] = part


def from_modes(in_ref, groups, from_z, from_y, sheet_ref):
    count = 4 * groups
    for g in range(groups):
        for p in range(UNITS):
            first = p * groups + g
            parts = [
                in_ref[pl.ds(i * UNITS * groups + first, THIRD, stride=BLOCKS * UNITS * groups), :]
                for i in range(BLOCKS)
            ]
            for i, part in enumerate(by_height(parts)):
                sheet_ref[pl.ds(NZ * (4 * g + p) + i, THIRD, stride=UNITS), :] = part
        units = [in_ref[pl.ds(j * groups + g, NZ, stride=BLOCKS * groups), :] for j in range(BLOCKS)]
        block = block_of(units[3])
        fourth = units[3]
        for j in range(UNITS):
            fourth = jnp.where(block == j, move(units[j], j + 1), fourth)
        sheet_ref[NZ * (4 * g + 3) : NZ * (4 * g + 4), :] = fourth
    rows = right_product(sheet_ref[: NZ * count, :], from_y, 3)
    side = jnp.concatenate([rows[NZ * i : NZ * (i + 1)] for i in range(count)], axis=1)
    side = left_product(from_z, side, 3)
    return [side[:, NY * i : NY * (i + 1)] for i in range(count)]


def gather_planes(in_ref, width):
    rows = [in_ref[pl.ds(i, SPACE, stride=width), :] for i in range(width)]
    if width == UNITS:
        return rows
    block = block_of(rows[0])
    fourth = jnp.where(block == 0, move(rows[0], 1), move(rows[2], 3))
    fourth = jnp.where(block == 1, move(rows[1], 2), fourth)
    return rows[:UNITS] + [fourth] + rows[UNITS:]


def scatter_planes(out_ref, wide, groups):
    for g in range(groups):
        sheet = wide[:, NY * g : NY * (g + 1)]
        planes = [sheet[SPACE * p : SPACE * (p + 1)] for p in range(4)]
        for u in range(UNITS):
            row = jnp.where(block_of(planes[u]) == 3, move(planes[3], 3 - u), planes[u])
            out_ref[pl.ds(u * groups + g, SPACE, stride=UNITS * groups), :] = row


def swap_waves(modes, sine):
    half = NX // 2
    return jnp.concatenate([sine[:half] * modes[half:], -sine[half:] * modes[:half]], axis=0)


def count_rotors(cells):
    stream = cells[0:1, :]
    span = cells[1:2, :]
    base = cells[2:3, :]
    turbines = cells.shape[1]
    spans = lax.broadcasted_iota(jnp.int32, (NY, turbines), 0)
    in_span = ((spans >= span) & (spans < span + ROTOR)).astype(F32).astype(BF16)
    heights = lax.broadcasted_iota(jnp.int32, (NZ, turbines), 0)
    in_height = (heights >= base) & (heights < base + ROTOR)
    first = lax.axis_index("space") * SLAB
    sheets = []
    for j in range(-1, 4):
        here = stream == lax.rem(first + (j + NX), NX)
        sheets.append((in_height & here).astype(F32).astype(BF16))
    counted = lax.dot_general(
        jnp.concatenate(sheets, axis=0), in_span, (((1,), (1,)), ((), ())),
        preferred_element_type=F32,
    )
    return [counted[NZ * i : NZ * (i + 1)] for i in range(5)]


def spread_profile(row):
    cells = lax.broadcasted_iota(jnp.int32, (NZ, NZ), 0)
    others = lax.broadcasted_iota(jnp.int32, (NZ, NZ), 1)
    column = jnp.sum(jnp.where(cells == others, row, 0.0), axis=1, keepdims=True)
    return jnp.broadcast_to(column, (NZ, NY))


def pack_kernel(own, correction, inner, outer, arrived):
    even = lax.rem(lax.axis_index("space"), 2) == 0

    def fill(first, last):
        copies = []
        for i, (target, start) in enumerate(((last, 1), (first, 0))):
            planes = pl.ds(start, 2)
            copies.append(
                pltpu.make_async_copy(own.at[:, planes], target.at[0:3], arrived.at[2 * i])
            )
            copies.append(
                pltpu.make_async_copy(
                    correction.at[planes], target.at[3], arrived.at[2 * i + 1]
                )
            )
        for copy in copies:
            copy.start()
        for copy in copies:
            copy.wait()

    @pl.when(even)
    def _():
        fill(outer, inner)

    @pl.when(jnp.logical_not(even))
    def _():
        fill(inner, outer)


def rolled(plane, shifts):
    return pltpu.roll(pltpu.roll(plane, shifts[0], 1), shifts[1], 0)


def shifts_of(seeds):
    row = seeds[...]
    return row[0, 0], row[0, 1]


def prepare_kernel(
    seeds, own, correction, cells, heights, state_out, viscosity_out, rotor_out, column_out
):
    shifts = shifts_of(seeds)
    profile = spread_profile(heights[...])
    column_out[...] = profile
    rotor = count_rotors(cells)
    for j in range(5):
        rotor_out[j] = rotor[j]
    for j in range(3):
        viscosity_out[j] = BASE_VISCOSITY * jnp.exp(correction[j])
        for c in range(3):
            plane = rolled(own[c, j], shifts)
            state_out[3 * c + j] = plane + profile if c == 0 else plane


def start_kernel(
    seeds, inner, outer, own_state, own_viscosity, rotor, column, to_z, to_y,
    buffer, first_trial, source_out, beside_out, laplace_out, viscosity_out, sheet,
):
    even = lax.rem(lax.axis_index("space"), 2) == 0
    shifts = shifts_of(seeds)
    profile = column[...]

    def halo(j, c):
        i = j + 2 if j < 0 else j - 3
        low = outer if j < 0 else inner
        high = inner if j < 0 else outer
        return jnp.where(even, low[c, i], high[c, i])

    viscosity = {}
    for j in range(-2, 5):
        if 0 <= j < 3:
            viscosity[j] = own_viscosity[j]
        else:
            viscosity[j] = BASE_VISCOSITY * jnp.exp(halo(j, 3))
        viscosity_out[j + 2] = viscosity[j]
    trial = []
    for c in range(3):
        state = {}
        for j in range(-2, 5):
            if 0 <= j < 3:
                state[j] = own_state[3 * c + j]
            else:
                state[j] = rolled(halo(j, c), shifts)
                if c == 0:
                    state[j] = state[j] + profile
        moved = {}
        for j in range(-1, 4):
            curvature = laplace(state, j)
            forcing = (
                viscosity[j] * curvature
                - profile * along_stream(state, j)
                - THRUST * rotor[j + 1] * state[j]
            )
            moved[j] = state[j] + TIME_STEP * forcing
            first_trial[5 * c + j + 1] = moved[j]
            if 0 <= j < 3:
                laplace_out[3 * c + j] = curvature
        trial.append(moved)
        if c == 0:
            beside_out[0] = state[-1]
            beside_out[1] = state[3]
    sources = [
        along_stream(trial[0], j) + along_span(trial[1][j]) + along_height(trial[2][j])
        for j in range(3)
    ]
    source_out[...] = sources[1]
    to_modes(sources, to_z, to_y, buffer, sheet)


def green_table(symbols):
    sine = symbols[:NX, :]
    summed = sine * sine + symbols[pl.ds(NX + lax.axis_index("space"), 1), :]
    null_mode = summed == 0.0
    return jnp.where(null_mode, 0.0, -1.0 / jnp.where(null_mode, 1.0, summed))


def solve_rows(modes_in, green, to_x, from_x, out):
    planes = jnp.concatenate(gather_planes(modes_in, 3), axis=0)
    spectrum = left_narrow_product(to_x, planes, 2) * green
    scatter_planes(out, left_narrow_product(from_x, spectrum, 3), 1)


def solve_first_kernel(modes_in, symbols, to_x, from_x, out, green_out):
    green = green_table(symbols)
    green_out[...] = green
    solve_rows(modes_in, green, to_x, from_x, out)


def solve_last_kernel(modes_in, green, to_x, from_x, velocity, out, velocity_out, sent):
    copy = pltpu.make_async_copy(velocity, velocity_out, sent)
    copy.start()
    solve_rows(modes_in, green[...], to_x, from_x, out)
    copy.wait()


def middle_kernel(
    modes_in, first_trial, source, state, beside, viscosity, rotor, observed, column,
    from_z, from_y, to_z, to_y,
    buffer, second_trial, source_out, laplace_out, sheet,
):
    profile = column[...]
    pressure = with_plane_below(from_modes(modes_in, 1, from_z, from_y, sheet), source[...])
    span = {j: first_trial[6 + j] - along_span(pressure[j]) for j in range(-1, 4)}
    height = {j: first_trial[11 + j] - along_height(pressure[j]) for j in range(-1, 4)}
    stream = {j: first_trial[1 + j] - along_stream(pressure, j) for j in range(3)}
    cross = {j: along_span(span[j]) + along_height(height[j]) for j in range(-1, 4)}
    stream[-1] = stream[1] + 2.0 * cross[0]
    stream[3] = stream[1] - 2.0 * cross[2]
    stream[-2] = stream[0] + 2.0 * cross[-1]
    stream[4] = stream[2] - 2.0 * cross[3]
    trial = []
    for c, middle in enumerate((stream, span, height)):
        moved = {}
        for j in range(-1, 4) if c == 0 else range(3):
            start = state[3 * c + j] if 0 <= j < 3 else beside[0 if j < 0 else 1]
            curvature = laplace(middle, j)
            forcing = (
                viscosity[j + 2] * curvature
                - profile * along_stream(middle, j)
                - THRUST * rotor[j + 1] * middle[j]
            )
            moved[j] = 0.5 * start + 0.5 * (middle[j] + TIME_STEP * forcing)
            if 0 <= j < 3:
                laplace_out[3 * c + j] = curvature
                second_trial[3 * c + j] = moved[j]
        trial.append(moved)
    sources = [
        along_stream(trial[0], j) + along_span(trial[1][j]) + along_height(trial[2][j])
        for j in range(3)
    ]
    source_out[...] = sources[1]
    sheets = [trial[0][j] - observed[j] for j in range(3)] + sources
    to_modes(sheets, to_z, to_y, buffer, sheet)


def solve_both_kernel(modes_in, green, symbols, to_x, from_x, out):
    sine = symbols[:NX, :]
    inverse = green[...]
    planes = gather_planes(modes_in, 5)
    both = jnp.concatenate(
        [jnp.concatenate(planes[:3], axis=0), jnp.concatenate(planes[3:], axis=0)], axis=1
    )
    both = left_product(to_x, both, 2)
    lead = both[:, :NY]
    second = inverse * both[:, NY:]
    third = inverse * swap_waves(lead - swap_waves(second, sine), sine)
    wide = left_product(from_x, jnp.concatenate([second, third], axis=1), 3)
    scatter_planes(out, wide, 2)


def adjoint_kernel(
    modes_in, second_trial, source, laplace_mid, viscosity, rotor, observed, column,
    from_z, from_y, to_z, to_y,
    buffer, fourth_trial, source_out, velocity, share_out, sheet,
):
    profile = column[...]
    found = from_modes(modes_in, 2, from_z, from_y, sheet)
    second = with_plane_below(found[:4], source[...])
    misfit = []
    for j in range(3):
        stream = second_trial[j] - along_stream(second, j)
        velocity[0, 0, j] = stream
        velocity[0, 1, j] = second_trial[3 + j] - along_span(second[j])
        velocity[0, 2, j] = second_trial[6 + j] - along_height(second[j])
        misfit.append(stream - observed[j])
    third = with_plane_below(found[4:], 0.5 * (misfit[2] - misfit[0]))
    span = {j: -along_span(third[j]) for j in range(-1, 4)}
    height = {j: -along_height(third[j]) for j in range(-1, 4)}
    cross = {j: along_span(span[j]) + along_height(height[j]) for j in range(-1, 4)}
    stream = {j: misfit[j] - along_stream(third, j) for j in range(3)}
    stream[-1] = stream[1] + 2.0 * cross[0]
    stream[3] = stream[1] - 2.0 * cross[2]
    stream[-2] = stream[0] + 2.0 * cross[-1]
    stream[4] = stream[2] - 2.0 * cross[3]
    share = [None] * 3
    trial = []
    for c, adjoint in enumerate((stream, span, height)):
        spread = {j: viscosity[j + 2] * adjoint[j] for j in adjoint}
        moved = {}
        for j in range(-1, 4) if c == 0 else range(3):
            pulled = (
                profile * along_stream(adjoint, j)
                + laplace(spread, j)
                - THRUST * rotor[j + 1] * adjoint[j]
            )
            moved[j] = 0.5 * adjoint[j] + 0.5 * TIME_STEP * pulled
        for j in range(3):
            fourth_trial[3 * c + j] = moved[j]
            term = adjoint[j] * laplace_mid[3 * c + j]
            share[j] = term if c == 0 else share[j] + term
        trial.append(moved)
    for j in range(3):
        share_out[j] = 0.5 * share[j]
    sources = [
        along_stream(trial[0], j) + along_span(trial[1][j]) + along_height(trial[2][j])
        for j in range(3)
    ]
    source_out[...] = sources[1]
    to_modes(sources, to_z, to_y, buffer, sheet)


def gradient_kernel(
    modes_in, fourth_trial, source, laplace_start, viscosity, share, from_z, from_y, out, sheet
):
    pressure = with_plane_below(from_modes(modes_in, 1, from_z, from_y, sheet), source[...])
    for j in range(3):
        push = [along_stream(pressure, j), along_span(pressure[j]), along_height(pressure[j])]
        total = share[j]
        for c in range(3):
            total = total + (fourth_trial[3 * c + j] - push[c]) * laplace_start[3 * c + j]
        total = TIME_STEP * viscosity[j + 2] * total
        for copy in range(out.shape[0]):
            out[copy, NZ * j : NZ * (j + 1), :] = total


def local_call(kernel, outs, *args, spaces={}, out_spaces={}, scratch=()):
    specs = [pl.BlockSpec(memory_space=spaces.get(i, pltpu.VMEM)) for i in range(len(args))]
    out_spaces = [out_spaces.get(i, pltpu.VMEM) for i in range(len(outs))]
    shapes = [space(shape, F32) for space, shape in zip(out_spaces, outs)]
    out_specs = [pl.BlockSpec(memory_space=space) for space in out_spaces]
    single = len(outs) == 1
    return pl.pallas_call(
        kernel,
        out_shape=shapes[0] if single else shapes,
        in_specs=specs,
        out_specs=out_specs[0] if single else out_specs,
        scratch_shapes=scratch,
        name=kernel.__name__,
        compiler_params=pltpu.CompilerParams(vmem_limit_bytes=24 * 1024 * 1024),
    )(*args)


def sheets(count):
    return [pltpu.VMEM((NZ * count, NY), F32)]


def exchange(rows, axis="space"):
    count = lax.axis_size(axis)
    wide = rows.reshape(count, 1, rows.size // count)
    return lax.all_to_all(wide, axis, 0, 0, tiled=True).reshape(rows.shape)


def shards(inflow_seeds, rotor_cells, fluctuation, profile, correction, observed):
    samples = lax.axis_size("sample")
    within = [(i, i + 1 - 2 * (i % 2)) for i in range(SPACE)]
    between = [(i, (i - 1 + 2 * (i % 2)) % SPACE) for i in range(SPACE)]
    plane = (NZ, NY)
    inner, outer = local_call(
        pack_kernel, [(4, 2, *plane), (4, 2, *plane)],
        pltpu.with_memory_space_constraint(fluctuation, pltpu.HBM),
        pltpu.with_memory_space_constraint(correction, pltpu.HBM),
        spaces={0: pltpu.HBM, 1: pltpu.HBM}, scratch=[pltpu.SemaphoreType.DMA((4,))],
    )
    inner = lax.ppermute(inner, "space", within)
    outer = lax.ppermute(outer, "space", between)
    to_x, from_x = jnp.asarray(TO_X), jnp.asarray(FROM_X)
    to_y, from_y = jnp.asarray(TO_Y), jnp.asarray(FROM_Y)
    to_z, from_z = jnp.asarray(TO_Z), jnp.asarray(FROM_Z)

    state, viscosity, rotor, column = local_call(
        prepare_kernel, [(9, *plane), (3, *plane), (5, *plane), plane],
        inflow_seeds, fluctuation, correction, rotor_cells.T, profile[None, :],
    )
    rows = NZ * BLOCKS
    symbols = jnp.asarray(SYMBOLS)
    buffer, first_trial, source, beside, laplace_start, viscosity = local_call(
        start_kernel,
        [(rows, NY), (15, *plane), plane, (2, *plane), (9, *plane), (7, *plane)],
        inflow_seeds, inner, outer, state, viscosity, rotor, column, to_z, to_y,
        scratch=sheets(3),
    )
    buffer = exchange(buffer)
    buffer, green = local_call(
        solve_first_kernel, [(rows, NY), (NX, NY)],
        buffer, symbols, to_x, from_x,
    )
    buffer = exchange(buffer)
    buffer, second_trial, source, laplace_mid = local_call(
        middle_kernel,
        [(5 * SPACE, NY), (9, *plane), plane, (9, *plane)],
        buffer, first_trial, source, state, beside, viscosity, rotor, observed, column,
        from_z, from_y, to_z, to_y, scratch=sheets(6),
    )
    buffer = exchange(buffer)
    buffer = local_call(
        solve_both_kernel, [(2 * rows, NY)],
        buffer, green, symbols, jnp.asarray(TO_X_WIDE), jnp.asarray(FROM_X_WIDE),
    )
    buffer = exchange(buffer)
    buffer, fourth_trial, source, velocity, share = local_call(
        adjoint_kernel,
        [(rows, NY), (9, *plane), plane, (1, 3, 3, *plane), (3, *plane)],
        buffer, second_trial, source, laplace_mid, viscosity, rotor, observed, column,
        from_z, from_y, to_z, to_y, scratch=sheets(8),
    )
    buffer = exchange(buffer)
    buffer, velocity = local_call(
        solve_last_kernel, [(rows, NY), velocity.shape],
        buffer, green, to_x, from_x, velocity,
        out_spaces={1: pltpu.HBM}, scratch=[pltpu.SemaphoreType.DMA],
    )
    buffer = exchange(buffer)
    terms = local_call(
        gradient_kernel, [(samples, SLAB * NZ, NY)],
        buffer, fourth_trial, source, laplace_start, viscosity, share, from_z, from_y,
        scratch=sheets(4),
    )
    terms = lax.all_to_all(terms, "sample", 0, 0, tiled=True)
    gradient = jnp.sum(terms, axis=0).reshape(SLAB, *plane)
    return (velocity, gradient)


def solution(mesh):
    return jax.shard_map(
        shards,
        mesh=mesh,
        in_specs=(
            P("sample", None),
            P(),
            P(None, "space", None, None),
            P(),
            P("space", None, None),
            P("space", None, None),
        ),
        out_specs=(P("sample", None, "space", None, None), P("space", None, None)),
        check_vma=False,
    )
```

```python
import functools
import math

import jax
import jax.numpy as jnp
import ml_dtypes
import numpy as np
from jax import lax
from jax.experimental import pallas as pl
from jax.experimental.pallas import tpu as pltpu
from jax.sharding import PartitionSpec as P

NX = 192
NY = 128
NZ = 48
ROTOR = 8
SPACE = 64
SLAB = NX // SPACE

TIME_STEP = 0.2
BASE_VISCOSITY = 0.15
THRUST = 1.0
F32 = jnp.float32
BF16 = jnp.bfloat16


def real_basis(length):
    half = length // 2
    cells = np.arange(length)[:, None]
    waves = np.arange(half)[None, :]
    phase = 2.0 * np.pi / length * ((cells * waves) % length)
    even = np.cos(phase) * math.sqrt(2.0 / length)
    even[:, 0] = math.sqrt(1.0 / length)
    odd = np.sin(phase) * math.sqrt(2.0 / length)
    odd[:, 0] = (1.0 - 2.0 * (np.arange(length) % 2)) * math.sqrt(1.0 / length)
    return np.concatenate([even, odd], axis=1)


def sine_of(length):
    half = length // 2
    waves = np.arange(length) % half
    return np.sin(2.0 * np.pi / length * waves)


def in_parts(matrix, count):
    parts = []
    rest = np.asarray(matrix, np.float64)
    for _ in range(count):
        parts.append(rest.astype(ml_dtypes.bfloat16))
        rest = rest - parts[-1].astype(np.float64)
    return np.stack(parts)


BASIS_X = real_basis(NX)
BASIS_Y = real_basis(NY)
BASIS_Z = real_basis(NZ)


def stream_rows(first, count):
    device = np.arange(SPACE)[None, :]
    slot = np.arange(first, first + count)[:, None]
    return ((SLAB * device + slot) % NX).reshape(-1)


def pairs_of(count):
    return [(i, order - i) for order in reversed(range(count)) for i in range(order + 1)]


def left_table(matrix, count):
    parts = in_parts(matrix, count)
    return np.concatenate([parts[i] for i, _ in pairs_of(count)], axis=1)


def left_narrow_table(matrix, count):
    parts = list(in_parts(matrix, count))
    return np.concatenate(parts if count == 2 else parts + parts[:1], axis=1)


def right_table(matrix, count):
    parts = list(in_parts(matrix, count))
    none = np.zeros_like(parts[0])
    if count == 2:
        rows = [(parts[0], parts[1]), (parts[0], none)]
    else:
        rows = [(parts[0], parts[1]), (parts[0], parts[1]), (parts[0], none), (parts[2], none)]
    return np.concatenate([np.concatenate(row, axis=1) for row in rows], axis=0)


TO_Y = right_table(BASIS_Y, 2)
TO_Z = left_table(BASIS_Z.T, 2)
TO_X = left_narrow_table(BASIS_X[stream_rows(0, 3)].T, 2)
TO_X_WIDE = left_table(BASIS_X[stream_rows(0, 3)].T, 2)
FROM_Y = right_table(BASIS_Y.T, 3)
FROM_Z = left_table(BASIS_Z, 3)
FROM_X = left_narrow_table(BASIS_X[stream_rows(0, 3)], 3)
FROM_X_WIDE = left_table(BASIS_X[stream_rows(0, 3)], 3)
BLOCK = 32
BLOCKS = NY // BLOCK
UNITS = NZ * BLOCKS // SPACE


def symbol_table():
    table = np.ones((NX + SPACE, NY))
    table[:NX] = sine_of(NX)[:, None]
    squares = (sine_of(NZ) ** 2)[:, None] + (sine_of(NY) ** 2)[None, :]
    table[NX:, : UNITS * BLOCK] = squares.reshape(SPACE, UNITS * BLOCK)
    return table.astype(np.float32)


SYMBOLS = symbol_table()


def split(value, count):
    parts = []
    for _ in range(count - 1):
        parts.append(value.astype(BF16))
        value = value - parts[-1].astype(F32)
    return parts + [value.astype(BF16)]


def dot(a, b):
    return jnp.dot(a, b, preferred_element_type=F32)


def left_product(table, value, count):
    parts = split(value, count)
    return dot(table[...], jnp.concatenate([parts[k] for _, k in pairs_of(count)], axis=0))


def left_narrow_product(table, value, count):
    parts = split(value, count)
    none = jnp.zeros_like(parts[0])
    if count == 2:
        rows = [(parts[0], parts[1]), (parts[0], none)]
    else:
        rows = [(parts[0], parts[1]), (parts[0], parts[1]), (parts[0], none), (none, parts[2])]
    wide = jnp.concatenate([jnp.concatenate(row, axis=1) for row in rows], axis=0)
    found = dot(table[...], wide)
    return found[:, :NY] + found[:, NY:]


def right_product(value, table, count):
    parts = split(value, count)
    wide = jnp.concatenate(parts if count == 2 else parts + parts[:1], axis=1)
    found = dot(wide, table[...])
    return found[:, :NY] + found[:, NY:]


def up_z(f):
    return pltpu.roll(f, NZ - 1, 0)


def down_z(f):
    return pltpu.roll(f, 1, 0)


def up_y(f):
    return pltpu.roll(f, NY - 1, 1)


def down_y(f):
    return pltpu.roll(f, 1, 1)


def along_height(f):
    return 0.5 * (up_z(f) - down_z(f))


def along_span(f):
    return 0.5 * (up_y(f) - down_y(f))


def along_stream(planes, j):
    return 0.5 * (planes[j + 1] - planes[j - 1])


def laplace(planes, j):
    f = planes[j]
    summed = planes[j + 1] + planes[j - 1] + up_z(f) + down_z(f) + up_y(f) + down_y(f)
    return summed - 6.0 * f


def cross_laplace(f):
    return along_span(along_span(f)) + along_height(along_height(f))


def with_plane_below(planes, source):
    below = 2.0 * planes[1] - planes[3] + 4.0 * (source - cross_laplace(planes[1]))
    return {-1: below, 0: planes[0], 1: planes[1], 2: planes[2], 3: planes[3]}


def block_of(array):
    return lax.broadcasted_iota(jnp.int32, array.shape, 1) // BLOCK


def move(array, blocks):
    return pltpu.roll(array, BLOCK * blocks, 1)


THIRD = NZ // UNITS


def by_device(sheet_ref, first):
    a, b, c = [sheet_ref[pl.ds(first + i, THIRD, stride=UNITS), :] for i in range(UNITS)]
    block = block_of(a)
    return [a, move(jnp.where(block == 3, a, b), 1), move(jnp.where(block >= 2, b, c), 2), move(c, 3)]


def by_height(parts):
    block = block_of(parts[0])
    b, c, d = move(parts[1], 3), move(parts[2], 2), move(parts[3], 1)
    return [
        jnp.where(block == 3, b, parts[0]),
        jnp.where(block < 2, b, c),
        jnp.where(block == 0, c, d),
    ]


def to_modes(planes, to_z, to_y, out_ref, sheet_ref):
    count = len(planes)
    side = left_product(to_z, jnp.concatenate(planes, axis=1), 2)
    rows = jnp.concatenate([side[:, NY * i : NY * (i + 1)] for i in range(count)], axis=0)
    sheet_ref[: NZ * count, :] = right_product(rows, to_y, 2)
    sheets = [by_device(sheet_ref, NZ * i) for i in range(count)]
    fourth = sheets.pop(3) if count > 3 else None
    width = len(sheets)
    for row, parts in enumerate(sheets):
        for i in range(BLOCKS):
            part = parts[i]
            if row < UNITS and fourth is not None:
                part = jnp.where(block_of(part) == 3, move(fourth[i], 3 - row), part)
            out_ref[pl.ds(i * width + row, THIRD, stride=BLOCKS * width), :] = part


def from_modes(in_ref, groups, from_z, from_y, sheet_ref):
    count = 4 * groups
    for g in range(groups):
        for p in range(UNITS):
            first = p * groups + g
            parts = [
                in_ref[pl.ds(i * UNITS * groups + first, THIRD, stride=BLOCKS * UNITS * groups), :]
                for i in range(BLOCKS)
            ]
            for i, part in enumerate(by_height(parts)):
                sheet_ref[pl.ds(NZ * (4 * g + p) + i, THIRD, stride=UNITS), :] = part
        units = [in_ref[pl.ds(j * groups + g, NZ, stride=BLOCKS * groups), :] for j in range(BLOCKS)]
        block = block_of(units[3])
        fourth = units[3]
        for j in range(UNITS):
            fourth = jnp.where(block == j, move(units[j], j + 1), fourth)
        sheet_ref[NZ * (4 * g + 3) : NZ * (4 * g + 4), :] = fourth
    rows = right_product(sheet_ref[: NZ * count, :], from_y, 3)
    side = jnp.concatenate([rows[NZ * i : NZ * (i + 1)] for i in range(count)], axis=1)
    side = left_product(from_z, side, 3)
    return [side[:, NY * i : NY * (i + 1)] for i in range(count)]


def gather_planes(in_ref, width):
    rows = [in_ref[pl.ds(i, SPACE, stride=width), :] for i in range(width)]
    if width == UNITS:
        return rows
    block = block_of(rows[0])
    fourth = jnp.where(block == 0, move(rows[0], 1), move(rows[2], 3))
    fourth = jnp.where(block == 1, move(rows[1], 2), fourth)
    return rows[:UNITS] + [fourth] + rows[UNITS:]


def scatter_planes(out_ref, wide, groups):
    for g in range(groups):
        sheet = wide[:, NY * g : NY * (g + 1)]
        planes = [sheet[SPACE * p : SPACE * (p + 1)] for p in range(SLAB)]
        planes.append(pltpu.roll(planes[0], SPACE - 1, 0))
        for u in range(UNITS):
            row = jnp.where(block_of(planes[u]) == 3, move(planes[3], 3 - u), planes[u])
            out_ref[pl.ds(u * groups + g, SPACE, stride=UNITS * groups), :] = row


def swap_waves(modes, sine):
    half = NX // 2
    return jnp.concatenate([sine[:half] * modes[half:], -sine[half:] * modes[:half]], axis=0)


def count_rotors(cells):
    stream = cells[0:1, :]
    span = cells[1:2, :]
    base = cells[2:3, :]
    turbines = cells.shape[1]
    spans = lax.broadcasted_iota(jnp.int32, (NY, turbines), 0)
    in_span = ((spans >= span) & (spans < span + ROTOR)).astype(F32).astype(BF16)
    heights = lax.broadcasted_iota(jnp.int32, (NZ, turbines), 0)
    in_height = (heights >= base) & (heights < base + ROTOR)
    first = lax.axis_index("space") * SLAB
    sheets = []
    for j in range(-1, 4):
        here = stream == lax.rem(first + (j + NX), NX)
        sheets.append((in_height & here).astype(F32).astype(BF16))
    counted = lax.dot_general(
        jnp.concatenate(sheets, axis=0), in_span, (((1,), (1,)), ((), ())),
        preferred_element_type=F32,
    )
    return [counted[NZ * i : NZ * (i + 1)] for i in range(5)]


def spread_profile(row):
    cells = lax.broadcasted_iota(jnp.int32, (NZ, NZ), 0)
    others = lax.broadcasted_iota(jnp.int32, (NZ, NZ), 1)
    column = jnp.sum(jnp.where(cells == others, row, 0.0), axis=1, keepdims=True)
    return jnp.broadcast_to(column, (NZ, NY))


def pack_kernel(own, correction, inner, outer, arrived):
    even = lax.rem(lax.axis_index("space"), 2) == 0

    def fill(first, last):
        copies = []
        for i, (target, start) in enumerate(((last, 1), (first, 0))):
            planes = pl.ds(start, 2)
            copies.append(
                pltpu.make_async_copy(own.at[:, planes], target.at[0:3], arrived.at[2 * i])
            )
            copies.append(
                pltpu.make_async_copy(
                    correction.at[planes], target.at[3], arrived.at[2 * i + 1]
                )
            )
        for copy in copies:
            copy.start()
        for copy in copies:
            copy.wait()

    @pl.when(even)
    def _():
        fill(outer, inner)

    @pl.when(jnp.logical_not(even))
    def _():
        fill(inner, outer)


def rolled(plane, shifts):
    return pltpu.roll(pltpu.roll(plane, shifts[0], 1), shifts[1], 0)


def shifts_of(seeds):
    row = seeds[...]
    return row[0, 0], row[0, 1]


def prepare_kernel(
    seeds, own, correction, cells, heights, state_out, viscosity_out, rotor_out, column_out
):
    shifts = shifts_of(seeds)
    profile = spread_profile(heights[...])
    column_out[...] = profile
    rotor = count_rotors(cells)
    for j in range(5):
        rotor_out[j] = rotor[j]
    for j in range(3):
        viscosity_out[j] = BASE_VISCOSITY * jnp.exp(correction[j])
        for c in range(3):
            plane = rolled(own[c, j], shifts)
            state_out[3 * c + j] = plane + profile if c == 0 else plane


def start_kernel(
    seeds, outer, inner, own_state, own_viscosity, rotor, column, to_z, to_y,
    buffer, first_trial, source_out, beside_out, laplace_out, viscosity_out, sheet,
):
    even = lax.rem(lax.axis_index("space"), 2) == 0
    shifts = shifts_of(seeds)
    profile = column[...]

    def halo(j, c):
        i = j + 2 if j < 0 else j - 3
        low = outer if j < 0 else inner
        high = inner if j < 0 else outer
        return jnp.where(even, low[c, i], high[c, i])

    viscosity = {}
    for j in range(-2, 5):
        if 0 <= j < 3:
            viscosity[j] = own_viscosity[j]
        else:
            viscosity[j] = BASE_VISCOSITY * jnp.exp(halo(j, 3))
        viscosity_out[j + 2] = viscosity[j]
    trial = []
    for c in range(3):
        state = {}
        for j in range(-2, 5):
            if 0 <= j < 3:
                state[j] = own_state[3 * c + j]
            else:
                state[j] = rolled(halo(j, c), shifts)
                if c == 0:
                    state[j] = state[j] + profile
        moved = {}
        for j in range(-1, 4):
            curvature = laplace(state, j)
            forcing = (
                viscosity[j] * curvature
                - profile * along_stream(state, j)
                - THRUST * rotor[j + 1] * state[j]
            )
            moved[j] = state[j] + TIME_STEP * forcing
            first_trial[5 * c + j + 1] = moved[j]
            if 0 <= j < 3:
                laplace_out[3 * c + j] = curvature
        trial.append(moved)
        if c == 0:
            beside_out[0] = state[-1]
            beside_out[1] = state[3]
    sources = [
        along_stream(trial[0], j) + along_span(trial[1][j]) + along_height(trial[2][j])
        for j in range(3)
    ]
    source_out[...] = sources[1]
    to_modes(sources, to_z, to_y, buffer, sheet)


def green_table(symbols):
    sine = symbols[:NX, :]
    summed = sine * sine + symbols[pl.ds(NX + lax.axis_index("space"), 1), :]
    null_mode = summed == 0.0
    return jnp.where(null_mode, 0.0, -1.0 / jnp.where(null_mode, 1.0, summed))


def solve_rows(modes_in, green, to_x, from_x, out):
    planes = jnp.concatenate(gather_planes(modes_in, 3), axis=0)
    spectrum = left_narrow_product(to_x, planes, 2) * green
    scatter_planes(out, left_narrow_product(from_x, spectrum, 3), 1)


def solve_first_kernel(modes_in, symbols, to_x, from_x, out, green_out):
    green = green_table(symbols)
    green_out[...] = green
    solve_rows(modes_in, green, to_x, from_x, out)


def solve_last_kernel(modes_in, green, to_x, from_x, velocity, out, velocity_out, sent):
    copy = pltpu.make_async_copy(velocity, velocity_out, sent)
    copy.start()
    solve_rows(modes_in, green[...], to_x, from_x, out)
    copy.wait()


def middle_kernel(
    modes_in, first_trial, source, state, beside, viscosity, rotor, observed, column,
    from_z, from_y, to_z, to_y,
    buffer, second_trial, source_out, laplace_out, sheet,
):
    profile = column[...]
    pressure = with_plane_below(from_modes(modes_in, 1, from_z, from_y, sheet), source[...])
    span = {j: first_trial[6 + j] - along_span(pressure[j]) for j in range(-1, 4)}
    height = {j: first_trial[11 + j] - along_height(pressure[j]) for j in range(-1, 4)}
    stream = {j: first_trial[1 + j] - along_stream(pressure, j) for j in range(3)}
    cross = {j: along_span(span[j]) + along_height(height[j]) for j in range(-1, 4)}
    stream[-1] = stream[1] + 2.0 * cross[0]
    stream[3] = stream[1] - 2.0 * cross[2]
    stream[-2] = stream[0] + 2.0 * cross[-1]
    stream[4] = stream[2] - 2.0 * cross[3]
    trial = []
    for c, middle in enumerate((stream, span, height)):
        moved = {}
        for j in range(-1, 4) if c == 0 else range(3):
            start = state[3 * c + j] if 0 <= j < 3 else beside[0 if j < 0 else 1]
            curvature = laplace(middle, j)
            forcing = (
                viscosity[j + 2] * curvature
                - profile * along_stream(middle, j)
                - THRUST * rotor[j + 1] * middle[j]
            )
            moved[j] = 0.5 * start + 0.5 * (middle[j] + TIME_STEP * forcing)
            if 0 <= j < 3:
                laplace_out[3 * c + j] = curvature
                second_trial[3 * c + j] = moved[j]
        trial.append(moved)
    sources = [
        along_stream(trial[0], j) + along_span(trial[1][j]) + along_height(trial[2][j])
        for j in range(3)
    ]
    source_out[...] = sources[1]
    sheets = [trial[0][j] - observed[j] for j in range(3)] + sources
    to_modes(sheets, to_z, to_y, buffer, sheet)


def solve_both_kernel(modes_in, green, symbols, to_x, from_x, out):
    sine = symbols[:NX, :]
    inverse = green[...]
    planes = gather_planes(modes_in, 5)
    both = jnp.concatenate(
        [jnp.concatenate(planes[:3], axis=0), jnp.concatenate(planes[3:], axis=0)], axis=1
    )
    both = left_product(to_x, both, 2)
    lead = both[:, :NY]
    second = inverse * both[:, NY:]
    third = inverse * swap_waves(lead - swap_waves(second, sine), sine)
    wide = left_product(from_x, jnp.concatenate([second, third], axis=1), 3)
    scatter_planes(out, wide, 2)


def adjoint_kernel(
    modes_in, second_trial, source, laplace_mid, viscosity, rotor, observed, column,
    from_z, from_y, to_z, to_y,
    buffer, fourth_trial, source_out, velocity, share_out, sheet,
):
    profile = column[...]
    found = from_modes(modes_in, 2, from_z, from_y, sheet)
    second = with_plane_below(found[:4], source[...])
    misfit = []
    for j in range(3):
        stream = second_trial[j] - along_stream(second, j)
        velocity[0, 0, j] = stream
        velocity[0, 1, j] = second_trial[3 + j] - along_span(second[j])
        velocity[0, 2, j] = second_trial[6 + j] - along_height(second[j])
        misfit.append(stream - observed[j])
    third = with_plane_below(found[4:], 0.5 * (misfit[2] - misfit[0]))
    span = {j: -along_span(third[j]) for j in range(-1, 4)}
    height = {j: -along_height(third[j]) for j in range(-1, 4)}
    cross = {j: along_span(span[j]) + along_height(height[j]) for j in range(-1, 4)}
    stream = {j: misfit[j] - along_stream(third, j) for j in range(3)}
    stream[-1] = stream[1] + 2.0 * cross[0]
    stream[3] = stream[1] - 2.0 * cross[2]
    stream[-2] = stream[0] + 2.0 * cross[-1]
    stream[4] = stream[2] - 2.0 * cross[3]
    share = [None] * 3
    trial = []
    for c, adjoint in enumerate((stream, span, height)):
        spread = {j: viscosity[j + 2] * adjoint[j] for j in adjoint}
        moved = {}
        for j in range(-1, 4) if c == 0 else range(3):
            pulled = (
                profile * along_stream(adjoint, j)
                + laplace(spread, j)
                - THRUST * rotor[j + 1] * adjoint[j]
            )
            moved[j] = 0.5 * adjoint[j] + 0.5 * TIME_STEP * pulled
        for j in range(3):
            fourth_trial[3 * c + j] = moved[j]
            term = adjoint[j] * laplace_mid[3 * c + j]
            share[j] = term if c == 0 else share[j] + term
        trial.append(moved)
    for j in range(3):
        share_out[j] = 0.5 * share[j]
    sources = [
        along_stream(trial[0], j) + along_span(trial[1][j]) + along_height(trial[2][j])
        for j in range(3)
    ]
    source_out[...] = sources[1]
    to_modes(sources, to_z, to_y, buffer, sheet)


def gradient_kernel(
    modes_in, fourth_trial, source, laplace_start, viscosity, share, from_z, from_y, out, sheet
):
    pressure = with_plane_below(from_modes(modes_in, 1, from_z, from_y, sheet), source[...])
    for j in range(3):
        push = [along_stream(pressure, j), along_span(pressure[j]), along_height(pressure[j])]
        total = share[j]
        for c in range(3):
            total = total + (fourth_trial[3 * c + j] - push[c]) * laplace_start[3 * c + j]
        total = TIME_STEP * viscosity[j + 2] * total
        for copy in range(out.shape[0]):
            out[copy, NZ * j : NZ * (j + 1), :] = total


def local_call(kernel, outs, *args, spaces={}, out_spaces={}, scratch=()):
    specs = [pl.BlockSpec(memory_space=spaces.get(i, pltpu.VMEM)) for i in range(len(args))]
    out_spaces = [out_spaces.get(i, pltpu.VMEM) for i in range(len(outs))]
    shapes = [space(shape, F32) for space, shape in zip(out_spaces, outs)]
    out_specs = [pl.BlockSpec(memory_space=space) for space in out_spaces]
    single = len(outs) == 1
    return pl.pallas_call(
        kernel,
        out_shape=shapes[0] if single else shapes,
        in_specs=specs,
        out_specs=out_specs[0] if single else out_specs,
        scratch_shapes=scratch,
        name=kernel.__name__,
        compiler_params=pltpu.CompilerParams(vmem_limit_bytes=24 * 1024 * 1024),
    )(*args)


def sheets(count):
    return [pltpu.VMEM((NZ * count, NY), F32)]


def exchange(rows, axis="space"):
    count = lax.axis_size(axis)
    wide = rows.reshape(count, 1, rows.size // count)
    return lax.all_to_all(wide, axis, 0, 0, tiled=True).reshape(rows.shape)


def shards(inflow_seeds, rotor_cells, fluctuation, profile, correction, observed):
    samples = lax.axis_size("sample")
    within = [(i, i + 1 - 2 * (i % 2)) for i in range(SPACE)]
    between = [(i, (i - 1 + 2 * (i % 2)) % SPACE) for i in range(SPACE)]
    plane = (NZ, NY)
    inner, outer = local_call(
        pack_kernel, [(4, 2, *plane), (4, 2, *plane)],
        pltpu.with_memory_space_constraint(fluctuation, pltpu.HBM),
        pltpu.with_memory_space_constraint(correction, pltpu.HBM),
        spaces={0: pltpu.HBM, 1: pltpu.HBM}, scratch=[pltpu.SemaphoreType.DMA((4,))],
    )
    inner = lax.ppermute(inner, "space", within)
    outer = lax.ppermute(outer, "space", between)
    to_x, from_x = jnp.asarray(TO_X), jnp.asarray(FROM_X)
    to_y, from_y = jnp.asarray(TO_Y), jnp.asarray(FROM_Y)
    to_z, from_z = jnp.asarray(TO_Z), jnp.asarray(FROM_Z)

    state, viscosity, rotor, column = local_call(
        prepare_kernel, [(9, *plane), (3, *plane), (5, *plane), plane],
        inflow_seeds, fluctuation, correction, rotor_cells.T, profile[None, :],
    )
    rows = NZ * BLOCKS
    symbols = jnp.asarray(SYMBOLS)
    buffer, first_trial, source, beside, laplace_start, viscosity = local_call(
        start_kernel,
        [(rows, NY), (15, *plane), plane, (2, *plane), (9, *plane), (7, *plane)],
        inflow_seeds, outer, inner, state, viscosity, rotor, column, to_z, to_y,
        scratch=sheets(3),
    )
    buffer = exchange(buffer)
    buffer, green = local_call(
        solve_first_kernel, [(rows, NY), (NX, NY)],
        buffer, symbols, to_x, from_x,
    )
    buffer = exchange(buffer)
    buffer, second_trial, source, laplace_mid = local_call(
        middle_kernel,
        [(5 * SPACE, NY), (9, *plane), plane, (9, *plane)],
        buffer, first_trial, source, state, beside, viscosity, rotor, observed, column,
        from_z, from_y, to_z, to_y, scratch=sheets(6),
    )
    buffer = exchange(buffer)
    buffer = local_call(
        solve_both_kernel, [(2 * rows, NY)],
        buffer, green, symbols, jnp.asarray(TO_X_WIDE), jnp.asarray(FROM_X_WIDE),
    )
    buffer = exchange(buffer)
    buffer, fourth_trial, source, velocity, share = local_call(
        adjoint_kernel,
        [(rows, NY), (9, *plane), plane, (1, 3, 3, *plane), (3, *plane)],
        buffer, second_trial, source, laplace_mid, viscosity, rotor, observed, column,
        from_z, from_y, to_z, to_y, scratch=sheets(8),
    )
    buffer = exchange(buffer)
    buffer, velocity = local_call(
        solve_last_kernel, [(rows, NY), velocity.shape],
        buffer, green, to_x, from_x, velocity,
        out_spaces={1: pltpu.HBM}, scratch=[pltpu.SemaphoreType.DMA],
    )
    buffer = exchange(buffer)
    terms = local_call(
        gradient_kernel, [(samples, SLAB * NZ, NY)],
        buffer, fourth_trial, source, laplace_start, viscosity, share, from_z, from_y,
        scratch=sheets(4),
    )
    terms = lax.all_to_all(terms, "sample", 0, 0, tiled=True)
    gradient = jnp.sum(terms, axis=0).reshape(SLAB, *plane)
    return (velocity, gradient)


def solution(mesh):
    return jax.shard_map(
        shards,
        mesh=mesh,
        in_specs=(
            P("sample", None),
            P(),
            P(None, "space", None, None),
            P(),
            P("space", None, None),
            P("space", None, None),
        ),
        out_specs=(P("sample", None, "space", None, None), P("space", None, None)),
        check_vma=False,
    )
```

```python
import functools
import math

import jax
import jax.numpy as jnp
import ml_dtypes
import numpy as np
from jax import lax
from jax.experimental import pallas as pl
from jax.experimental.pallas import tpu as pltpu
from jax.sharding import PartitionSpec as P

NX = 192
NY = 128
NZ = 48
ROTOR = 8
SPACE = 64
SLAB = NX // SPACE

TIME_STEP = 0.2
BASE_VISCOSITY = 0.15
THRUST = 1.0
F32 = jnp.float32
BF16 = jnp.bfloat16


def real_basis(length):
    half = length // 2
    cells = np.arange(length)[:, None]
    waves = np.arange(half)[None, :]
    phase = 2.0 * np.pi / length * ((cells * waves) % length)
    even = np.cos(phase) * math.sqrt(2.0 / length)
    even[:, 0] = math.sqrt(1.0 / length)
    odd = np.sin(phase) * math.sqrt(2.0 / length)
    odd[:, 0] = (1.0 - 2.0 * (np.arange(length) % 2)) * math.sqrt(1.0 / length)
    return np.concatenate([even, odd], axis=1)


def sine_of(length):
    half = length // 2
    waves = np.arange(length) % half
    return np.sin(2.0 * np.pi / length * waves)


def in_parts(matrix, count):
    parts = []
    rest = np.asarray(matrix, np.float64)
    for _ in range(count):
        parts.append(rest.astype(ml_dtypes.bfloat16))
        rest = rest - parts[-1].astype(np.float64)
    return np.stack(parts)


BASIS_X = real_basis(NX)
BASIS_Y = real_basis(NY)
BASIS_Z = real_basis(NZ)


def stream_rows(first, count):
    device = np.arange(SPACE)[None, :]
    slot = np.arange(first, first + count)[:, None]
    return ((SLAB * device + slot) % NX).reshape(-1)


def pairs_of(count):
    return [(i, order - i) for order in reversed(range(count)) for i in range(order + 1)]


def left_table(matrix, count):
    parts = in_parts(matrix, count)
    return np.concatenate([parts[i] for i, _ in pairs_of(count)], axis=1)


def left_narrow_table(matrix, count):
    parts = list(in_parts(matrix, count))
    return np.concatenate(parts if count == 2 else parts + parts[:1], axis=1)


def right_table(matrix, count):
    parts = list(in_parts(matrix, count))
    none = np.zeros_like(parts[0])
    if count == 2:
        rows = [(parts[0], parts[1]), (parts[0], none)]
    else:
        rows = [(parts[0], parts[1]), (parts[0], parts[1]), (parts[0], none), (parts[2], none)]
    return np.concatenate([np.concatenate(row, axis=1) for row in rows], axis=0)


TO_Y = right_table(BASIS_Y, 2)
TO_Z = left_table(BASIS_Z.T, 2)
TO_X = left_narrow_table(BASIS_X[stream_rows(0, 3)].T, 2)
TO_X_WIDE = left_table(BASIS_X[stream_rows(0, 3)].T, 2)
FROM_Y = right_table(BASIS_Y.T, 3)
FROM_Z = left_table(BASIS_Z, 3)
FROM_X = left_narrow_table(BASIS_X[stream_rows(0, 3)], 3)
FROM_X_WIDE = left_table(BASIS_X[stream_rows(0, 3)], 3)
BLOCK = 32
BLOCKS = NY // BLOCK
UNITS = NZ * BLOCKS // SPACE


def symbol_table():
    table = np.ones((NX + SPACE, NY))
    table[:NX] = sine_of(NX)[:, None]
    squares = (sine_of(NZ) ** 2)[:, None] + (sine_of(NY) ** 2)[None, :]
    table[NX:, : UNITS * BLOCK] = squares.reshape(SPACE, UNITS * BLOCK)
    return table.astype(np.float32)


SYMBOLS = symbol_table()


def split(value, count):
    parts = []
    for _ in range(count - 1):
        parts.append(value.astype(BF16))
        value = value - parts[-1].astype(F32)
    return parts + [value.astype(BF16)]


def dot(a, b):
    return jnp.dot(a, b, preferred_element_type=F32)


def left_product(table, value, count):
    parts = split(value, count)
    return dot(table[...], jnp.concatenate([parts[k] for _, k in pairs_of(count)], axis=0))


def left_narrow_product(table, value, count):
    parts = split(value, count)
    none = jnp.zeros_like(parts[0])
    if count == 2:
        rows = [(parts[0], parts[1]), (parts[0], none)]
    else:
        rows = [(parts[0], parts[1]), (parts[0], parts[1]), (parts[0], none), (none, parts[2])]
    wide = jnp.concatenate([jnp.concatenate(row, axis=1) for row in rows], axis=0)
    found = dot(table[...], wide)
    return found[:, :NY] + found[:, NY:]


def right_product(value, table, count):
    parts = split(value, count)
    wide = jnp.concatenate(parts if count == 2 else parts + parts[:1], axis=1)
    found = dot(wide, table[...])
    return found[:, :NY] + found[:, NY:]


def up_z(f):
    return pltpu.roll(f, NZ - 1, 0)


def down_z(f):
    return pltpu.roll(f, 1, 0)


def up_y(f):
    return pltpu.roll(f, NY - 1, 1)


def down_y(f):
    return pltpu.roll(f, 1, 1)


def along_height(f):
    return 0.5 * (up_z(f) - down_z(f))


def along_span(f):
    return 0.5 * (up_y(f) - down_y(f))


def along_stream(planes, j):
    return 0.5 * (planes[j + 1] - planes[j - 1])


def flat_laplace(f):
    return up_z(f) + down_z(f) + up_y(f) + down_y(f) - 6.0 * f


def laplace(planes, j):
    return planes[j + 1] + planes[j - 1] + flat_laplace(planes[j])


def cross_laplace(f):
    return along_span(along_span(f)) + along_height(along_height(f))


def with_plane_below(planes, source):
    below = 2.0 * planes[1] - planes[3] + 4.0 * (source - cross_laplace(planes[1]))
    return {-1: below, 0: planes[0], 1: planes[1], 2: planes[2], 3: planes[3]}


def block_of(array):
    return lax.broadcasted_iota(jnp.int32, array.shape, 1) // BLOCK


def move(array, blocks):
    return pltpu.roll(array, BLOCK * blocks, 1)


THIRD = NZ // UNITS


def by_device(sheet_ref, first):
    a, b, c = [sheet_ref[pl.ds(first + i, THIRD, stride=UNITS), :] for i in range(UNITS)]
    block = block_of(a)
    return [a, move(jnp.where(block == 3, a, b), 1), move(jnp.where(block >= 2, b, c), 2), move(c, 3)]


def by_height(parts):
    block = block_of(parts[0])
    b, c, d = move(parts[1], 3), move(parts[2], 2), move(parts[3], 1)
    return [
        jnp.where(block == 3, b, parts[0]),
        jnp.where(block < 2, b, c),
        jnp.where(block == 0, c, d),
    ]


def to_modes(planes, to_z, to_y, out_ref, sheet_ref):
    count = len(planes)
    side = left_product(to_z, jnp.concatenate(planes, axis=1), 2)
    rows = jnp.concatenate([side[:, NY * i : NY * (i + 1)] for i in range(count)], axis=0)
    sheet_ref[: NZ * count, :] = right_product(rows, to_y, 2)
    sheets = [by_device(sheet_ref, NZ * i) for i in range(count)]
    fourth = sheets.pop(3) if count > 3 else None
    width = len(sheets)
    for row, parts in enumerate(sheets):
        for i in range(BLOCKS):
            part = parts[i]
            if row < UNITS and fourth is not None:
                part = jnp.where(block_of(part) == 3, move(fourth[i], 3 - row), part)
            out_ref[pl.ds(i * width + row, THIRD, stride=BLOCKS * width), :] = part


def from_modes(in_ref, groups, from_z, from_y, sheet_ref):
    count = 4 * groups
    for g in range(groups):
        for p in range(UNITS):
            first = p * groups + g
            parts = [
                in_ref[pl.ds(i * UNITS * groups + first, THIRD, stride=BLOCKS * UNITS * groups), :]
                for i in range(BLOCKS)
            ]
            for i, part in enumerate(by_height(parts)):
                sheet_ref[pl.ds(NZ * (4 * g + p) + i, THIRD, stride=UNITS), :] = part
        units = [in_ref[pl.ds(j * groups + g, NZ, stride=BLOCKS * groups), :] for j in range(BLOCKS)]
        block = block_of(units[3])
        fourth = units[3]
        for j in range(UNITS):
            fourth = jnp.where(block == j, move(units[j], j + 1), fourth)
        sheet_ref[NZ * (4 * g + 3) : NZ * (4 * g + 4), :] = fourth
    side = jnp.concatenate([sheet_ref[NZ * i : NZ * (i + 1), :] for i in range(count)], axis=1)
    side = left_product(from_z, side, 3)
    rows = jnp.concatenate([side[:, NY * i : NY * (i + 1)] for i in range(count)], axis=0)
    rows = right_product(rows, from_y, 3)
    return [rows[NZ * i : NZ * (i + 1)] for i in range(count)]


def gather_planes(in_ref, width):
    rows = [in_ref[pl.ds(i, SPACE, stride=width), :] for i in range(width)]
    if width == UNITS:
        return rows
    block = block_of(rows[0])
    fourth = jnp.where(block == 0, move(rows[0], 1), move(rows[2], 3))
    fourth = jnp.where(block == 1, move(rows[1], 2), fourth)
    return rows[:UNITS] + [fourth] + rows[UNITS:]


def scatter_planes(out_ref, wide, groups):
    for g in range(groups):
        sheet = wide[:, NY * g : NY * (g + 1)]
        planes = [sheet[SPACE * p : SPACE * (p + 1)] for p in range(SLAB)]
        planes.append(pltpu.roll(planes[0], SPACE - 1, 0))
        for u in range(UNITS):
            row = jnp.where(block_of(planes[u]) == 3, move(planes[3], 3 - u), planes[u])
            out_ref[pl.ds(u * groups + g, SPACE, stride=UNITS * groups), :] = row


def swap_waves(modes, sine):
    half = NX // 2
    return jnp.concatenate([sine[:half] * modes[half:], -sine[half:] * modes[:half]], axis=0)


def count_rotors(cells):
    stream = cells[0:1, :]
    span = cells[1:2, :]
    base = cells[2:3, :]
    turbines = cells.shape[1]
    spans = lax.broadcasted_iota(jnp.int32, (NY, turbines), 0)
    in_span = ((spans >= span) & (spans < span + ROTOR)).astype(F32).astype(BF16)
    heights = lax.broadcasted_iota(jnp.int32, (NZ, turbines), 0)
    in_height = (heights >= base) & (heights < base + ROTOR)
    first = lax.axis_index("space") * SLAB
    sheets = []
    for j in range(-1, 4):
        here = stream == lax.rem(first + (j + NX), NX)
        sheets.append((in_height & here).astype(F32).astype(BF16))
    counted = lax.dot_general(
        jnp.concatenate(sheets, axis=0), in_span, (((1,), (1,)), ((), ())),
        preferred_element_type=F32,
    )
    return [counted[NZ * i : NZ * (i + 1)] for i in range(5)]


def spread_profile(row):
    cells = lax.broadcasted_iota(jnp.int32, (NZ, NZ), 0)
    others = lax.broadcasted_iota(jnp.int32, (NZ, NZ), 1)
    column = jnp.sum(jnp.where(cells == others, row, 0.0), axis=1, keepdims=True)
    return jnp.broadcast_to(column, (NZ, NY))


def pack_kernel(own, correction, inner, outer, arrived):
    even = lax.rem(lax.axis_index("space"), 2) == 0

    def fill(first, last):
        copies = []
        for i, (target, start) in enumerate(((last, 1), (first, 0))):
            planes = pl.ds(start, 2)
            copies.append(
                pltpu.make_async_copy(own.at[:, planes], target.at[0:3], arrived.at[2 * i])
            )
            copies.append(
                pltpu.make_async_copy(
                    correction.at[planes], target.at[3], arrived.at[2 * i + 1]
                )
            )
        for copy in copies:
            copy.start()
        for copy in copies:
            copy.wait()

    @pl.when(even)
    def _():
        fill(outer, inner)

    @pl.when(jnp.logical_not(even))
    def _():
        fill(inner, outer)


def rolled(plane, shifts):
    return pltpu.roll(pltpu.roll(plane, shifts[0], 1), shifts[1], 0)


def shifts_of(seeds):
    row = seeds[...]
    return row[0, 0], row[0, 1]


def trial_terms(state, flat, viscosity, rotor):
    return state + TIME_STEP * (viscosity * flat - rotor * state)


def stream_terms(viscosity, profile):
    return TIME_STEP * (viscosity - 0.5 * profile), TIME_STEP * (viscosity + 0.5 * profile)


def prepare_kernel(
    seeds, own, correction, cells, heights,
    state_out, flat_out, part_out, stream_out, viscosity_out, rotor_out, column_out,
):
    shifts = shifts_of(seeds)
    profile = spread_profile(heights[...])
    column_out[...] = profile
    rotor = count_rotors(cells)
    for j in range(5):
        rotor[j] = THRUST * rotor[j]
        rotor_out[j] = rotor[j]
    for j in range(3):
        viscosity = BASE_VISCOSITY * jnp.exp(correction[j])
        viscosity_out[j] = viscosity
        stream_out[0, j], stream_out[1, j] = stream_terms(viscosity, profile)
        for c in range(3):
            state = rolled(own[c, j], shifts)
            if c == 0:
                state = state + profile
            flat = flat_laplace(state)
            state_out[3 * c + j] = state
            flat_out[3 * c + j] = flat
            part_out[3 * c + j] = trial_terms(state, flat, viscosity, rotor[j + 1])


def start_kernel(
    seeds, outer, inner, own_state, own_flat, own_part, own_stream, own_viscosity, rotor, column,
    to_z, to_y,
    buffer, first_trial, source_out, beside_out, laplace_out, viscosity_out, sheet,
):
    even = lax.rem(lax.axis_index("space"), 2) == 0
    shifts = shifts_of(seeds)
    profile = column[...]

    def halo(j, c):
        i = j + 2 if j < 0 else j - 3
        low = outer if j < 0 else inner
        high = inner if j < 0 else outer
        return jnp.where(even, low[c, i], high[c, i])

    stream = {j: (own_stream[0, j], own_stream[1, j]) for j in range(3)}
    beside = {}
    for j in (-2, -1, 3, 4):
        viscosity = BASE_VISCOSITY * jnp.exp(halo(j, 3))
        viscosity_out[j + 2] = viscosity
        if j in (-1, 3):
            beside[j] = viscosity
            stream[j] = stream_terms(viscosity, profile)
    for j in range(3):
        viscosity_out[j + 2] = own_viscosity[j]
    trial = []
    for c in range(3):
        state = {j: own_state[3 * c + j] for j in range(3)}
        for j in (-2, -1, 3, 4):
            state[j] = rolled(halo(j, c), shifts)
            if c == 0:
                state[j] = state[j] + profile
        moved = {}
        for j in range(-1, 4):
            if 0 <= j < 3:
                part = own_part[3 * c + j]
                laplace_out[3 * c + j] = own_flat[3 * c + j] + (state[j + 1] + state[j - 1])
            else:
                part = trial_terms(state[j], flat_laplace(state[j]), beside[j], rotor[j + 1])
            moved[j] = part + stream[j][0] * state[j + 1] + stream[j][1] * state[j - 1]
            if c > 0 or 0 <= j < 3:
                first_trial[5 * c + j + 1] = moved[j]
        trial.append(moved)
        if c == 0:
            beside_out[0] = state[-1]
            beside_out[1] = state[3]
    sources = [
        along_stream(trial[0], j) + along_span(trial[1][j]) + along_height(trial[2][j])
        for j in range(3)
    ]
    source_out[...] = sources[1]
    to_modes(sources, to_z, to_y, buffer, sheet)


def green_table(symbols):
    sine = symbols[:NX, :]
    summed = sine * sine + symbols[pl.ds(NX + lax.axis_index("space"), 1), :]
    null_mode = summed == 0.0
    return jnp.where(null_mode, 0.0, -1.0 / jnp.where(null_mode, 1.0, summed))


def solve_rows(modes_in, green, to_x, from_x, out):
    planes = jnp.concatenate(gather_planes(modes_in, 3), axis=0)
    spectrum = left_narrow_product(to_x, planes, 2) * green
    scatter_planes(out, left_narrow_product(from_x, spectrum, 3), 1)


def solve_first_kernel(modes_in, symbols, to_x, from_x, out, green_out):
    green = green_table(symbols)
    green_out[...] = green
    solve_rows(modes_in, green, to_x, from_x, out)


def solve_last_kernel(modes_in, green, to_x, from_x, velocity, out, velocity_out, sent):
    copy = pltpu.make_async_copy(velocity, velocity_out, sent)
    copy.start()
    solve_rows(modes_in, green[...], to_x, from_x, out)
    copy.wait()


def middle_kernel(
    modes_in, first_trial, source, state, beside, viscosity, rotor, observed, column,
    from_z, from_y, to_z, to_y,
    buffer, second_trial, source_out, laplace_out, sheet,
):
    profile = column[...]
    pressure = with_plane_below(from_modes(modes_in, 1, from_z, from_y, sheet), source[...])
    span = {j: first_trial[6 + j] - along_span(pressure[j]) for j in range(-1, 4)}
    height = {j: first_trial[11 + j] - along_height(pressure[j]) for j in range(-1, 4)}
    stream = {j: first_trial[1 + j] - along_stream(pressure, j) for j in range(3)}
    cross = {j: along_span(span[j]) + along_height(height[j]) for j in range(-1, 4)}
    stream[-1] = stream[1] + 2.0 * cross[0]
    stream[3] = stream[1] - 2.0 * cross[2]
    stream[-2] = stream[0] + 2.0 * cross[-1]
    stream[4] = stream[2] - 2.0 * cross[3]
    trial = []
    for c, middle in enumerate((stream, span, height)):
        moved = {}
        for j in range(-1, 4) if c == 0 else range(3):
            start = state[3 * c + j] if 0 <= j < 3 else beside[0 if j < 0 else 1]
            curvature = laplace(middle, j)
            forcing = (
                viscosity[j + 2] * curvature
                - profile * along_stream(middle, j)
                - rotor[j + 1] * middle[j]
            )
            moved[j] = 0.5 * start + 0.5 * (middle[j] + TIME_STEP * forcing)
            if 0 <= j < 3:
                laplace_out[3 * c + j] = curvature
                second_trial[3 * c + j] = moved[j]
        trial.append(moved)
    sources = [
        along_stream(trial[0], j) + along_span(trial[1][j]) + along_height(trial[2][j])
        for j in range(3)
    ]
    source_out[...] = sources[1]
    sheets = [trial[0][j] - observed[j] for j in range(3)] + sources
    to_modes(sheets, to_z, to_y, buffer, sheet)


def solve_both_kernel(modes_in, green, symbols, to_x, from_x, out):
    sine = symbols[:NX, :]
    inverse = green[...]
    planes = gather_planes(modes_in, 5)
    both = jnp.concatenate(
        [jnp.concatenate(planes[:3], axis=0), jnp.concatenate(planes[3:], axis=0)], axis=1
    )
    both = left_product(to_x, both, 2)
    lead = both[:, :NY]
    second = inverse * both[:, NY:]
    third = inverse * swap_waves(lead - swap_waves(second, sine), sine)
    wide = left_product(from_x, jnp.concatenate([second, third], axis=1), 3)
    scatter_planes(out, wide, 2)


def adjoint_kernel(
    modes_in, second_trial, source, laplace_mid, viscosity, rotor, observed, column,
    from_z, from_y, to_z, to_y,
    buffer, fourth_trial, source_out, velocity, share_out, sheet,
):
    profile = column[...]
    found = from_modes(modes_in, 2, from_z, from_y, sheet)
    second = with_plane_below(found[:4], source[...])
    misfit = []
    for j in range(3):
        stream = second_trial[j] - along_stream(second, j)
        velocity[0, 0, j] = stream
        velocity[0, 1, j] = second_trial[3 + j] - along_span(second[j])
        velocity[0, 2, j] = second_trial[6 + j] - along_height(second[j])
        misfit.append(stream - observed[j])
    third = with_plane_below(found[4:], 0.5 * (misfit[2] - misfit[0]))
    span = {j: -along_span(third[j]) for j in range(-1, 4)}
    height = {j: -along_height(third[j]) for j in range(-1, 4)}
    cross = {j: along_span(span[j]) + along_height(height[j]) for j in range(-1, 4)}
    stream = {j: misfit[j] - along_stream(third, j) for j in range(3)}
    stream[-1] = stream[1] + 2.0 * cross[0]
    stream[3] = stream[1] - 2.0 * cross[2]
    stream[-2] = stream[0] + 2.0 * cross[-1]
    stream[4] = stream[2] - 2.0 * cross[3]
    share = [None] * 3
    trial = []
    for c, adjoint in enumerate((stream, span, height)):
        spread = {j: viscosity[j + 2] * adjoint[j] for j in adjoint}
        moved = {}
        for j in range(-1, 4) if c == 0 else range(3):
            pulled = (
                profile * along_stream(adjoint, j)
                + laplace(spread, j)
                - rotor[j + 1] * adjoint[j]
            )
            moved[j] = 0.5 * adjoint[j] + 0.5 * TIME_STEP * pulled
        for j in range(3):
            fourth_trial[3 * c + j] = moved[j]
            term = adjoint[j] * laplace_mid[3 * c + j]
            share[j] = term if c == 0 else share[j] + term
        trial.append(moved)
    for j in range(3):
        share_out[j] = 0.5 * share[j]
    sources = [
        along_stream(trial[0], j) + along_span(trial[1][j]) + along_height(trial[2][j])
        for j in range(3)
    ]
    source_out[...] = sources[1]
    to_modes(sources, to_z, to_y, buffer, sheet)


def gradient_kernel(
    modes_in, fourth_trial, source, laplace_start, viscosity, share, from_z, from_y, out, sheet
):
    pressure = with_plane_below(from_modes(modes_in, 1, from_z, from_y, sheet), source[...])
    for j in range(3):
        push = [along_stream(pressure, j), along_span(pressure[j]), along_height(pressure[j])]
        total = share[j]
        for c in range(3):
            total = total + (fourth_trial[3 * c + j] - push[c]) * laplace_start[3 * c + j]
        total = TIME_STEP * viscosity[j + 2] * total
        for copy in range(out.shape[0]):
            out[copy, NZ * j : NZ * (j + 1), :] = total


def local_call(kernel, outs, *args, spaces={}, out_spaces={}, scratch=()):
    specs = [pl.BlockSpec(memory_space=spaces.get(i, pltpu.VMEM)) for i in range(len(args))]
    out_spaces = [out_spaces.get(i, pltpu.VMEM) for i in range(len(outs))]
    shapes = [space(shape, F32) for space, shape in zip(out_spaces, outs)]
    out_specs = [pl.BlockSpec(memory_space=space) for space in out_spaces]
    single = len(outs) == 1
    return pl.pallas_call(
        kernel,
        out_shape=shapes[0] if single else shapes,
        in_specs=specs,
        out_specs=out_specs[0] if single else out_specs,
        scratch_shapes=scratch,
        name=kernel.__name__,
        compiler_params=pltpu.CompilerParams(vmem_limit_bytes=24 * 1024 * 1024),
    )(*args)


def sheets(count):
    return [pltpu.VMEM((NZ * count, NY), F32)]


def exchange(rows, axis="space"):
    count = lax.axis_size(axis)
    wide = rows.reshape(count, 1, rows.size // count)
    return lax.all_to_all(wide, axis, 0, 0, tiled=True).reshape(rows.shape)


def shards(inflow_seeds, rotor_cells, fluctuation, profile, correction, observed):
    samples = lax.axis_size("sample")
    within = [(i, i + 1 - 2 * (i % 2)) for i in range(SPACE)]
    between = [(i, (i - 1 + 2 * (i % 2)) % SPACE) for i in range(SPACE)]
    plane = (NZ, NY)
    inner, outer = local_call(
        pack_kernel, [(4, 2, *plane), (4, 2, *plane)],
        pltpu.with_memory_space_constraint(fluctuation, pltpu.HBM),
        pltpu.with_memory_space_constraint(correction, pltpu.HBM),
        spaces={0: pltpu.HBM, 1: pltpu.HBM}, scratch=[pltpu.SemaphoreType.DMA((4,))],
    )
    inner = lax.ppermute(inner, "space", within)
    outer = lax.ppermute(outer, "space", between)
    to_x, from_x = jnp.asarray(TO_X), jnp.asarray(FROM_X)
    to_y, from_y = jnp.asarray(TO_Y), jnp.asarray(FROM_Y)
    to_z, from_z = jnp.asarray(TO_Z), jnp.asarray(FROM_Z)

    state, flat, part, stream, viscosity, rotor, column = local_call(
        prepare_kernel,
        [
            (9, *plane), (9, *plane), (9, *plane), (2, 3, *plane), (3, *plane), (5, *plane),
            plane,
        ],
        inflow_seeds, fluctuation, correction, rotor_cells.T, profile[None, :],
    )
    rows = NZ * BLOCKS
    symbols = jnp.asarray(SYMBOLS)
    buffer, first_trial, source, beside, laplace_start, viscosity = local_call(
        start_kernel,
        [(rows, NY), (15, *plane), plane, (2, *plane), (9, *plane), (7, *plane)],
        inflow_seeds, outer, inner, state, flat, part, stream, viscosity, rotor, column,
        to_z, to_y,
        scratch=sheets(3),
    )
    buffer = exchange(buffer)
    buffer, green = local_call(
        solve_first_kernel, [(rows, NY), (NX, NY)],
        buffer, symbols, to_x, from_x,
    )
    buffer = exchange(buffer)
    buffer, second_trial, source, laplace_mid = local_call(
        middle_kernel,
        [(5 * SPACE, NY), (9, *plane), plane, (9, *plane)],
        buffer, first_trial, source, state, beside, viscosity, rotor, observed, column,
        from_z, from_y, to_z, to_y, scratch=sheets(6),
    )
    buffer = exchange(buffer)
    buffer = local_call(
        solve_both_kernel, [(2 * rows, NY)],
        buffer, green, symbols, jnp.asarray(TO_X_WIDE), jnp.asarray(FROM_X_WIDE),
    )
    buffer = exchange(buffer)
    buffer, fourth_trial, source, velocity, share = local_call(
        adjoint_kernel,
        [(rows, NY), (9, *plane), plane, (1, 3, 3, *plane), (3, *plane)],
        buffer, second_trial, source, laplace_mid, viscosity, rotor, observed, column,
        from_z, from_y, to_z, to_y, scratch=sheets(8),
    )
    buffer = exchange(buffer)
    buffer, velocity = local_call(
        solve_last_kernel, [(rows, NY), velocity.shape],
        buffer, green, to_x, from_x, velocity,
        out_spaces={1: pltpu.HBM}, scratch=[pltpu.SemaphoreType.DMA],
    )
    buffer = exchange(buffer)
    terms = local_call(
        gradient_kernel, [(samples, SLAB * NZ, NY)],
        buffer, fourth_trial, source, laplace_start, viscosity, share, from_z, from_y,
        scratch=sheets(4),
    )
    terms = lax.all_to_all(terms, "sample", 0, 0, tiled=True)
    gradient = jnp.sum(terms, axis=0).reshape(SLAB, *plane)
    return (velocity, gradient)


def solution(mesh):
    return jax.shard_map(
        shards,
        mesh=mesh,
        in_specs=(
            P("sample", None),
            P(),
            P(None, "space", None, None),
            P(),
            P("space", None, None),
            P("space", None, None),
        ),
        out_specs=(P("sample", None, "space", None, None), P("space", None, None)),
        check_vma=False,
    )
```

```python
import functools
import math

import jax
import jax.numpy as jnp
import ml_dtypes
import numpy as np
from jax import lax
from jax.experimental import pallas as pl
from jax.experimental.pallas import tpu as pltpu
from jax.sharding import PartitionSpec as P

NX = 192
NY = 128
NZ = 48
ROTOR = 8
SPACE = 64
SLAB = NX // SPACE

TIME_STEP = 0.2
BASE_VISCOSITY = 0.15
THRUST = 1.0
F32 = jnp.float32
BF16 = jnp.bfloat16


def real_basis(length):
    half = length // 2
    cells = np.arange(length)[:, None]
    waves = np.arange(half)[None, :]
    phase = 2.0 * np.pi / length * ((cells * waves) % length)
    even = np.cos(phase) * math.sqrt(2.0 / length)
    even[:, 0] = math.sqrt(1.0 / length)
    odd = np.sin(phase) * math.sqrt(2.0 / length)
    odd[:, 0] = (1.0 - 2.0 * (np.arange(length) % 2)) * math.sqrt(1.0 / length)
    return np.concatenate([even, odd], axis=1)


def sine_of(length):
    half = length // 2
    waves = np.arange(length) % half
    return np.sin(2.0 * np.pi / length * waves)


def in_parts(matrix, count):
    parts = []
    rest = np.asarray(matrix, np.float64)
    for _ in range(count):
        parts.append(rest.astype(ml_dtypes.bfloat16))
        rest = rest - parts[-1].astype(np.float64)
    return np.stack(parts)


BASIS_X = real_basis(NX)
BASIS_Y = real_basis(NY)
BASIS_Z = real_basis(NZ)


def stream_rows(first, count):
    device = np.arange(SPACE)[None, :]
    slot = np.arange(first, first + count)[:, None]
    return ((SLAB * device + slot) % NX).reshape(-1)


def pairs_of(count):
    return [(i, order - i) for order in reversed(range(count)) for i in range(order + 1)]


def left_table(matrix, count):
    parts = in_parts(matrix, count)
    return np.concatenate([parts[i] for i, _ in pairs_of(count)], axis=1)


def left_narrow_table(matrix, count):
    parts = list(in_parts(matrix, count))
    return np.concatenate(parts if count == 2 else parts + parts[:1], axis=1)


def right_table(matrix, count):
    parts = list(in_parts(matrix, count))
    none = np.zeros_like(parts[0])
    if count == 2:
        rows = [(parts[0], parts[1]), (parts[0], none)]
    else:
        rows = [(parts[0], parts[1]), (parts[0], parts[1]), (parts[0], none), (parts[2], none)]
    return np.concatenate([np.concatenate(row, axis=1) for row in rows], axis=0)


TO_Y = right_table(BASIS_Y, 2)
TO_Z = left_table(BASIS_Z.T, 2)
EDGE_ROWS = np.where(np.arange(SPACE) % 2 == 0, stream_rows(-1, 1), stream_rows(3, 1))
TO_X = left_narrow_table(BASIS_X[np.concatenate([stream_rows(0, 3), EDGE_ROWS])].T, 2)
TO_X_WIDE = left_table(BASIS_X[stream_rows(0, 3)].T, 2)
FROM_Y = right_table(BASIS_Y.T, 3)
FROM_Z = left_table(BASIS_Z, 3)
FROM_X = left_narrow_table(BASIS_X[stream_rows(0, 3)], 3)
FROM_X_WIDE = left_table(BASIS_X[stream_rows(0, 3)], 3)
BLOCK = 32
BLOCKS = NY // BLOCK
UNITS = NZ * BLOCKS // SPACE


def symbol_table():
    table = np.ones((NX + SPACE, NY))
    table[:NX] = sine_of(NX)[:, None]
    squares = (sine_of(NZ) ** 2)[:, None] + (sine_of(NY) ** 2)[None, :]
    table[NX:, : UNITS * BLOCK] = squares.reshape(SPACE, UNITS * BLOCK)
    return table.astype(np.float32)


SYMBOLS = symbol_table()


def split(value, count):
    parts = []
    for _ in range(count - 1):
        parts.append(value.astype(BF16))
        value = value - parts[-1].astype(F32)
    return parts + [value.astype(BF16)]


def dot(a, b):
    return jnp.dot(a, b, preferred_element_type=F32)


def left_product(table, value, count):
    parts = split(value, count)
    wide = jnp.concatenate([parts[k] for _, k in pairs_of(count)], axis=0)
    columns = range(0, wide.shape[1], NY)
    return jnp.concatenate([dot(table[...], wide[:, i : i + NY]) for i in columns], axis=1)


def left_narrow_product(table, value, count):
    parts = split(value, count)
    none = jnp.zeros_like(parts[0])
    if count == 2:
        rows = [(parts[0], parts[1]), (parts[0], none)]
    else:
        rows = [(parts[0], parts[1]), (parts[0], parts[1]), (parts[0], none), (none, parts[2])]
    wide = jnp.concatenate([jnp.concatenate(row, axis=1) for row in rows], axis=0)
    found = dot(table[...], wide)
    return found[:, :NY] + found[:, NY:]


def right_product(value, table, count):
    parts = split(value, count)
    wide = jnp.concatenate(parts if count == 2 else parts + parts[:1], axis=1)
    found = dot(wide, table[...])
    return found[:, :NY] + found[:, NY:]


def up_z(f):
    return pltpu.roll(f, NZ - 1, 0)


def down_z(f):
    return pltpu.roll(f, 1, 0)


def up_y(f):
    return pltpu.roll(f, NY - 1, 1)


def down_y(f):
    return pltpu.roll(f, 1, 1)


def along_height(f):
    return 0.5 * (up_z(f) - down_z(f))


def along_span(f):
    return 0.5 * (up_y(f) - down_y(f))


def along_stream(planes, j):
    return 0.5 * (planes[j + 1] - planes[j - 1])


def without_edge(planes, even):
    planes[-1] = jnp.where(even, 0.0, planes[-1])
    planes[3] = jnp.where(even, planes[3], 0.0)


def edge_term(planes, even):
    return jnp.where(even, 0.5 * planes[0], -0.5 * planes[2])


def flat_laplace(f):
    return up_z(f) + down_z(f) + up_y(f) + down_y(f) - 6.0 * f


def laplace(planes, j):
    return planes[j + 1] + planes[j - 1] + flat_laplace(planes[j])


def cross_laplace(f):
    return along_span(along_span(f)) + along_height(along_height(f))


def with_plane_below(planes, source):
    below = 2.0 * planes[1] - planes[3] + 4.0 * (source - cross_laplace(planes[1]))
    return {-1: below, 0: planes[0], 1: planes[1], 2: planes[2], 3: planes[3]}


def block_of(array):
    return lax.broadcasted_iota(jnp.int32, array.shape, 1) // BLOCK


def move(array, blocks):
    return pltpu.roll(array, BLOCK * blocks, 1)


THIRD = NZ // UNITS


def by_device(sheet_ref, first):
    a, b, c = [sheet_ref[pl.ds(first + i, THIRD, stride=UNITS), :] for i in range(UNITS)]
    block = block_of(a)
    return [a, move(jnp.where(block == 3, a, b), 1), move(jnp.where(block >= 2, b, c), 2), move(c, 3)]


def by_height(parts):
    block = block_of(parts[0])
    b, c, d = move(parts[1], 3), move(parts[2], 2), move(parts[3], 1)
    return [
        jnp.where(block == 3, b, parts[0]),
        jnp.where(block < 2, b, c),
        jnp.where(block == 0, c, d),
    ]


def to_modes(planes, to_z, to_y, out_ref, sheet_ref):
    count = len(planes)
    side = left_product(to_z, jnp.concatenate(planes, axis=1), 2)
    rows = jnp.concatenate([side[:, NY * i : NY * (i + 1)] for i in range(count)], axis=0)
    sheet_ref[: NZ * count, :] = right_product(rows, to_y, 2)
    sheets = [by_device(sheet_ref, NZ * i) for i in range(count)]
    fourth = sheets.pop(3) if count > 3 else None
    width = len(sheets)
    for row, parts in enumerate(sheets):
        for i in range(BLOCKS):
            part = parts[i]
            if row < UNITS and fourth is not None:
                part = jnp.where(block_of(part) == 3, move(fourth[i], 3 - row), part)
            out_ref[pl.ds(i * width + row, THIRD, stride=BLOCKS * width), :] = part


def from_modes(in_ref, groups, from_z, from_y, sheet_ref):
    count = 4 * groups
    for g in range(groups):
        for p in range(UNITS):
            first = p * groups + g
            parts = [
                in_ref[pl.ds(i * UNITS * groups + first, THIRD, stride=BLOCKS * UNITS * groups), :]
                for i in range(BLOCKS)
            ]
            for i, part in enumerate(by_height(parts)):
                sheet_ref[pl.ds(NZ * (4 * g + p) + i, THIRD, stride=UNITS), :] = part
        units = [in_ref[pl.ds(j * groups + g, NZ, stride=BLOCKS * groups), :] for j in range(BLOCKS)]
        block = block_of(units[3])
        fourth = units[3]
        for j in range(UNITS):
            fourth = jnp.where(block == j, move(units[j], j + 1), fourth)
        sheet_ref[NZ * (4 * g + 3) : NZ * (4 * g + 4), :] = fourth
    side = jnp.concatenate([sheet_ref[NZ * i : NZ * (i + 1), :] for i in range(count)], axis=1)
    side = left_product(from_z, side, 3)
    rows = jnp.concatenate([side[:, NY * i : NY * (i + 1)] for i in range(count)], axis=0)
    rows = right_product(rows, from_y, 3)
    return [rows[NZ * i : NZ * (i + 1)] for i in range(count)]


def gather_planes(in_ref, width):
    rows = [in_ref[pl.ds(i, SPACE, stride=width), :] for i in range(width)]
    block = block_of(rows[0])
    fourth = jnp.where(block == 0, move(rows[0], 1), move(rows[2], 3))
    fourth = jnp.where(block == 1, move(rows[1], 2), fourth)
    return rows[:UNITS] + [fourth] + rows[UNITS:]


def scatter_planes(out_ref, wide, groups):
    for g in range(groups):
        sheet = wide[:, NY * g : NY * (g + 1)]
        planes = [sheet[SPACE * p : SPACE * (p + 1)] for p in range(SLAB)]
        planes.append(pltpu.roll(planes[0], SPACE - 1, 0))
        for u in range(UNITS):
            row = jnp.where(block_of(planes[u]) == 3, move(planes[3], 3 - u), planes[u])
            out_ref[pl.ds(u * groups + g, SPACE, stride=UNITS * groups), :] = row


def swap_waves(modes, sine):
    half = NX // 2
    return jnp.concatenate([sine[:half] * modes[half:], -sine[half:] * modes[:half]], axis=0)


def count_rotors(cells):
    stream = cells[0:1, :]
    span = cells[1:2, :]
    base = cells[2:3, :]
    turbines = cells.shape[1]
    spans = lax.broadcasted_iota(jnp.int32, (NY, turbines), 0)
    in_span = ((spans >= span) & (spans < span + ROTOR)).astype(F32).astype(BF16)
    heights = lax.broadcasted_iota(jnp.int32, (NZ, turbines), 0)
    in_height = (heights >= base) & (heights < base + ROTOR)
    first = lax.axis_index("space") * SLAB
    sheets = []
    for j in range(-1, 4):
        here = stream == lax.rem(first + (j + NX), NX)
        sheets.append((in_height & here).astype(F32).astype(BF16))
    counted = lax.dot_general(
        jnp.concatenate(sheets, axis=0), in_span, (((1,), (1,)), ((), ())),
        preferred_element_type=F32,
    )
    return [counted[NZ * i : NZ * (i + 1)] for i in range(5)]


def spread_profile(row):
    cells = lax.broadcasted_iota(jnp.int32, (NZ, NZ), 0)
    others = lax.broadcasted_iota(jnp.int32, (NZ, NZ), 1)
    column = jnp.sum(jnp.where(cells == others, row, 0.0), axis=1, keepdims=True)
    return jnp.broadcast_to(column, (NZ, NY))


def pack_kernel(
    own, correction, seeds, cells, heights, inner, outer, seeds_out, cells_out, heights_out, arrived
):
    even = lax.rem(lax.axis_index("space"), 2) == 0

    def fill(first, last):
        copies = []

        def add(source, target):
            copies.append(pltpu.make_async_copy(source, target, arrived.at[len(copies)]))

        add(seeds, seeds_out)
        add(cells, cells_out)
        add(heights, heights_out)
        for target, start, near in ((last, 1, 2), (first, 0, 0)):
            planes = pl.ds(start, 2)
            if target is inner:
                add(own.at[:, planes], inner.at[0:3])
                add(correction.at[planes], inner.at[3])
            else:
                add(own.at[1:3, planes], outer.at[1:3])
                add(own.at[0, near], outer.at[0, 0])
                add(correction.at[near], outer.at[0, 1])
        for copy in copies:
            copy.start()
        for copy in copies:
            copy.wait()

    @pl.when(even)
    def _():
        fill(outer, inner)

    @pl.when(jnp.logical_not(even))
    def _():
        fill(inner, outer)


def rolled(plane, shifts):
    return pltpu.roll(pltpu.roll(plane, shifts[0], 1), shifts[1], 0)


def shifts_of(seeds):
    row = seeds[...]
    return row[0, 0], row[0, 1]


def trial_terms(state, flat, viscosity, rotor):
    return state + TIME_STEP * (viscosity * flat - rotor * state)


def stream_terms(viscosity, profile):
    return TIME_STEP * (viscosity - 0.5 * profile), TIME_STEP * (viscosity + 0.5 * profile)


def prepare_kernel(
    seeds, own, correction, cells, heights,
    state_out, flat_out, part_out, stream_out, viscosity_out, rotor_out, column_out,
):
    shifts = shifts_of(seeds)
    profile = spread_profile(heights[...])
    column_out[...] = profile
    rotor = count_rotors(cells)
    for j in range(5):
        rotor[j] = THRUST * rotor[j]
        rotor_out[j] = rotor[j]
    for j in range(3):
        viscosity = BASE_VISCOSITY * jnp.exp(correction[j])
        viscosity_out[j] = viscosity
        stream_out[0, j], stream_out[1, j] = stream_terms(viscosity, profile)
        for c in range(3):
            state = rolled(own[c, j], shifts)
            if c == 0:
                state = state + profile
            flat = flat_laplace(state)
            state_out[3 * c + j] = state
            flat_out[3 * c + j] = flat
            part_out[3 * c + j] = trial_terms(state, flat, viscosity, rotor[j + 1])


def outer_kernel(seeds, outer, column, to_z, to_y, outer_out):
    shifts = shifts_of(seeds)
    outer_out[0, 0] = rolled(outer[0, 0], shifts) + column[...]
    outer_out[0, 1] = BASE_VISCOSITY * jnp.exp(outer[0, 1])
    for c in (1, 2):
        for i in range(2):
            outer_out[c, i] = rolled(outer[c, i], shifts)


def start_kernel(
    seeds, outer, inner, own_state, own_flat, own_part, own_stream, own_viscosity, rotor, column,
    to_z, to_y,
    buffer, first_trial, source_out, beside_out, laplace_out, viscosity_out, sheet,
):
    even = lax.rem(lax.axis_index("space"), 2) == 0
    shifts = shifts_of(seeds)
    profile = column[...]

    def halo(j, c):
        i = j + 2 if j < 0 else j - 3
        if c == 3:
            within = BASE_VISCOSITY * jnp.exp(inner[c, i])
        else:
            within = rolled(inner[c, i], shifts)
            if c == 0:
                within = within + profile
        if c in (1, 2):
            between = outer[c, i]
        elif j in (-1, 3):
            between = outer[0, 0 if c == 0 else 1]
        else:
            return within
        return jnp.where(even, between, within) if j < 0 else jnp.where(even, within, between)

    stream = {j: (own_stream[0, j], own_stream[1, j]) for j in range(3)}
    beside = {}
    for j in (-2, -1, 3, 4):
        viscosity = halo(j, 3)
        viscosity_out[j + 2] = viscosity
        if j in (-1, 3):
            beside[j] = viscosity
            stream[j] = stream_terms(viscosity, profile)
    for j in range(3):
        viscosity_out[j + 2] = own_viscosity[j]
    trial = []
    for c in range(3):
        state = {j: own_state[3 * c + j] for j in range(3)}
        for j in (-2, -1, 3, 4):
            state[j] = halo(j, c)
        moved = {}
        for j in range(-1, 4):
            if 0 <= j < 3:
                part = own_part[3 * c + j]
                laplace_out[3 * c + j] = own_flat[3 * c + j] + (state[j + 1] + state[j - 1])
            else:
                part = trial_terms(state[j], flat_laplace(state[j]), beside[j], rotor[j + 1])
            moved[j] = part + stream[j][0] * state[j + 1] + stream[j][1] * state[j - 1]
            if c > 0 or 0 <= j < 3:
                first_trial[5 * c + j + 1] = moved[j]
        if c == 0:
            without_edge(moved, even)
        trial.append(moved)
        if c == 0:
            beside_out[0] = state[-1]
            beside_out[1] = state[3]
    sources = [
        along_stream(trial[0], j) + along_span(trial[1][j]) + along_height(trial[2][j])
        for j in range(3)
    ]
    source_out[...] = sources[1]
    to_modes(sources + [edge_term(trial[0], even)], to_z, to_y, buffer, sheet)


def green_table(symbols):
    sine = symbols[:NX, :]
    summed = sine * sine + symbols[pl.ds(NX + lax.axis_index("space"), 1), :]
    null_mode = summed == 0.0
    return jnp.where(null_mode, 0.0, -1.0 / jnp.where(null_mode, 1.0, summed))


def solve_rows(modes_in, green, to_x, from_x, out):
    planes = jnp.concatenate(gather_planes(modes_in, 3), axis=0)
    spectrum = left_narrow_product(to_x, planes, 2) * green
    scatter_planes(out, left_narrow_product(from_x, spectrum, 3), 1)


def solve_first_kernel(modes_in, symbols, to_x, from_x, out, green_out):
    green = green_table(symbols)
    green_out[...] = green
    solve_rows(modes_in, green, to_x, from_x, out)


def solve_last_kernel(modes_in, green, to_x, from_x, velocity, out, velocity_out, sent):
    copy = pltpu.make_async_copy(velocity, velocity_out, sent)
    copy.start()
    solve_rows(modes_in, green[...], to_x, from_x, out)
    copy.wait()


def middle_kernel(
    modes_in, first_trial, source, state, beside, viscosity, rotor, observed, column,
    from_z, from_y, to_z, to_y,
    buffer, second_trial, source_out, laplace_out, sheet,
):
    profile = column[...]
    pressure = with_plane_below(from_modes(modes_in, 1, from_z, from_y, sheet), source[...])
    span = {j: first_trial[6 + j] - along_span(pressure[j]) for j in range(-1, 4)}
    height = {j: first_trial[11 + j] - along_height(pressure[j]) for j in range(-1, 4)}
    stream = {j: first_trial[1 + j] - along_stream(pressure, j) for j in range(3)}
    cross = {j: along_span(span[j]) + along_height(height[j]) for j in range(-1, 4)}
    stream[-1] = stream[1] + 2.0 * cross[0]
    stream[3] = stream[1] - 2.0 * cross[2]
    stream[-2] = stream[0] + 2.0 * cross[-1]
    stream[4] = stream[2] - 2.0 * cross[3]
    trial = []
    for c, middle in enumerate((stream, span, height)):
        moved = {}
        for j in range(-1, 4) if c == 0 else range(3):
            start = state[3 * c + j] if 0 <= j < 3 else beside[0 if j < 0 else 1]
            curvature = laplace(middle, j)
            forcing = (
                viscosity[j + 2] * curvature
                - profile * along_stream(middle, j)
                - rotor[j + 1] * middle[j]
            )
            moved[j] = 0.5 * start + 0.5 * (middle[j] + TIME_STEP * forcing)
            if 0 <= j < 3:
                laplace_out[3 * c + j] = curvature
                second_trial[3 * c + j] = moved[j]
        trial.append(moved)
    sources = [
        along_stream(trial[0], j) + along_span(trial[1][j]) + along_height(trial[2][j])
        for j in range(3)
    ]
    source_out[...] = sources[1]
    sheets = [trial[0][j] - observed[j] for j in range(3)] + sources
    to_modes(sheets, to_z, to_y, buffer, sheet)


def solve_both_kernel(modes_in, green, symbols, to_x, from_x, out):
    sine = symbols[:NX, :]
    inverse = green[...]
    planes = gather_planes(modes_in, 5)
    both = jnp.concatenate(
        [jnp.concatenate(planes[:3], axis=0), jnp.concatenate(planes[3:], axis=0)], axis=1
    )
    both = left_product(to_x, both, 2)
    lead = both[:, :NY]
    second = inverse * both[:, NY:]
    third = inverse * swap_waves(lead - swap_waves(second, sine), sine)
    wide = left_product(from_x, jnp.concatenate([second, third], axis=1), 3)
    scatter_planes(out, wide, 2)


def adjoint_kernel(
    modes_in, second_trial, source, laplace_mid, viscosity, rotor, observed, column,
    from_z, from_y, to_z, to_y,
    buffer, fourth_trial, source_out, velocity, share_out, sheet,
):
    even = lax.rem(lax.axis_index("space"), 2) == 0
    profile = column[...]
    found = from_modes(modes_in, 2, from_z, from_y, sheet)
    second = with_plane_below(found[:4], source[...])
    misfit = []
    for j in range(3):
        stream = second_trial[j] - along_stream(second, j)
        velocity[0, 0, j] = stream
        velocity[0, 1, j] = second_trial[3 + j] - along_span(second[j])
        velocity[0, 2, j] = second_trial[6 + j] - along_height(second[j])
        misfit.append(stream - observed[j])
    third = with_plane_below(found[4:], 0.5 * (misfit[2] - misfit[0]))
    span = {j: -along_span(third[j]) for j in range(-1, 4)}
    height = {j: -along_height(third[j]) for j in range(-1, 4)}
    cross = {j: along_span(span[j]) + along_height(height[j]) for j in range(-1, 4)}
    stream = {j: misfit[j] - along_stream(third, j) for j in range(3)}
    stream[-1] = stream[1] + 2.0 * cross[0]
    stream[3] = stream[1] - 2.0 * cross[2]
    stream[-2] = stream[0] + 2.0 * cross[-1]
    stream[4] = stream[2] - 2.0 * cross[3]
    share = [None] * 3
    trial = []
    for c, adjoint in enumerate((stream, span, height)):
        spread = {j: viscosity[j + 2] * adjoint[j] for j in adjoint}
        moved = {}
        for j in range(-1, 4) if c == 0 else range(3):
            pulled = (
                profile * along_stream(adjoint, j)
                + laplace(spread, j)
                - rotor[j + 1] * adjoint[j]
            )
            moved[j] = 0.5 * adjoint[j] + 0.5 * TIME_STEP * pulled
        if c == 0:
            without_edge(moved, even)
        for j in range(3):
            fourth_trial[3 * c + j] = moved[j]
            term = adjoint[j] * laplace_mid[3 * c + j]
            share[j] = term if c == 0 else share[j] + term
        trial.append(moved)
    for j in range(3):
        share_out[j] = 0.5 * share[j]
    sources = [
        along_stream(trial[0], j) + along_span(trial[1][j]) + along_height(trial[2][j])
        for j in range(3)
    ]
    source_out[...] = sources[1]
    to_modes(sources + [edge_term(trial[0], even)], to_z, to_y, buffer, sheet)


def gradient_kernel(
    modes_in, fourth_trial, source, laplace_start, viscosity, share, from_z, from_y, out, sheet
):
    pressure = with_plane_below(from_modes(modes_in, 1, from_z, from_y, sheet), source[...])
    for j in range(3):
        push = [along_stream(pressure, j), along_span(pressure[j]), along_height(pressure[j])]
        total = share[j]
        for c in range(3):
            total = total + (fourth_trial[3 * c + j] - push[c]) * laplace_start[3 * c + j]
        total = TIME_STEP * viscosity[j + 2] * total
        for copy in range(out.shape[0]):
            out[copy, NZ * j : NZ * (j + 1), :] = total


def local_call(kernel, outs, *args, spaces={}, out_spaces={}, scratch=(), cost=None):
    specs = [pl.BlockSpec(memory_space=spaces.get(i, pltpu.VMEM)) for i in range(len(args))]
    out_spaces = [out_spaces.get(i, pltpu.VMEM) for i in range(len(outs))]
    shapes = [
        space(*(out if isinstance(out[0], tuple) else (out, F32)))
        for space, out in zip(out_spaces, outs)
    ]
    out_specs = [pl.BlockSpec(memory_space=space) for space in out_spaces]
    single = len(outs) == 1
    return pl.pallas_call(
        kernel,
        out_shape=shapes[0] if single else shapes,
        in_specs=specs,
        out_specs=out_specs[0] if single else out_specs,
        scratch_shapes=scratch,
        name=kernel.__name__,
        cost_estimate=cost,
        compiler_params=pltpu.CompilerParams(vmem_limit_bytes=24 * 1024 * 1024),
    )(*args)


def sheets(count):
    return [pltpu.VMEM((NZ * count, NY), F32)]


def exchange(rows, axis="space"):
    count = lax.axis_size(axis)
    wide = rows.reshape(count, 1, rows.size // count)
    return lax.all_to_all(wide, axis, 0, 0, tiled=True).reshape(rows.shape)


def shards(inflow_seeds, rotor_cells, fluctuation, profile, correction, observed):
    samples = lax.axis_size("sample")
    within = [(i, i + 1 - 2 * (i % 2)) for i in range(SPACE)]
    between = [(i, (i - 1 + 2 * (i % 2)) % SPACE) for i in range(SPACE)]
    plane = (NZ, NY)
    inputs = [fluctuation, correction, inflow_seeds, rotor_cells.T, profile[None, :]]
    inner, outer, seeds, cells, heights = local_call(
        pack_kernel,
        [
            (4, 2, *plane), (3, 2, *plane), (inflow_seeds.shape, jnp.int32),
            (inputs[3].shape, jnp.int32), (1, NZ),
        ],
        *[pltpu.with_memory_space_constraint(f, pltpu.HBM) for f in inputs],
        spaces={i: pltpu.HBM for i in range(len(inputs))},
        scratch=[pltpu.SemaphoreType.DMA((8,))],
    )
    inner = lax.ppermute(inner, "space", within)
    outer = lax.ppermute(outer, "space", between)
    to_x, from_x = jnp.asarray(TO_X), jnp.asarray(FROM_X)
    to_y, from_y = jnp.asarray(TO_Y), jnp.asarray(FROM_Y)
    to_z, from_z = jnp.asarray(TO_Z), jnp.asarray(FROM_Z)

    state, flat, part, stream, viscosity, rotor, column = local_call(
        prepare_kernel,
        [
            (9, *plane), (9, *plane), (9, *plane), (2, 3, *plane), (3, *plane), (5, *plane),
            plane,
        ],
        seeds, fluctuation, correction, cells, heights,
    )
    outer = local_call(
        outer_kernel, [(3, 2, *plane)], seeds, outer, column, to_z, to_y,
        cost=pl.CostEstimate(flops=10**10, bytes_accessed=10**6, transcendentals=0),
    )
    rows = NZ * BLOCKS
    symbols = jnp.asarray(SYMBOLS)
    buffer, first_trial, source, beside, laplace_start, viscosity = local_call(
        start_kernel,
        [(rows, NY), (15, *plane), plane, (2, *plane), (9, *plane), (7, *plane)],
        seeds, outer, inner, state, flat, part, stream, viscosity, rotor, column,
        to_z, to_y,
        scratch=sheets(4),
    )
    buffer = exchange(buffer)
    buffer, green = local_call(
        solve_first_kernel, [(rows, NY), (NX, NY)],
        buffer, symbols, to_x, from_x,
    )
    buffer = exchange(buffer)
    buffer, second_trial, source, laplace_mid = local_call(
        middle_kernel,
        [(5 * SPACE, NY), (9, *plane), plane, (9, *plane)],
        buffer, first_trial, source, state, beside, viscosity, rotor, observed, column,
        from_z, from_y, to_z, to_y, scratch=sheets(6),
    )
    buffer = exchange(buffer)
    buffer = local_call(
        solve_both_kernel, [(2 * rows, NY)],
        buffer, green, symbols, jnp.asarray(TO_X_WIDE), jnp.asarray(FROM_X_WIDE),
    )
    buffer = exchange(buffer)
    buffer, fourth_trial, source, velocity, share = local_call(
        adjoint_kernel,
        [(rows, NY), (9, *plane), plane, (1, 3, 3, *plane), (3, *plane)],
        buffer, second_trial, source, laplace_mid, viscosity, rotor, observed, column,
        from_z, from_y, to_z, to_y, scratch=sheets(8),
    )
    buffer = exchange(buffer)
    buffer, velocity = local_call(
        solve_last_kernel, [(rows, NY), velocity.shape],
        buffer, green, to_x, from_x, velocity,
        out_spaces={1: pltpu.HBM}, scratch=[pltpu.SemaphoreType.DMA],
    )
    buffer = exchange(buffer)
    terms = local_call(
        gradient_kernel, [(samples, SLAB * NZ, NY)],
        buffer, fourth_trial, source, laplace_start, viscosity, share, from_z, from_y,
        scratch=sheets(4),
    )
    terms = lax.all_to_all(terms, "sample", 0, 0, tiled=True)
    gradient = jnp.sum(terms, axis=0).reshape(SLAB, *plane)
    return (velocity, gradient)


def solution(mesh):
    return jax.shard_map(
        shards,
        mesh=mesh,
        in_specs=(
            P("sample", None),
            P(),
            P(None, "space", None, None),
            P(),
            P("space", None, None),
            P("space", None, None),
        ),
        out_specs=(P("sample", None, "space", None, None), P("space", None, None)),
        check_vma=False,
    )
```

```python
import functools
import math

import jax
import jax.numpy as jnp
import ml_dtypes
import numpy as np
from jax import lax
from jax.experimental import pallas as pl
from jax.experimental.pallas import tpu as pltpu
from jax.sharding import PartitionSpec as P

NX = 192
NY = 128
NZ = 48
ROTOR = 8
SPACE = 64
SLAB = NX // SPACE

TIME_STEP = 0.2
BASE_VISCOSITY = 0.15
THRUST = 1.0
F32 = jnp.float32
BF16 = jnp.bfloat16


def real_basis(length):
    half = length // 2
    cells = np.arange(length)[:, None]
    waves = np.arange(half)[None, :]
    phase = 2.0 * np.pi / length * ((cells * waves) % length)
    even = np.cos(phase) * math.sqrt(2.0 / length)
    even[:, 0] = math.sqrt(1.0 / length)
    odd = np.sin(phase) * math.sqrt(2.0 / length)
    odd[:, 0] = (1.0 - 2.0 * (np.arange(length) % 2)) * math.sqrt(1.0 / length)
    return np.concatenate([even, odd], axis=1)


def sine_of(length):
    half = length // 2
    waves = np.arange(length) % half
    return np.sin(2.0 * np.pi / length * waves)


def in_parts(matrix, count):
    parts = []
    rest = np.asarray(matrix, np.float64)
    for _ in range(count):
        parts.append(rest.astype(ml_dtypes.bfloat16))
        rest = rest - parts[-1].astype(np.float64)
    return np.stack(parts)


BASIS_X = real_basis(NX)
BASIS_Y = real_basis(NY)
BASIS_Z = real_basis(NZ)


def stream_rows(first, count):
    device = np.arange(SPACE)[None, :]
    slot = np.arange(first, first + count)[:, None]
    return ((SLAB * device + slot) % NX).reshape(-1)


def pairs_of(count):
    return [(i, order - i) for order in reversed(range(count)) for i in range(order + 1)]


def left_table(matrix, count):
    parts = in_parts(matrix, count)
    return np.concatenate([parts[i] for i, _ in pairs_of(count)], axis=1)


def left_narrow_table(matrix, count):
    parts = list(in_parts(matrix, count))
    return np.concatenate(parts if count == 2 else parts + parts[:1], axis=1)


def right_table(matrix, count):
    parts = list(in_parts(matrix, count))
    none = np.zeros_like(parts[0])
    if count == 2:
        rows = [(parts[0], parts[1]), (parts[0], none)]
    else:
        rows = [(parts[0], parts[1]), (parts[0], parts[1]), (parts[0], none), (parts[2], none)]
    return np.concatenate([np.concatenate(row, axis=1) for row in rows], axis=0)


TO_Y = right_table(BASIS_Y, 2)
TO_Z = left_table(BASIS_Z.T, 2)
EDGE_ROWS = np.where(np.arange(SPACE) % 2 == 0, stream_rows(-1, 1), stream_rows(3, 1))
TO_X = left_narrow_table(BASIS_X[np.concatenate([stream_rows(0, 3), EDGE_ROWS])].T, 2)
TO_X_WIDE = left_table(BASIS_X[stream_rows(0, 3)].T, 2)
FROM_Y = right_table(BASIS_Y.T, 3)
FROM_Z = left_table(BASIS_Z, 3)
FROM_X = left_narrow_table(BASIS_X[stream_rows(0, 3)], 3)
FROM_X_WIDE = left_table(BASIS_X[stream_rows(0, 3)], 3)
BLOCK = 32
BLOCKS = NY // BLOCK
UNITS = NZ * BLOCKS // SPACE


def symbol_table():
    table = np.ones((NX + SPACE, NY))
    table[:NX] = sine_of(NX)[:, None]
    squares = (sine_of(NZ) ** 2)[:, None] + (sine_of(NY) ** 2)[None, :]
    table[NX:, : UNITS * BLOCK] = squares.reshape(SPACE, UNITS * BLOCK)
    return table.astype(np.float32)


SYMBOLS = symbol_table()


def split(value, count):
    parts = []
    for _ in range(count - 1):
        parts.append(value.astype(BF16))
        value = value - parts[-1].astype(F32)
    return parts + [value.astype(BF16)]


def dot(a, b):
    return jnp.dot(a, b, preferred_element_type=F32)


def left_product(table, value, count):
    parts = split(value, count)
    wide = jnp.concatenate([parts[k] for _, k in pairs_of(count)], axis=0)
    columns = range(0, wide.shape[1], NY)
    return jnp.concatenate([dot(table[...], wide[:, i : i + NY]) for i in columns], axis=1)


def left_narrow_product(table, value, count):
    parts = split(value, count)
    none = jnp.zeros_like(parts[0])
    if count == 2:
        rows = [(parts[0], parts[1]), (parts[0], none)]
    else:
        rows = [(parts[0], parts[1]), (parts[0], parts[1]), (parts[0], none), (none, parts[2])]
    wide = jnp.concatenate([jnp.concatenate(row, axis=1) for row in rows], axis=0)
    found = dot(table[...], wide)
    return found[:, :NY] + found[:, NY:]


def right_product(value, table, count):
    parts = split(value, count)
    wide = jnp.concatenate(parts if count == 2 else parts + parts[:1], axis=1)
    found = dot(wide, table[...])
    return found[:, :NY] + found[:, NY:]


def up_z(f):
    return pltpu.roll(f, NZ - 1, 0)


def down_z(f):
    return pltpu.roll(f, 1, 0)


def up_y(f):
    return pltpu.roll(f, NY - 1, 1)


def down_y(f):
    return pltpu.roll(f, 1, 1)


def along_height(f):
    return 0.5 * (up_z(f) - down_z(f))


def along_span(f):
    return 0.5 * (up_y(f) - down_y(f))


def along_stream(planes, j):
    return 0.5 * (planes[j + 1] - planes[j - 1])


def without_edge(planes, even):
    planes[-1] = jnp.where(even, 0.0, planes[-1])
    planes[3] = jnp.where(even, planes[3], 0.0)


def edge_term(planes, even):
    return jnp.where(even, 0.5 * planes[0], -0.5 * planes[2])


def flat_laplace(f):
    return up_z(f) + down_z(f) + up_y(f) + down_y(f) - 6.0 * f


def laplace(planes, j):
    return planes[j + 1] + planes[j - 1] + flat_laplace(planes[j])


def cross_laplace(f):
    span = pltpu.roll(f, 2, 1) + pltpu.roll(f, NY - 2, 1)
    height = pltpu.roll(f, 2, 0) + pltpu.roll(f, NZ - 2, 0)
    return 0.25 * (span + height) - f


def with_plane_below(planes, source):
    below = 2.0 * planes[1] - planes[3] + 4.0 * (source - cross_laplace(planes[1]))
    return {-1: below, 0: planes[0], 1: planes[1], 2: planes[2], 3: planes[3]}


def block_of(array):
    return lax.broadcasted_iota(jnp.int32, array.shape, 1) // BLOCK


def move(array, blocks):
    return pltpu.roll(array, BLOCK * blocks, 1)


THIRD = NZ // UNITS


def by_device(sheet_ref, first):
    a, b, c = [sheet_ref[pl.ds(first + i, THIRD, stride=UNITS), :] for i in range(UNITS)]
    block = block_of(a)
    return [a, move(jnp.where(block == 3, a, b), 1), move(jnp.where(block >= 2, b, c), 2), move(c, 3)]


def by_height(parts):
    block = block_of(parts[0])
    b, c, d = move(parts[1], 3), move(parts[2], 2), move(parts[3], 1)
    return [
        jnp.where(block == 3, b, parts[0]),
        jnp.where(block < 2, b, c),
        jnp.where(block == 0, c, d),
    ]


def to_modes(planes, to_z, to_y, out_ref, sheet_ref):
    count = len(planes)
    side = left_product(to_z, jnp.concatenate(planes, axis=1), 2)
    rows = jnp.concatenate([side[:, NY * i : NY * (i + 1)] for i in range(count)], axis=0)
    sheet_ref[: NZ * count, :] = right_product(rows, to_y, 2)
    sheets = [by_device(sheet_ref, NZ * i) for i in range(count)]
    fourth = sheets.pop(3) if count > 3 else None
    width = len(sheets)
    for row, parts in enumerate(sheets):
        for i in range(BLOCKS):
            part = parts[i]
            if row < UNITS and fourth is not None:
                part = jnp.where(block_of(part) == 3, move(fourth[i], 3 - row), part)
            out_ref[pl.ds(i * width + row, THIRD, stride=BLOCKS * width), :] = part


def from_modes(in_ref, groups, from_z, from_y, sheet_ref):
    count = 4 * groups
    for g in range(groups):
        for p in range(UNITS):
            first = p * groups + g
            parts = [
                in_ref[pl.ds(i * UNITS * groups + first, THIRD, stride=BLOCKS * UNITS * groups), :]
                for i in range(BLOCKS)
            ]
            for i, part in enumerate(by_height(parts)):
                sheet_ref[pl.ds(NZ * (4 * g + p) + i, THIRD, stride=UNITS), :] = part
        units = [in_ref[pl.ds(j * groups + g, NZ, stride=BLOCKS * groups), :] for j in range(BLOCKS)]
        block = block_of(units[3])
        fourth = units[3]
        for j in range(UNITS):
            fourth = jnp.where(block == j, move(units[j], j + 1), fourth)
        sheet_ref[NZ * (4 * g + 3) : NZ * (4 * g + 4), :] = fourth
    side = jnp.concatenate([sheet_ref[NZ * i : NZ * (i + 1), :] for i in range(count)], axis=1)
    side = left_product(from_z, side, 3)
    rows = jnp.concatenate([side[:, NY * i : NY * (i + 1)] for i in range(count)], axis=0)
    rows = right_product(rows, from_y, 3)
    return [rows[NZ * i : NZ * (i + 1)] for i in range(count)]


def gather_planes(in_ref, width):
    rows = [in_ref[pl.ds(i, SPACE, stride=width), :] for i in range(width)]
    block = block_of(rows[0])
    fourth = jnp.where(block == 0, move(rows[0], 1), move(rows[2], 3))
    fourth = jnp.where(block == 1, move(rows[1], 2), fourth)
    return rows[:UNITS] + [fourth] + rows[UNITS:]


def scatter_planes(out_ref, wide, groups):
    for g in range(groups):
        sheet = wide[:, NY * g : NY * (g + 1)]
        planes = [sheet[SPACE * p : SPACE * (p + 1)] for p in range(SLAB)]
        planes.append(pltpu.roll(planes[0], SPACE - 1, 0))
        for u in range(UNITS):
            row = jnp.where(block_of(planes[u]) == 3, move(planes[3], 3 - u), planes[u])
            out_ref[pl.ds(u * groups + g, SPACE, stride=UNITS * groups), :] = row


def swap_waves(modes, sine):
    half = NX // 2
    return jnp.concatenate([sine[:half] * modes[half:], -sine[half:] * modes[:half]], axis=0)


def count_rotors(cells):
    stream = cells[0:1, :]
    span = cells[1:2, :]
    base = cells[2:3, :]
    turbines = cells.shape[1]
    spans = lax.broadcasted_iota(jnp.int32, (NY, turbines), 0)
    in_span = ((spans >= span) & (spans < span + ROTOR)).astype(F32).astype(BF16)
    heights = lax.broadcasted_iota(jnp.int32, (NZ, turbines), 0)
    in_height = (heights >= base) & (heights < base + ROTOR)
    first = lax.axis_index("space") * SLAB
    sheets = []
    for j in range(-1, 4):
        here = stream == lax.rem(first + (j + NX), NX)
        sheets.append((in_height & here).astype(F32).astype(BF16))
    counted = lax.dot_general(
        jnp.concatenate(sheets, axis=0), in_span, (((1,), (1,)), ((), ())),
        preferred_element_type=F32,
    )
    return [counted[NZ * i : NZ * (i + 1)] for i in range(5)]


def spread_profile(row):
    cells = lax.broadcasted_iota(jnp.int32, (NZ, NZ), 0)
    others = lax.broadcasted_iota(jnp.int32, (NZ, NZ), 1)
    column = jnp.sum(jnp.where(cells == others, row, 0.0), axis=1, keepdims=True)
    return jnp.broadcast_to(column, (NZ, NY))


def pack_kernel(
    own, correction, seeds, cells, heights, inner, outer, seeds_out, cells_out, heights_out, arrived
):
    even = lax.rem(lax.axis_index("space"), 2) == 0

    def fill(first, last):
        copies = []

        def add(source, target):
            copies.append(pltpu.make_async_copy(source, target, arrived.at[len(copies)]))

        add(seeds, seeds_out)
        add(cells, cells_out)
        add(heights, heights_out)
        for target, start, near in ((last, 1, 2), (first, 0, 0)):
            planes = pl.ds(start, 2)
            if target is inner:
                add(own.at[:, planes], inner.at[0:3])
                add(correction.at[planes], inner.at[3])
            else:
                add(own.at[1:3, planes], outer.at[1:3])
                add(own.at[0, near], outer.at[0, 0])
                add(correction.at[near], outer.at[0, 1])
        for copy in copies:
            copy.start()
        for copy in copies:
            copy.wait()

    @pl.when(even)
    def _():
        fill(outer, inner)

    @pl.when(jnp.logical_not(even))
    def _():
        fill(inner, outer)


def rolled(plane, shifts):
    return pltpu.roll(pltpu.roll(plane, shifts[0], 1), shifts[1], 0)


def shifts_of(seeds):
    row = seeds[...]
    return row[0, 0], row[0, 1]


def trial_terms(state, flat, viscosity, rotor):
    return state + TIME_STEP * (viscosity * flat - rotor * state)


def stream_terms(viscosity, profile):
    return TIME_STEP * (viscosity - 0.5 * profile), TIME_STEP * (viscosity + 0.5 * profile)


def prepare_kernel(
    seeds, own, correction, cells, heights,
    state_out, flat_out, part_out, stream_out, viscosity_out, rotor_out, column_out,
):
    shifts = shifts_of(seeds)
    profile = spread_profile(heights[...])
    column_out[...] = profile
    rotor = count_rotors(cells)
    for j in range(5):
        rotor[j] = THRUST * rotor[j]
        rotor_out[j] = rotor[j]
    for j in range(3):
        viscosity = BASE_VISCOSITY * jnp.exp(correction[j])
        viscosity_out[j] = viscosity
        stream_out[0, j], stream_out[1, j] = stream_terms(viscosity, profile)
        for c in range(3):
            state = rolled(own[c, j], shifts)
            if c == 0:
                state = state + profile
            flat = flat_laplace(state)
            state_out[3 * c + j] = state
            flat_out[3 * c + j] = flat
            part_out[3 * c + j] = trial_terms(state, flat, viscosity, rotor[j + 1])


def outer_kernel(seeds, outer, column, to_z, to_y, outer_out):
    shifts = shifts_of(seeds)
    outer_out[0, 0] = rolled(outer[0, 0], shifts) + column[...]
    outer_out[0, 1] = BASE_VISCOSITY * jnp.exp(outer[0, 1])
    for c in (1, 2):
        for i in range(2):
            outer_out[c, i] = rolled(outer[c, i], shifts)


def start_kernel(
    seeds, outer, inner, own_state, own_flat, own_part, own_stream, own_viscosity, rotor, column,
    to_z, to_y,
    buffer, first_trial, source_out, beside_out, laplace_out, viscosity_out, sheet,
):
    even = lax.rem(lax.axis_index("space"), 2) == 0
    shifts = shifts_of(seeds)
    profile = column[...]

    def halo(j, c):
        i = j + 2 if j < 0 else j - 3
        if c == 3:
            within = BASE_VISCOSITY * jnp.exp(inner[c, i])
        else:
            within = rolled(inner[c, i], shifts)
            if c == 0:
                within = within + profile
        if c in (1, 2):
            between = outer[c, i]
        elif j in (-1, 3):
            between = outer[0, 0 if c == 0 else 1]
        else:
            return within
        return jnp.where(even, between, within) if j < 0 else jnp.where(even, within, between)

    stream = {j: (own_stream[0, j], own_stream[1, j]) for j in range(3)}
    beside = {}
    for j in (-2, -1, 3, 4):
        viscosity = halo(j, 3)
        viscosity_out[j + 2] = viscosity
        if j in (-1, 3):
            beside[j] = viscosity
            stream[j] = stream_terms(viscosity, profile)
    for j in range(3):
        viscosity_out[j + 2] = own_viscosity[j]
    trial = []
    for c in range(3):
        state = {j: own_state[3 * c + j] for j in range(3)}
        for j in (-2, -1, 3, 4):
            state[j] = halo(j, c)
        moved = {}
        for j in range(-1, 4):
            if 0 <= j < 3:
                part = own_part[3 * c + j]
                laplace_out[3 * c + j] = own_flat[3 * c + j] + (state[j + 1] + state[j - 1])
            else:
                part = trial_terms(state[j], flat_laplace(state[j]), beside[j], rotor[j + 1])
            moved[j] = part + stream[j][0] * state[j + 1] + stream[j][1] * state[j - 1]
            if c > 0 or 0 <= j < 3:
                first_trial[5 * c + j + 1] = moved[j]
        if c == 0:
            without_edge(moved, even)
        trial.append(moved)
        if c == 0:
            beside_out[0] = state[-1]
            beside_out[1] = state[3]
    sources = [
        along_stream(trial[0], j) + along_span(trial[1][j]) + along_height(trial[2][j])
        for j in range(3)
    ]
    source_out[...] = sources[1]
    to_modes(sources + [edge_term(trial[0], even)], to_z, to_y, buffer, sheet)


def green_table(symbols):
    sine = symbols[:NX, :]
    summed = sine * sine + symbols[pl.ds(NX + lax.axis_index("space"), 1), :]
    null_mode = summed == 0.0
    return jnp.where(null_mode, 0.0, -1.0 / jnp.where(null_mode, 1.0, summed))


def solve_rows(modes_in, green, to_x, from_x, out):
    planes = jnp.concatenate(gather_planes(modes_in, 3), axis=0)
    spectrum = left_narrow_product(to_x, planes, 2) * green
    scatter_planes(out, left_narrow_product(from_x, spectrum, 3), 1)


def solve_first_kernel(modes_in, symbols, to_x, from_x, out, green_out):
    green = green_table(symbols)
    green_out[...] = green
    solve_rows(modes_in, green, to_x, from_x, out)


def solve_last_kernel(modes_in, green, to_x, from_x, velocity, out, velocity_out, sent):
    copy = pltpu.make_async_copy(velocity, velocity_out, sent)
    copy.start()
    solve_rows(modes_in, green[...], to_x, from_x, out)
    copy.wait()


def middle_kernel(
    modes_in, first_trial, source, state, beside, viscosity, rotor, observed, column,
    from_z, from_y, to_z, to_y,
    buffer, second_trial, source_out, laplace_out, sheet,
):
    profile = column[...]
    pressure = with_plane_below(from_modes(modes_in, 1, from_z, from_y, sheet), source[...])
    span = {j: first_trial[6 + j] - along_span(pressure[j]) for j in range(-1, 4)}
    height = {j: first_trial[11 + j] - along_height(pressure[j]) for j in range(-1, 4)}
    stream = {j: first_trial[1 + j] - along_stream(pressure, j) for j in range(3)}
    cross = {j: along_span(span[j]) + along_height(height[j]) for j in range(-1, 4)}
    stream[-1] = stream[1] + 2.0 * cross[0]
    stream[3] = stream[1] - 2.0 * cross[2]
    stream[-2] = stream[0] + 2.0 * cross[-1]
    stream[4] = stream[2] - 2.0 * cross[3]
    trial = []
    for c, middle in enumerate((stream, span, height)):
        moved = {}
        for j in range(-1, 4) if c == 0 else range(3):
            start = state[3 * c + j] if 0 <= j < 3 else beside[0 if j < 0 else 1]
            curvature = laplace(middle, j)
            forcing = (
                viscosity[j + 2] * curvature
                - profile * along_stream(middle, j)
                - rotor[j + 1] * middle[j]
            )
            moved[j] = 0.5 * start + 0.5 * (middle[j] + TIME_STEP * forcing)
            if 0 <= j < 3:
                laplace_out[3 * c + j] = curvature
                second_trial[3 * c + j] = moved[j]
        trial.append(moved)
    sources = [
        along_stream(trial[0], j) + along_span(trial[1][j]) + along_height(trial[2][j])
        for j in range(3)
    ]
    source_out[...] = sources[1]
    sheets = [trial[0][j] - observed[j] for j in range(3)] + sources
    to_modes(sheets, to_z, to_y, buffer, sheet)


def solve_both_kernel(modes_in, green, symbols, to_x, from_x, out):
    sine = symbols[:NX, :]
    inverse = green[...]
    planes = gather_planes(modes_in, 5)
    both = jnp.concatenate(
        [jnp.concatenate(planes[:3], axis=0), jnp.concatenate(planes[3:], axis=0)], axis=1
    )
    both = left_product(to_x, both, 2)
    lead = both[:, :NY]
    second = inverse * both[:, NY:]
    third = inverse * swap_waves(lead - swap_waves(second, sine), sine)
    wide = left_product(from_x, jnp.concatenate([second, third], axis=1), 3)
    scatter_planes(out, wide, 2)


def adjoint_kernel(
    modes_in, second_trial, source, laplace_mid, viscosity, rotor, observed, column,
    from_z, from_y, to_z, to_y,
    buffer, fourth_trial, source_out, velocity, share_out, sheet,
):
    even = lax.rem(lax.axis_index("space"), 2) == 0
    profile = column[...]
    found = from_modes(modes_in, 2, from_z, from_y, sheet)
    second = with_plane_below(found[:4], source[...])
    misfit = []
    for j in range(3):
        stream = second_trial[j] - along_stream(second, j)
        velocity[0, 0, j] = stream
        velocity[0, 1, j] = second_trial[3 + j] - along_span(second[j])
        velocity[0, 2, j] = second_trial[6 + j] - along_height(second[j])
        misfit.append(stream - observed[j])
    third = with_plane_below(found[4:], 0.5 * (misfit[2] - misfit[0]))
    span = {j: -along_span(third[j]) for j in range(-1, 4)}
    height = {j: -along_height(third[j]) for j in range(-1, 4)}
    cross = {j: along_span(span[j]) + along_height(height[j]) for j in range(-1, 4)}
    stream = {j: misfit[j] - along_stream(third, j) for j in range(3)}
    stream[-1] = stream[1] + 2.0 * cross[0]
    stream[3] = stream[1] - 2.0 * cross[2]
    stream[-2] = stream[0] + 2.0 * cross[-1]
    stream[4] = stream[2] - 2.0 * cross[3]
    share = [None] * 3
    trial = []
    for c, adjoint in enumerate((stream, span, height)):
        spread = {j: viscosity[j + 2] * adjoint[j] for j in adjoint}
        moved = {}
        for j in range(-1, 4) if c == 0 else range(3):
            pulled = (
                profile * along_stream(adjoint, j)
                + laplace(spread, j)
                - rotor[j + 1] * adjoint[j]
            )
            moved[j] = 0.5 * adjoint[j] + 0.5 * TIME_STEP * pulled
        if c == 0:
            without_edge(moved, even)
        for j in range(3):
            fourth_trial[3 * c + j] = moved[j]
            term = adjoint[j] * laplace_mid[3 * c + j]
            share[j] = term if c == 0 else share[j] + term
        trial.append(moved)
    for j in range(3):
        share_out[j] = 0.5 * share[j]
    sources = [
        along_stream(trial[0], j) + along_span(trial[1][j]) + along_height(trial[2][j])
        for j in range(3)
    ]
    source_out[...] = sources[1]
    to_modes(sources + [edge_term(trial[0], even)], to_z, to_y, buffer, sheet)


def gradient_kernel(
    modes_in, fourth_trial, source, laplace_start, viscosity, share, from_z, from_y, out, sheet
):
    pressure = with_plane_below(from_modes(modes_in, 1, from_z, from_y, sheet), source[...])
    for j in range(3):
        push = [along_stream(pressure, j), along_span(pressure[j]), along_height(pressure[j])]
        total = share[j]
        for c in range(3):
            total = total + (fourth_trial[3 * c + j] - push[c]) * laplace_start[3 * c + j]
        total = TIME_STEP * viscosity[j + 2] * total
        for copy in range(out.shape[0]):
            out[copy, NZ * j : NZ * (j + 1), :] = total


def local_call(kernel, outs, *args, spaces={}, out_spaces={}, scratch=(), cost=None):
    specs = [pl.BlockSpec(memory_space=spaces.get(i, pltpu.VMEM)) for i in range(len(args))]
    out_spaces = [out_spaces.get(i, pltpu.VMEM) for i in range(len(outs))]
    shapes = [
        space(*(out if isinstance(out[0], tuple) else (out, F32)))
        for space, out in zip(out_spaces, outs)
    ]
    out_specs = [pl.BlockSpec(memory_space=space) for space in out_spaces]
    single = len(outs) == 1
    return pl.pallas_call(
        kernel,
        out_shape=shapes[0] if single else shapes,
        in_specs=specs,
        out_specs=out_specs[0] if single else out_specs,
        scratch_shapes=scratch,
        name=kernel.__name__,
        cost_estimate=cost,
        compiler_params=pltpu.CompilerParams(vmem_limit_bytes=24 * 1024 * 1024),
    )(*args)


def sheets(count):
    return [pltpu.VMEM((NZ * count, NY), F32)]


def exchange(rows, axis="space"):
    count = lax.axis_size(axis)
    wide = rows.reshape(count, 1, rows.size // count)
    return lax.all_to_all(wide, axis, 0, 0, tiled=True).reshape(rows.shape)


def shards(inflow_seeds, rotor_cells, fluctuation, profile, correction, observed):
    samples = lax.axis_size("sample")
    within = [(i, i + 1 - 2 * (i % 2)) for i in range(SPACE)]
    between = [(i, (i - 1 + 2 * (i % 2)) % SPACE) for i in range(SPACE)]
    plane = (NZ, NY)
    inputs = [fluctuation, correction, inflow_seeds, rotor_cells.T, profile[None, :]]
    inner, outer, seeds, cells, heights = local_call(
        pack_kernel,
        [
            (4, 2, *plane), (3, 2, *plane), (inflow_seeds.shape, jnp.int32),
            (inputs[3].shape, jnp.int32), (1, NZ),
        ],
        *[pltpu.with_memory_space_constraint(f, pltpu.HBM) for f in inputs],
        spaces={i: pltpu.HBM for i in range(len(inputs))},
        scratch=[pltpu.SemaphoreType.DMA((8,))],
    )
    inner = lax.ppermute(inner, "space", within)
    outer = lax.ppermute(outer, "space", between)
    to_x, from_x = jnp.asarray(TO_X), jnp.asarray(FROM_X)
    to_y, from_y = jnp.asarray(TO_Y), jnp.asarray(FROM_Y)
    to_z, from_z = jnp.asarray(TO_Z), jnp.asarray(FROM_Z)

    state, flat, part, stream, viscosity, rotor, column = local_call(
        prepare_kernel,
        [
            (9, *plane), (9, *plane), (9, *plane), (2, 3, *plane), (3, *plane), (5, *plane),
            plane,
        ],
        seeds, fluctuation, correction, cells, heights,
    )
    outer = local_call(
        outer_kernel, [(3, 2, *plane)], seeds, outer, column, to_z, to_y,
        cost=pl.CostEstimate(flops=10**10, bytes_accessed=10**6, transcendentals=0),
    )
    rows = NZ * BLOCKS
    symbols = jnp.asarray(SYMBOLS)
    buffer, first_trial, source, beside, laplace_start, viscosity = local_call(
        start_kernel,
        [(rows, NY), (15, *plane), plane, (2, *plane), (9, *plane), (7, *plane)],
        seeds, outer, inner, state, flat, part, stream, viscosity, rotor, column,
        to_z, to_y,
        scratch=sheets(4),
    )
    buffer = exchange(buffer)
    buffer, green = local_call(
        solve_first_kernel, [(rows, NY), (NX, NY)],
        buffer, symbols, to_x, from_x,
    )
    buffer = exchange(buffer)
    buffer, second_trial, source, laplace_mid = local_call(
        middle_kernel,
        [(5 * SPACE, NY), (9, *plane), plane, (9, *plane)],
        buffer, first_trial, source, state, beside, viscosity, rotor, observed, column,
        from_z, from_y, to_z, to_y, scratch=sheets(6),
    )
    buffer = exchange(buffer)
    buffer = local_call(
        solve_both_kernel, [(2 * rows, NY)],
        buffer, green, symbols, jnp.asarray(TO_X_WIDE), jnp.asarray(FROM_X_WIDE),
    )
    buffer = exchange(buffer)
    buffer, fourth_trial, source, velocity, share = local_call(
        adjoint_kernel,
        [(rows, NY), (9, *plane), plane, (1, 3, 3, *plane), (3, *plane)],
        buffer, second_trial, source, laplace_mid, viscosity, rotor, observed, column,
        from_z, from_y, to_z, to_y, scratch=sheets(8),
    )
    buffer = exchange(buffer)
    buffer, velocity = local_call(
        solve_last_kernel, [(rows, NY), velocity.shape],
        buffer, green, to_x, from_x, velocity,
        out_spaces={1: pltpu.HBM}, scratch=[pltpu.SemaphoreType.DMA],
    )
    buffer = exchange(buffer)
    terms = local_call(
        gradient_kernel, [(samples, SLAB * NZ, NY)],
        buffer, fourth_trial, source, laplace_start, viscosity, share, from_z, from_y,
        scratch=sheets(4),
    )
    terms = lax.all_to_all(terms, "sample", 0, 0, tiled=True)
    gradient = jnp.sum(terms, axis=0).reshape(SLAB, *plane)
    return (velocity, gradient)


def solution(mesh):
    return jax.shard_map(
        shards,
        mesh=mesh,
        in_specs=(
            P("sample", None),
            P(),
            P(None, "space", None, None),
            P(),
            P("space", None, None),
            P("space", None, None),
        ),
        out_specs=(P("sample", None, "space", None, None), P("space", None, None)),
        check_vma=False,
    )
```
